32 devices in a mesh: sect: 2 (over core), grp: 4 (over y, x), dev: 4 (over z).
Axes of the slice: x: 2, y: 2, z: 4, core: 2. Of those that a mesh axis runs over, the one named last changes fastest.
Arguments:
- tokens: bfloat16 [128, 7168], P(('sect', 'grp', 'dev')), may hold values from -6 to 6
- expert_ids: int32 [128, 8], P(('sect', 'grp', 'dev')), may hold values from 0 to 15, all different within a row; in each aligned block of 4 rows (0 to 3, 4 to 7, ...) at most 2 rows name the same one
- gate_weights: float32 [128, 8], P(('sect', 'grp', 'dev')), may hold values from 0.1 to 0.6
- w_gate: bfloat16 [16, 7168, 2048], P(('sect', 'grp'), None, 'dev'), may hold values from -0.0625 to 0.0625
- w_up: bfloat16 [16, 7168, 2048], P(('sect', 'grp'), None, 'dev'), may hold values from -0.0625 to 0.0625
- w_down: bfloat16 [16, 2048, 7168], P(('sect', 'grp'), 'dev'), may hold values from -0.125 to 0.125
Outputs:
- mixed: bfloat16 [128, 7168], P(('sect', 'grp', 'dev'))
The draws below stay inside these ranges and needn't reach their ends.
Inputs may be any that keep to these rules, and one draw needn't show every extreme that they name: `expert_ids`: each row names 8 different experts. Within the 4 rows of one device no expert is named by more than 2 rows, and on some device some expert is named by exactly 2.
All inputs are finite; a program needn't handle non-finite values.
Results may differ from the reference program's by a relative error of at most 0.015.
Values may be sent and summed in bfloat16 or wider, within the bound.
No kernel may reach another device: no remote copies, remote signals or barrier semaphores. Data moves between devices by JAX's collectives and lax.ppermute only.
A program may use at most 128 MiB of HBM per device.

```python
import math
import jax
import jax.numpy as jnp
import numpy as np
from jax import lax

D = 7168
FF = 2048
TOP = 8
TOK_DEV = 4
CAP = 2
EXPERTS = 16
FF_DEV = 512
TOKENS = 128


def shard_levels(stream_key, shape, shards, least, top_value):
    def one(position, shards_of):
        heights = jax.random.uniform(jax.random.fold_in(jax.random.fold_in(stream_key, 6), position), (shards_of,), jnp.float32, least / len(shards), top_value / len(shards))
        return jnp.repeat(jnp.exp(heights), shape[position] // shards_of).reshape((-1,) + (1,) * (len(shape) - position - 1))

    factor_of = one(*shards[0])
    for cut in shards[1:]:
        factor_of = factor_of * one(*cut)
    return factor_of


def deal_out(own_key, own, number, rows, count, top, limit, slope):
    order = jax.random.permutation(own_key, count)
    crowded, ordinary = portions_of(count, rows * top, limit, slope, True), portions_of(count, rows * top, limit, slope, False)
    places = jnp.arange(count)

    def named(tallies, offset_by):
        used = int((tallies > 0).sum())
        fixed = max(1, used // 4)
        passed = fixed + (places - fixed + offset_by * (used - fixed)) % max(1, count - fixed)
        return jnp.zeros((count,), jnp.int32).at[order[jnp.where(places < fixed, places, passed)]].set(jnp.asarray(tallies, jnp.int32))

    tallies = jnp.where(number % 4 == 0, named(crowded, number // 4), named(ordinary, number - number // 4 - 1))
    mixed = jax.random.permutation(jax.random.fold_in(own, 3), count)
    source_of, sink = mixed[0:count // 2 * 2:2], mixed[1:count // 2 * 2:2]
    room = jnp.minimum(tallies[source_of] - 1, limit - tallies[sink]) // 2
    room = jnp.where((source_of == order[0]) | (sink == order[0]) | (tallies[sink] == 0), 0, jnp.maximum(room, 0))
    passed = jax.random.randint(jax.random.fold_in(own, 4), (count // 2,), 0, 1 << 20) % (room + 1)
    tallies = tallies.at[source_of].add(-passed).at[sink].add(passed)
    items = jnp.searchsorted(jnp.cumsum(tallies), jnp.arange(rows * top), side="right").astype(jnp.int32)
    listing = items.reshape(top, rows).T
    listing = listing[jax.random.permutation(jax.random.fold_in(own, 1), rows)]
    offset_by = jax.random.randint(jax.random.fold_in(own, 2), (rows, 1), 0, top)
    return jnp.take_along_axis(listing, (jnp.arange(top)[None, :] + offset_by) % top, axis=1)


def portions_of(number_of, total, limit, lean, full):
    loads = [(1 << 20) // math.isqrt(rank ** lean) + 1 for rank in range(1, number_of + 1)]
    largest = limit if full else min(limit, max(-(-total // number_of), total * loads[0] // sum(loads)))
    least = 1 if total - largest >= number_of - 1 else 0
    counts, rest = [largest] + [least] * (number_of - 1), total - largest - least * (number_of - 1)
    while rest > 0:
        candidates = [i for i in range(1, number_of) if counts[i] < largest] or [i for i in range(1, number_of) if counts[i] < limit]
        whole, remaining = sum([loads[i] for i in candidates]), rest
        for i in candidates:
            extra = min(limit - counts[i], max(1, remaining * loads[i] // whole), rest)
            counts[i] = counts[i] + extra
            rest = rest - extra
    return np.array(counts)


def scatter_about(key, extent, spread, bound, split=(), kind=jnp.bfloat16):
    factor_of = shard_levels(key, extent, split, -0.22, 0.18) if split else 1.0
    drawn = jax.random.normal(key, extent, jnp.float32) * spread * factor_of
    return jnp.minimum(jnp.maximum(drawn, -bound), bound).astype(kind)


def setup_inputs(seed: int = 0) -> dict:
    seeds = jax.random.split(jax.random.key(seed), 7)
    tokens = scatter_about(seeds[0], (TOKENS, D), 1.0, 6.0, ((0, 32),))
    expert_ids_keys = jax.random.split(jax.random.fold_in(seeds[1], 1), TOKENS // TOK_DEV)
    expert_ids_turns = jax.random.permutation(jax.random.fold_in(seeds[1], 3), TOKENS // TOK_DEV)
    expert_ids = jax.vmap(lambda own, number: deal_out(jax.random.fold_in(seeds[1], 2), own, number, TOK_DEV, EXPERTS, TOP, CAP, 2))(expert_ids_keys, expert_ids_turns).reshape((TOKENS, TOP))
    gate_weights = jnp.clip(0.1 + 0.5 * jax.random.uniform(seeds[2], (TOKENS, TOP), jnp.float32) ** shard_levels(seeds[2], (TOKENS, TOP), ((0, 32),), -0.2, 0.2), 0.1, 0.6)
    w_gate = scatter_about(seeds[3], (EXPERTS, D, FF), D ** -0.5, 0.0625, ((0, 8), (2, 4)))
    w_up = scatter_about(seeds[4], (EXPERTS, D, FF), D ** -0.5, 0.0625, ((0, 8), (2, 4)))
    w_down = scatter_about(seeds[5], (EXPERTS, FF, D), FF ** -0.5, 0.125, ((0, 8), (1, 4)))
    return {"tokens": tokens, "expert_ids": expert_ids, "gate_weights": gate_weights, "w_gate": w_gate, "w_up": w_up, "w_down": w_down}


def reference(tokens, expert_ids, gate_weights, w_gate, w_up, w_down):
    buffer_rows = (TOKENS // TOK_DEV) * CAP
    blocks = FF // FF_DEV

    def one_expert(running, expert_index):
        naming = expert_ids == expert_index
        chosen = jnp.any(naming, axis=1)
        weight = jnp.sum(jnp.where(naming, gate_weights, 0.0), axis=1)
        picked = jnp.nonzero(chosen, size=buffer_rows, fill_value=0)[0].astype(jnp.int32)
        occupied = jnp.arange(buffer_rows, dtype=jnp.int32) < jnp.sum(chosen.astype(jnp.int32))
        gathered = tokens[picked]
        gate_proj = jnp.dot(gathered, w_gate[expert_index], preferred_element_type=jnp.float32)
        up_proj = jnp.dot(gathered, w_up[expert_index], preferred_element_type=jnp.float32)
        hidden = (jax.nn.silu(gate_proj) * up_proj).astype(jnp.bfloat16)
        down_rows = w_down[expert_index]
        result = jnp.zeros((buffer_rows, D), jnp.float32)
        for block_index in range(blocks):
            lower = block_index * FF_DEV
            block_part = jnp.dot(hidden[:, lower:lower + FF_DEV], down_rows[lower:lower + FF_DEV], preferred_element_type=jnp.float32).astype(jnp.bfloat16)
            result = result + lax.optimization_barrier(block_part).astype(jnp.float32)
        expert_out = lax.optimization_barrier(result.astype(jnp.bfloat16)).astype(jnp.float32)
        row_scale = jnp.where(occupied, weight[picked], 0.0)
        running = running.at[picked].add(row_scale[:, None] * expert_out)
        return running, None

    running, _ = lax.scan(one_expert, jnp.zeros((TOKENS, D), jnp.float32), jnp.arange(EXPERTS, dtype=jnp.int32))
    return running.astype(jnp.bfloat16)
```

```python
import jax
import jax.numpy as jnp
from jax import lax
from jax.sharding import PartitionSpec as P

AXES = ("sect", "grp", "dev")


def body(tokens, expert_ids, gate_weights, w_gate, w_up, w_down):
    local_experts = w_gate.shape[0]
    first = lax.axis_index(("sect", "grp")) * local_experts
    rows = lax.all_gather(tokens, AXES, axis=0, tiled=True)
    ids = lax.all_gather(expert_ids, AXES, axis=0, tiled=True)
    weights = lax.all_gather(gate_weights, AXES, axis=0, tiled=True)
    local = first + jnp.arange(local_experts, dtype=jnp.int32)
    scale = jnp.sum(
        jnp.where(ids[None] == local[:, None, None], weights[None], 0.0), axis=2
    )
    gate_proj = jnp.einsum("rd,jdf->jrf", rows, w_gate, preferred_element_type=jnp.float32)
    up_proj = jnp.einsum("rd,jdf->jrf", rows, w_up, preferred_element_type=jnp.float32)
    hidden = (jax.nn.silu(gate_proj) * up_proj * scale[:, :, None]).astype(jnp.bfloat16)
    partial = jnp.einsum(
        "jrf,jfd->rd", hidden, w_down, preferred_element_type=jnp.float32
    ).astype(jnp.bfloat16)
    return lax.psum_scatter(partial, AXES, scatter_dimension=0, tiled=True)


def solution(mesh):
    in_specs = (
        P(AXES, None),
        P(AXES, None),
        P(AXES, None),
        P(("sect", "grp"), None, "dev"),
        P(("sect", "grp"), None, "dev"),
        P(("sect", "grp"), "dev", None),
    )
    return jax.shard_map(
        body, mesh=mesh, in_specs=in_specs, out_specs=P(AXES, None), check_vma=False
    )
```

```python
import functools

import jax
import jax.numpy as jnp
from jax import lax
from jax.experimental import pallas as pl
from jax.experimental.pallas import tpu as pltpu
from jax.sharding import PartitionSpec as P

AXES = ("sect", "grp", "dev")
CHUNKS = 2


def swap(value, axis, mask):
    return lax.ppermute(value, axis, [(i, i ^ mask) for i in range(lax.axis_size(axis))])


def bits_of(size):
    return [1 << b for b in range(size.bit_length() - 1)]


def split_columns(width):
    half = width // 256 * 128
    return half


def gather_rows(block):
    lanes, groups, sects = (lax.axis_size(a) for a in ("dev", "grp", "sect"))
    line = jnp.concatenate([block] + [swap(block, "dev", m) for m in range(1, lanes)], axis=0)
    half = split_columns(block.shape[1])
    if groups == 4:
        by_x, by_y = swap(line, "grp", 1), swap(line, "grp", 2)
        corner = [swap(by_x[:, :half], "grp", 2), swap(by_y[:, half:], "grp", 1)]
        entries = [[line], [by_x], [by_y], corner]
    else:
        entries = [[line]]
        for bit in bits_of(groups):
            entries = entries + [[swap(p, "grp", bit) for p in e] for e in entries]
    for bit in bits_of(sects):
        entries = entries + [[swap(p, "sect", bit) for p in e] for e in entries]
    return entries


def up_kernel(layout, width, first_ref, *refs):
    pieces = refs[: sum(layout)]
    gate_ref, upw_ref, hidden_ref, rows_ref, acc_ref = refs[sum(layout):]
    step = pl.program_id(0)
    experts, depth, hidden = gate_ref.shape
    line = pieces[0].shape[0]

    @pl.when(step == 0)
    def _():
        at = 0
        for entry, count in enumerate(layout):
            left = 0
            for piece in pieces[at:at + count]:
                rows_ref[pl.ds(entry * line, line), pl.ds(left, piece.shape[1])] = piece[...]
                left += piece.shape[1]
            at += count
        acc_ref[...] = jnp.zeros_like(acc_ref)

    here = rows_ref[:, pl.ds(pl.multiple_of(step * depth, 128), depth)]
    for e in range(experts):
        acc_ref[2 * e] += jnp.dot(here, gate_ref[e], preferred_element_type=jnp.float32)
        acc_ref[2 * e + 1] += jnp.dot(here, upw_ref[e], preferred_element_type=jnp.float32)

    @pl.when(step == pl.num_programs(0) - 1)
    def _():
        extra = rows_ref[:, width:].astype(jnp.float32)
        lane = lax.broadcasted_iota(jnp.int32, extra.shape, 1)
        for e in range(experts):
            mine = lax.rem(lane, extra.shape[1] // 2) == first_ref[0] + e
            scale = jnp.sum(jnp.where(mine, extra, 0.0), axis=1, keepdims=True)
            gate = acc_ref[2 * e]
            value = gate / (1.0 + jnp.exp(-gate)) * acc_ref[2 * e + 1] * scale
            hidden_ref[:, pl.ds(e * hidden, hidden)] = value.astype(jnp.bfloat16)


def up_call(first, entries, w_gate, w_up):
    layout = [len(e) for e in entries]
    flat = [p for e in entries for p in e]
    experts, width, hidden = w_gate.shape
    line = flat[0].shape[0]
    full = sum(p.shape[1] for p in entries[0])
    rows = line * len(entries)
    depth = 1024 if width % 1024 == 0 else 128
    weight = pl.BlockSpec((experts, depth, hidden), lambda i: (0, i, 0))
    return pl.pallas_call(
        functools.partial(up_kernel, layout, width),
        out_shape=jax.ShapeDtypeStruct((rows, experts * hidden), jnp.bfloat16),
        grid=(width // depth,),
        in_specs=[pl.BlockSpec(memory_space=pltpu.SMEM)]
        + [pl.BlockSpec(p.shape, lambda i: (0, 0)) for p in flat]
        + [weight, weight],
        out_specs=pl.BlockSpec((rows, experts * hidden), lambda i: (0, 0)),
        scratch_shapes=[
            pltpu.VMEM((rows, full), jnp.bfloat16),
            pltpu.VMEM((2 * experts, rows, hidden), jnp.float32),
        ],
        compiler_params=pltpu.CompilerParams(vmem_limit_bytes=48 * 2**20),
        cost_estimate=pl.CostEstimate(
            flops=4 * rows * experts * width * hidden,
            bytes_accessed=4 * experts * width * hidden,
            transcendentals=0,
        ),
        name="gate_up",
    )(first, *flat, w_gate, w_up)


def down_kernel(order, line, hidden_ref, down_ref, keep_ref, send_ref):
    experts, hidden, _ = down_ref.shape
    total = None
    for e in range(experts):
        part = jnp.dot(
            hidden_ref[:, pl.ds(e * hidden, hidden)], down_ref[e],
            preferred_element_type=jnp.float32,
        )
        total = part if total is None else total + part
    total = total.astype(jnp.bfloat16)
    groups = len(order)
    for place, entry in enumerate(order):
        keep_ref[pl.ds(place * line, line), :] = total[entry * line:(entry + 1) * line]
        low = (groups + entry) * line
        send_ref[pl.ds(place * line, line), :] = total[low:low + line]


def down_call(order, line, hidden, w_down, start, columns):
    experts, depth, _ = w_down.shape
    rows = line * len(order)
    block = 896 if columns % 896 == 0 else 128
    offset = start // block
    out = jax.ShapeDtypeStruct((rows, columns), jnp.bfloat16)
    out_block = pl.BlockSpec((rows, block), lambda i: (0, i))
    return pl.pallas_call(
        functools.partial(down_kernel, order, line),
        out_shape=(out, out),
        grid=(columns // block,),
        in_specs=[
            pl.BlockSpec(hidden.shape, lambda i: (0, 0)),
            pl.BlockSpec((experts, depth, block), lambda i: (0, 0, offset + i)),
        ],
        out_specs=(out_block, out_block),
        compiler_params=pltpu.CompilerParams(vmem_limit_bytes=32 * 2**20),
        cost_estimate=pl.CostEstimate(
            flops=2 * hidden.shape[0] * experts * depth * columns,
            bytes_accessed=2 * experts * depth * columns,
            transcendentals=0,
        ),
        name="down",
    )(hidden, w_down)


def add(*values):
    total = values[0].astype(jnp.float32)
    for value in values[1:]:
        total = total + value.astype(jnp.float32)
    return total.astype(jnp.bfloat16)


def body(tokens, expert_ids, gate_weights, w_gate, w_up, w_down):
    sects, groups, lanes = (lax.axis_size(a) for a in AXES)
    row_count, width = tokens.shape
    experts = w_gate.shape[0]
    expert_count = sects * groups * experts
    first = lax.axis_index(("sect", "grp")).astype(jnp.int32) * experts

    half = -(-expert_count // 64) * 64
    catalog = jnp.arange(half, dtype=jnp.int32)
    dense = jnp.sum(
        jnp.where(expert_ids[:, :, None] == catalog, gate_weights[:, :, None], 0.0), axis=1
    )
    high = lax.reduce_precision(dense, 8, 7)
    extra = jnp.concatenate([high, dense - high], axis=1).astype(jnp.bfloat16)
    entries = gather_rows(jnp.concatenate([tokens, extra], axis=1))

    hidden = up_call(first.reshape(1), entries, w_gate, w_up)

    line = lanes * row_count
    results = []
    chunk = width // CHUNKS
    for c in range(CHUNKS):
        bits = bits_of(groups)
        bits = bits if c % 2 else bits[::-1]
        order = [0]
        for bit in bits:
            order = order + [o | bit for o in order]
        keep, send = down_call(order, line, hidden, w_down, c * chunk, chunk)
        value = add(keep, swap(send, "sect", 1))
        for bit in bits[::-1]:
            middle = value.shape[0] // 2
            arrived = swap(value[middle:], "grp", bit)
            value = add(value[:middle], arrived)
        pieces = [value[:row_count]]
        for m in range(1, lanes):
            pieces.append(swap(value[m * row_count:(m + 1) * row_count], "dev", m))
        results.append(add(*pieces))
    return jnp.concatenate(results, axis=1)


def solution(mesh):
    in_specs = (
        P(AXES, None),
        P(AXES, None),
        P(AXES, None),
        P(("sect", "grp"), None, "dev"),
        P(("sect", "grp"), None, "dev"),
        P(("sect", "grp"), "dev", None),
    )
    return jax.shard_map(
        body, mesh=mesh, in_specs=in_specs, out_specs=P(AXES, None), check_vma=False
    )
```

```python
import functools

import jax
import jax.numpy as jnp
from jax import lax
from jax.experimental import pallas as pl
from jax.experimental.pallas import tpu as pltpu
from jax.sharding import PartitionSpec as P

AXES = ("sect", "grp", "dev")
CHUNKS = 2


def swap(value, axis, mask):
    return lax.ppermute(value, axis, [(i, i ^ mask) for i in range(lax.axis_size(axis))])


def bits_of(size):
    return [1 << b for b in range(size.bit_length() - 1)]


def split_columns(width):
    half = width // 256 * 128
    return half


def gather_rows(block):
    lanes, groups, sects = (lax.axis_size(a) for a in ("dev", "grp", "sect"))
    line = jnp.concatenate([block] + [swap(block, "dev", m) for m in range(1, lanes)], axis=0)
    half = split_columns(block.shape[1])
    if groups == 4:
        by_x, by_y = swap(line, "grp", 1), swap(line, "grp", 2)
        corner = [swap(by_x[:, :half], "grp", 2), swap(by_y[:, half:], "grp", 1)]
        entries = [[line], [by_x], [by_y], corner]
    else:
        entries = [[line]]
        for bit in bits_of(groups):
            entries = entries + [[swap(p, "grp", bit) for p in e] for e in entries]
    for bit in bits_of(sects):
        entries = entries + [[swap(p, "sect", bit) for p in e] for e in entries]
    return entries


def up_kernel(layout, width, first_ref, *refs):
    pieces = refs[: sum(layout)]
    gate_ref, upw_ref, hidden_ref, rows_ref, acc_ref = refs[sum(layout):]
    experts, _, hidden = gate_ref.shape
    line = pieces[0].shape[0]
    depth = 1024 if width % 1024 == 0 else 128

    at = 0
    for entry, count in enumerate(layout):
        left = 0
        for piece in pieces[at:at + count]:
            rows_ref[pl.ds(entry * line, line), pl.ds(left, piece.shape[1])] = piece[...]
            left += piece.shape[1]
        at += count
    acc_ref[...] = jnp.zeros_like(acc_ref)

    @pl.loop(0, width // depth)
    def _(step):
        span = pl.ds(pl.multiple_of(step * depth, depth), depth)
        here = rows_ref[:, span]
        for e in range(experts):
            acc_ref[2 * e] += jnp.dot(
                here, gate_ref[e, span, :], preferred_element_type=jnp.float32
            )
            acc_ref[2 * e + 1] += jnp.dot(
                here, upw_ref[e, span, :], preferred_element_type=jnp.float32
            )

    extra = rows_ref[:, width:].astype(jnp.float32)
    lane = lax.broadcasted_iota(jnp.int32, extra.shape, 1)
    for e in range(experts):
        mine = lax.rem(lane, extra.shape[1] // 2) == first_ref[0] + e
        scale = jnp.sum(jnp.where(mine, extra, 0.0), axis=1, keepdims=True)
        gate = acc_ref[2 * e]
        value = gate / (1.0 + jnp.exp(-gate)) * acc_ref[2 * e + 1] * scale
        hidden_ref[:, pl.ds(e * hidden, hidden)] = value.astype(jnp.bfloat16)


def in_vmem(value):
    return pltpu.with_memory_space_constraint(value, pltpu.VMEM)


def up_call(first, entries, w_gate, w_up):
    layout = [len(e) for e in entries]
    flat = [p for e in entries for p in e]
    experts, width, hidden = w_gate.shape
    line = flat[0].shape[0]
    full = sum(p.shape[1] for p in entries[0])
    rows = line * len(entries)
    whole = pl.BlockSpec(memory_space=pltpu.VMEM)
    return pl.pallas_call(
        functools.partial(up_kernel, layout, width),
        out_shape=jax.ShapeDtypeStruct((rows, experts * hidden), jnp.bfloat16),
        in_specs=[pl.BlockSpec(memory_space=pltpu.SMEM)] + [whole] * (len(flat) + 2),
        out_specs=whole,
        scratch_shapes=[
            pltpu.VMEM((rows, full), jnp.bfloat16),
            pltpu.VMEM((2 * experts, rows, hidden), jnp.float32),
        ],
        compiler_params=pltpu.CompilerParams(vmem_limit_bytes=kernel_bytes(rows, full)),
        cost_estimate=pl.CostEstimate(
            flops=4 * rows * experts * width * hidden,
            bytes_accessed=2 * rows * width,
            transcendentals=rows * experts * hidden,
        ),
        name="gate_up",
    )(first, *flat, in_vmem(w_gate), in_vmem(w_up))


def kernel_bytes(rows, width):
    return 6 * rows * width + 6 * 2**20


def down_kernel(order, line, start, hidden_ref, down_ref, keep_ref, send_ref):
    experts, hidden, _ = down_ref.shape
    columns = keep_ref.shape[1]
    block = 512 if columns % 512 == 0 else 128
    groups = len(order)

    @pl.loop(0, columns // block)
    def _(step):
        at = pl.multiple_of(step * block, block)
        total = None
        for e in range(experts):
            part = jnp.dot(
                hidden_ref[:, pl.ds(e * hidden, hidden)],
                down_ref[e, :, pl.ds(start + at, block)],
                preferred_element_type=jnp.float32,
            )
            total = part if total is None else total + part
        total = total.astype(jnp.bfloat16)
        for place, entry in enumerate(order):
            rows = pl.ds(place * line, line)
            keep_ref[rows, pl.ds(at, block)] = total[entry * line:(entry + 1) * line]
            low = (groups + entry) * line
            send_ref[rows, pl.ds(at, block)] = total[low:low + line]


def down_call(order, line, hidden, w_down, start, columns):
    experts, depth, _ = w_down.shape
    rows = line * len(order)
    out = jax.ShapeDtypeStruct((rows, columns), jnp.bfloat16)
    whole = pl.BlockSpec(memory_space=pltpu.VMEM)
    return pl.pallas_call(
        functools.partial(down_kernel, order, line, start),
        out_shape=(out, out),
        in_specs=[whole, whole],
        out_specs=(whole, whole),
        compiler_params=pltpu.CompilerParams(
            vmem_limit_bytes=kernel_bytes(2 * rows, columns)
        ),
        cost_estimate=pl.CostEstimate(
            flops=2 * hidden.shape[0] * experts * depth * columns,
            bytes_accessed=4 * rows * columns,
            transcendentals=0,
        ),
        name="down",
    )(hidden, in_vmem(w_down))


def add(*values):
    total = values[0].astype(jnp.float32)
    for value in values[1:]:
        total = total + value.astype(jnp.float32)
    return total.astype(jnp.bfloat16)


def body(tokens, expert_ids, gate_weights, w_gate, w_up, w_down):
    sects, groups, lanes = (lax.axis_size(a) for a in AXES)
    row_count, width = tokens.shape
    experts = w_gate.shape[0]
    expert_count = sects * groups * experts
    first = lax.axis_index(("sect", "grp")).astype(jnp.int32) * experts

    half = -(-expert_count // 64) * 64
    catalog = jnp.arange(half, dtype=jnp.int32)
    dense = jnp.sum(
        jnp.where(expert_ids[:, :, None] == catalog, gate_weights[:, :, None], 0.0), axis=1
    )
    high = lax.reduce_precision(dense, 8, 7)
    extra = jnp.concatenate([high, dense - high], axis=1).astype(jnp.bfloat16)
    entries = gather_rows(jnp.concatenate([tokens, extra], axis=1))

    hidden = up_call(first.reshape(1), entries, w_gate, w_up)

    line = lanes * row_count
    results = []
    chunk = width // CHUNKS
    for c in range(CHUNKS):
        bits = bits_of(groups)
        bits = bits if c % 2 else bits[::-1]
        order = [0]
        for bit in bits:
            order = order + [o | bit for o in order]
        keep, send = down_call(order, line, hidden, w_down, c * chunk, chunk)
        value = add(keep, swap(send, "sect", 1))
        for bit in bits[::-1]:
            middle = value.shape[0] // 2
            arrived = swap(value[middle:], "grp", bit)
            value = add(value[:middle], arrived)
        pieces = [value[:row_count]]
        for m in range(1, lanes):
            pieces.append(swap(value[m * row_count:(m + 1) * row_count], "dev", m))
        results.append(add(*pieces))
    return jnp.concatenate(results, axis=1)


def solution(mesh):
    in_specs = (
        P(AXES, None),
        P(AXES, None),
        P(AXES, None),
        P(("sect", "grp"), None, "dev"),
        P(("sect", "grp"), None, "dev"),
        P(("sect", "grp"), "dev", None),
    )
    return jax.shard_map(
        body, mesh=mesh, in_specs=in_specs, out_specs=P(AXES, None), check_vma=False
    )
```

```python
import functools

import jax
import jax.numpy as jnp
from jax import lax
from jax.experimental import pallas as pl
from jax.experimental.pallas import tpu as pltpu
from jax.sharding import PartitionSpec as P

AXES = ("sect", "grp", "dev")
CHUNKS = 2


def swap(value, axis, mask):
    return lax.ppermute(value, axis, [(i, i ^ mask) for i in range(lax.axis_size(axis))])


def bits_of(size):
    return [1 << b for b in range(size.bit_length() - 1)]


def split_columns(width):
    half = width // 256 * 128
    return half


def gather_rows(block, w_up):
    lanes, groups, sects = (lax.axis_size(a) for a in ("dev", "grp", "sect"))
    arrived = [swap(block, "dev", m) for m in range(1, lanes)]
    w_up, token = fetch(w_up, block)
    arrived, token = lax.optimization_barrier((arrived, token))
    line = jnp.concatenate([block] + arrived, axis=0)
    half = split_columns(block.shape[1])
    if groups == 4:
        by_x, by_y = swap(line, "grp", 1), swap(line, "grp", 2)
        corner = [swap(by_x[:, :half], "grp", 2), swap(by_y[:, half:], "grp", 1)]
        entries = [[line], [by_x], [by_y], corner]
    else:
        entries = [[line]]
        for bit in bits_of(groups):
            entries = entries + [[swap(p, "grp", bit) for p in e] for e in entries]
    for bit in bits_of(sects):
        entries = entries + [[swap(p, "sect", bit) for p in e] for e in entries]
    return entries, w_up, token


def up_kernel(layout, width, first_ref, token_ref, *refs):
    pieces = refs[: sum(layout)]
    gate_hbm, upw_ref, hidden_ref, rows_ref, gate_ref, up_ref, sems = refs[sum(layout):]
    experts, _, hidden = upw_ref.shape
    line = pieces[0].shape[0]
    block = min(256, hidden)
    steps = hidden // block

    def span_of(step):
        return pl.ds(pl.multiple_of(step * block, block), block)

    def copy_of(e, step):
        span = span_of(step)
        return pltpu.make_async_copy(
            gate_hbm.at[e, :, span], gate_ref.at[e, :, span], sems.at[e, step]
        )

    for e in range(experts):
        for step in range(steps):
            copy_of(e, step).start()

    at = 0
    for entry, count in enumerate(layout):
        left = 0
        for piece in pieces[at:at + count]:
            rows_ref[pl.ds(entry * line, line), pl.ds(left, piece.shape[1])] = piece[...]
            left += piece.shape[1]
        at += count

    for e in range(experts):

        @pl.loop(0, steps)
        def _(step):
            span = span_of(step)
            up_ref[e, :, span] = jnp.dot(
                rows_ref[:, :width], upw_ref[e, :, span], preferred_element_type=jnp.float32
            )

    extra = rows_ref[:, width:].astype(jnp.float32)
    lane = lax.broadcasted_iota(jnp.int32, extra.shape, 1)
    for e in range(experts):
        mine = lax.rem(lane, extra.shape[1] // 2) == first_ref[0] + e
        scale = jnp.sum(jnp.where(mine, extra, 0.0), axis=1, keepdims=True)

        @pl.loop(0, steps)
        def _(step):
            span = span_of(step)
            copy_of(e, step).wait()
            gate = jnp.dot(
                rows_ref[:, :width], gate_ref[e, :, span], preferred_element_type=jnp.float32
            )
            value = gate / (1.0 + jnp.exp(-gate)) * up_ref[e, :, span] * scale
            out = pl.ds(pl.multiple_of(e * hidden + step * block, block), block)
            hidden_ref[:, out] = value.astype(jnp.bfloat16)


def fetch_kernel(parts, *refs):
    source_ref, target_ref, token_ref, sems = refs[-4:]
    depth = source_ref.shape[1] // parts
    copies = [
        pltpu.make_async_copy(
            source_ref.at[e, pl.ds(p * depth, depth)],
            target_ref.at[e, pl.ds(p * depth, depth)],
            sems.at[e * parts + p],
        )
        for e in range(source_ref.shape[0])
        for p in range(parts)
    ]
    for copy in copies:
        copy.start()
    token_ref[...] = jnp.zeros_like(token_ref)
    for copy in copies:
        copy.wait()


def fetch(weight, *after):
    parts = 4
    return pl.pallas_call(
        functools.partial(fetch_kernel, parts),
        out_shape=(
            pltpu.VMEM(weight.shape, weight.dtype),
            jax.ShapeDtypeStruct((8, 128), jnp.float32),
        ),
        in_specs=[pl.BlockSpec(memory_space=pl.ANY)] * (len(after) + 1),
        out_specs=(pl.BlockSpec(memory_space=pltpu.VMEM),) * 2,
        scratch_shapes=[pltpu.SemaphoreType.DMA((weight.shape[0] * parts,))],
        compiler_params=pltpu.CompilerParams(vmem_limit_bytes=2**20),
        cost_estimate=pl.CostEstimate(
            flops=0, bytes_accessed=2 * weight.size, transcendentals=0
        ),
        name="fetch",
    )(*after, pltpu.with_memory_space_constraint(weight, pltpu.HBM))


def up_call(first, entries, w_gate, w_up, token):
    layout = [len(e) for e in entries]
    flat = [p for e in entries for p in e]
    experts, width, hidden = w_gate.shape
    line = flat[0].shape[0]
    full = sum(p.shape[1] for p in entries[0])
    rows = line * len(entries)
    whole = pl.BlockSpec(memory_space=pltpu.VMEM)
    return pl.pallas_call(
        functools.partial(up_kernel, layout, width),
        out_shape=jax.ShapeDtypeStruct((rows, experts * hidden), jnp.bfloat16),
        in_specs=[pl.BlockSpec(memory_space=pltpu.SMEM), pl.BlockSpec(memory_space=pl.ANY)]
        + [whole] * len(flat)
        + [pl.BlockSpec(memory_space=pl.ANY), whole],
        out_specs=whole,
        scratch_shapes=[
            pltpu.VMEM((rows, full), jnp.bfloat16),
            pltpu.VMEM(w_gate.shape, w_gate.dtype),
            pltpu.VMEM((experts, rows, hidden), jnp.float32),
            pltpu.SemaphoreType.DMA((experts, hidden // min(256, hidden))),
        ],
        compiler_params=pltpu.CompilerParams(
            vmem_limit_bytes=kernel_bytes(rows, full) + 2 * w_gate.size
        ),
        cost_estimate=pl.CostEstimate(
            flops=4 * rows * experts * width * hidden,
            bytes_accessed=2 * rows * width,
            transcendentals=rows * experts * hidden,
        ),
        name="gate_up",
    )(
        first,
        token,
        *flat,
        pltpu.with_memory_space_constraint(w_gate, pltpu.HBM),
        pltpu.with_memory_space_constraint(w_up, pltpu.VMEM),
    )


def kernel_bytes(rows, width):
    return 4 * rows * width + 4 * 2**20


def down_kernel(order, line, hidden_ref, down_ref, keep_ref, send_ref):
    experts, hidden, block = down_ref.shape
    groups = len(order)
    weight = down_ref[...].reshape(experts * hidden, block)
    total = jnp.dot(hidden_ref[...], weight, preferred_element_type=jnp.float32)
    total = total.astype(jnp.bfloat16)
    for place, entry in enumerate(order):
        rows = pl.ds(place * line, line)
        keep_ref[rows, :] = total[entry * line:(entry + 1) * line]
        low = (groups + entry) * line
        send_ref[rows, :] = total[low:low + line]


def down_call(order, line, hidden, w_down, start, columns):
    experts, depth, _ = w_down.shape
    rows = line * len(order)
    block = 512 if columns % 512 == 0 else 128
    offset = start // block
    out = jax.ShapeDtypeStruct((rows, columns), jnp.bfloat16)
    out_block = pl.BlockSpec((rows, block), lambda i: (0, i))
    return pl.pallas_call(
        functools.partial(down_kernel, order, line),
        out_shape=(out, out),
        grid=(columns // block,),
        in_specs=[
            pl.BlockSpec(hidden.shape, lambda i: (0, 0)),
            pl.BlockSpec((experts, depth, block), lambda i: (0, 0, offset + i)),
        ],
        out_specs=(out_block, out_block),
        compiler_params=pltpu.CompilerParams(vmem_limit_bytes=kernel_bytes(2 * rows, 4096)),
        cost_estimate=pl.CostEstimate(
            flops=2 * hidden.shape[0] * experts * depth * columns,
            bytes_accessed=2 * experts * depth * columns,
            transcendentals=0,
        ),
        name="down",
    )(hidden, pltpu.with_memory_space_constraint(w_down, pltpu.HBM))


def add(*values):
    total = values[0].astype(jnp.float32)
    for value in values[1:]:
        total = total + value.astype(jnp.float32)
    return total.astype(jnp.bfloat16)


def body(tokens, expert_ids, gate_weights, w_gate, w_up, w_down):
    sects, groups, lanes = (lax.axis_size(a) for a in AXES)
    row_count, width = tokens.shape
    experts = w_gate.shape[0]
    expert_count = sects * groups * experts
    first = lax.axis_index(("sect", "grp")).astype(jnp.int32) * experts

    half = -(-expert_count // 64) * 64
    catalog = jnp.arange(half, dtype=jnp.int32)
    dense = jnp.sum(
        jnp.where(expert_ids[:, :, None] == catalog, gate_weights[:, :, None], 0.0), axis=1
    )
    high = lax.reduce_precision(dense, 8, 7)
    extra = jnp.concatenate([high, dense - high], axis=1).astype(jnp.bfloat16)
    entries, w_up, token = gather_rows(jnp.concatenate([tokens, extra], axis=1), w_up)

    hidden = up_call(first.reshape(1), entries, w_gate, w_up, token)

    line = lanes * row_count
    results = []
    chunk = width // CHUNKS
    for c in range(CHUNKS):
        bits = bits_of(groups)
        bits = bits if c % 2 else bits[::-1]
        order = [0]
        for bit in bits:
            order = order + [o | bit for o in order]
        keep, send = down_call(order, line, hidden, w_down, c * chunk, chunk)
        value = add(keep, swap(send, "sect", 1))
        for bit in bits[::-1]:
            middle = value.shape[0] // 2
            arrived = swap(value[middle:], "grp", bit)
            value = add(value[:middle], arrived)
        pieces = [value[:row_count]]
        for m in range(1, lanes):
            pieces.append(swap(value[m * row_count:(m + 1) * row_count], "dev", m))
        results.append(add(*pieces))
    return jnp.concatenate(results, axis=1)


def solution(mesh):
    in_specs = (
        P(AXES, None),
        P(AXES, None),
        P(AXES, None),
        P(("sect", "grp"), None, "dev"),
        P(("sect", "grp"), None, "dev"),
        P(("sect", "grp"), "dev", None),
    )
    return jax.shard_map(
        body, mesh=mesh, in_specs=in_specs, out_specs=P(AXES, None), check_vma=False
    )
```

```python
import functools

import jax
import jax.numpy as jnp
from jax import lax
from jax.experimental import pallas as pl
from jax.experimental.pallas import tpu as pltpu
from jax.sharding import PartitionSpec as P

AXES = ("sect", "grp", "dev")
CHUNKS = 2


def swap(value, axis, mask):
    return lax.ppermute(value, axis, [(i, i ^ mask) for i in range(lax.axis_size(axis))])


def bits_of(size):
    return [1 << b for b in range(size.bit_length() - 1)]


def vmem_call(kernel, out_shape, name, *operands):
    whole = pl.BlockSpec(memory_space=pltpu.VMEM)
    return pl.pallas_call(
        kernel,
        out_shape=out_shape,
        in_specs=[whole] * len(operands),
        out_specs=jax.tree.map(lambda _: whole, out_shape),
        compiler_params=pltpu.CompilerParams(vmem_limit_bytes=4 * 2**20),
        name=name,
    )(*operands)


def extend_kernel(tokens_ref, ids_ref, weights_ref, out_ref):
    rows, width = tokens_ref.shape
    half = (out_ref.shape[1] - width) // 2
    lane = lax.broadcasted_iota(jnp.int32, (rows, half * 2), 1)
    dense = jnp.zeros((rows, half * 2), jnp.float32)
    for k in range(ids_ref.shape[1]):
        mine = lax.rem(lane, half) == ids_ref[:, k:k + 1]
        dense = dense + jnp.where(mine, weights_ref[:, k:k + 1], 0.0)
    high = dense.astype(jnp.bfloat16).astype(jnp.float32)
    out_ref[:, :width] = tokens_ref[...]
    out_ref[:, width:] = jnp.where(lane < half, high, dense - high).astype(jnp.bfloat16)


def extend(tokens, ids, weights, half):
    rows, width = tokens.shape
    out = jax.ShapeDtypeStruct((rows, width + 2 * half), tokens.dtype)
    return vmem_call(extend_kernel, out, "extend", tokens, ids, weights)


def join_kernel(*refs):
    pieces, out_ref = refs[:-1], refs[-1]
    values = [p[...].astype(jnp.float32) for p in pieces]
    out_ref[...] = jnp.concatenate(values, axis=0).astype(out_ref.dtype)


def join(pieces):
    rows, width = pieces[0].shape
    out = jax.ShapeDtypeStruct((rows * len(pieces), width), pieces[0].dtype)
    return vmem_call(join_kernel, out, "join", *pieces)


def halves_kernel(left_ref, right_ref, left_out, right_out):
    half = left_out.shape[1]
    left_out[...] = left_ref[:, :half]
    right_out[...] = right_ref[:, half:]


def halves(left, right):
    rows, width = left.shape
    half = width // 256 * 128
    out = (
        jax.ShapeDtypeStruct((rows, half), left.dtype),
        jax.ShapeDtypeStruct((rows, width - half), left.dtype),
    )
    return vmem_call(halves_kernel, out, "halves", left, right)


def gather_rows(block, w_gate, w_up):
    lanes, groups, sects = (lax.axis_size(a) for a in ("dev", "grp", "sect"))
    arrived = [swap(block, "dev", m) for m in range(1, lanes)]
    w_gate, token = fetch(w_gate, (block,))
    arrived, token = lax.optimization_barrier((arrived, token))
    line = join([block] + arrived)
    if groups == 4:
        by_x, by_y = swap(line, "grp", 1), swap(line, "grp", 2)
        w_up, token, w_gate = fetch(w_up, (line, token), (w_gate,))
        by_x, by_y, token = lax.optimization_barrier((by_x, by_y, token))
        from_x, from_y = halves(by_x, by_y)
        corner = [swap(from_x, "grp", 2), swap(from_y, "grp", 1)]
        entries = [[line], [by_x], [by_y], corner]
    else:
        entries = [[line]]
        w_up, token, w_gate = fetch(w_up, (line, token), (w_gate,))
        for bit in bits_of(groups):
            entries = entries + [[swap(p, "grp", bit) for p in e] for e in entries]
    for bit in bits_of(sects):
        entries = entries + [[swap(p, "sect", bit) for p in e] for e in entries]
    return entries, w_gate, w_up, token


def up_kernel(layout, width, first_ref, token_ref, *refs):
    pieces = refs[: sum(layout)]
    gate_ref, upw_ref, down_hbm, hidden_ref, down_ref, rows_ref, value_ref, sems = refs[
        sum(layout):
    ]
    experts, _, hidden = upw_ref.shape
    line = pieces[0].shape[0]
    block = min(256, hidden)

    def copies(e):
        for c in range(width // hidden):
            yield pltpu.make_async_copy(
                down_hbm.at[e, :, pl.ds(c * hidden, hidden)],
                down_ref.at[e, pl.ds(c * hidden, hidden)],
                sems.at[e, c],
            )

    at = 0
    for entry, count in enumerate(layout):
        left = 0
        for piece in pieces[at:at + count]:
            rows_ref[pl.ds(entry * line, line), pl.ds(left, piece.shape[1])] = piece[...]
            left += piece.shape[1]
        at += count

    for e in range(experts):

        @pl.loop(0, hidden // block)
        def _(step):
            span = pl.ds(pl.multiple_of(step * block, block), block)
            gate = jnp.dot(
                rows_ref[:, :width], gate_ref[e, :, span], preferred_element_type=jnp.float32
            )
            value_ref[e, :, span] = gate / (1.0 + jnp.exp(-gate))

        for copy in copies(e):
            copy.start()

    extra = rows_ref[:, width:].astype(jnp.float32)
    lane = lax.broadcasted_iota(jnp.int32, extra.shape, 1)
    for e in range(experts):
        mine = lax.rem(lane, extra.shape[1] // 2) == first_ref[0] + e
        scale = jnp.sum(jnp.where(mine, extra, 0.0), axis=1, keepdims=True)

        @pl.loop(0, hidden // block)
        def _(step):
            span = pl.ds(pl.multiple_of(step * block, block), block)
            up = jnp.dot(
                rows_ref[:, :width], upw_ref[e, :, span], preferred_element_type=jnp.float32
            )
            out = pl.ds(pl.multiple_of(e * hidden + step * block, block), block)
            hidden_ref[:, out] = (value_ref[e, :, span] * up * scale).astype(jnp.bfloat16)

    for e in range(experts):
        for copy in copies(e):
            copy.wait()


def fetch_kernel(parts, *refs):
    source_ref, target_ref, token_ref, *_, sems = refs
    depth = source_ref.shape[1] // parts
    copies = [
        pltpu.make_async_copy(
            source_ref.at[e, pl.ds(p * depth, depth)],
            target_ref.at[e, pl.ds(p * depth, depth)],
            sems.at[e * parts + p],
        )
        for e in range(source_ref.shape[0])
        for p in range(parts)
    ]
    for copy in copies:
        copy.start()
    token_ref[...] = jnp.zeros_like(token_ref)
    for copy in copies:
        copy.wait()


def fetch(weight, after, carried=()):
    parts = 4
    in_hbm = pl.BlockSpec(memory_space=pl.ANY)
    in_vmem = pl.BlockSpec(memory_space=pltpu.VMEM)
    carry, pins = len(carried), [pltpu.with_memory_space_constraint(c, pltpu.VMEM) for c in carried]

    def kernel(*refs):
        fetch_kernel(parts, *refs[len(after) + carry:])

    return pl.pallas_call(
        kernel,
        out_shape=(
            pltpu.VMEM(weight.shape, weight.dtype),
            jax.ShapeDtypeStruct((8, 128), jnp.float32),
        )
        + tuple(pltpu.VMEM(c.shape, c.dtype) for c in carried),
        in_specs=[in_hbm] * len(after) + [in_vmem] * carry + [in_hbm],
        out_specs=(in_vmem,) * (2 + carry),
        input_output_aliases={len(after) + i: 2 + i for i in range(carry)},
        scratch_shapes=[pltpu.SemaphoreType.DMA((weight.shape[0] * parts,))],
        compiler_params=pltpu.CompilerParams(vmem_limit_bytes=2**20),
        cost_estimate=pl.CostEstimate(
            flops=0, bytes_accessed=2 * weight.size, transcendentals=0
        ),
        name="fetch",
    )(*after, *pins, pltpu.with_memory_space_constraint(weight, pltpu.HBM))


def up_call(first, entries, w_gate, w_up, w_down, token):
    layout = [len(e) for e in entries]
    flat = [p for e in entries for p in e]
    experts, width, hidden = w_up.shape
    line = flat[0].shape[0]
    full = sum(p.shape[1] for p in entries[0])
    rows = line * len(entries)
    whole = pl.BlockSpec(memory_space=pltpu.VMEM)
    anywhere = pl.BlockSpec(memory_space=pl.ANY)
    return pl.pallas_call(
        functools.partial(up_kernel, layout, width),
        out_shape=(
            jax.ShapeDtypeStruct((rows, experts * hidden), jnp.bfloat16),
            pltpu.VMEM(w_gate.shape, w_gate.dtype),
        ),
        in_specs=[pl.BlockSpec(memory_space=pltpu.SMEM), anywhere]
        + [whole] * (len(flat) + 2)
        + [anywhere],
        out_specs=(whole, whole),
        scratch_shapes=[
            pltpu.VMEM((rows, full), jnp.bfloat16),
            pltpu.VMEM((experts, rows, hidden), jnp.float32),
            pltpu.SemaphoreType.DMA((experts, width // hidden)),
        ],
        input_output_aliases={2 + len(flat): 1},
        compiler_params=pltpu.CompilerParams(vmem_limit_bytes=kernel_bytes(rows, full)),
        cost_estimate=pl.CostEstimate(
            flops=4 * rows * experts * width * hidden,
            bytes_accessed=2 * w_down.size,
            transcendentals=rows * experts * hidden,
        ),
        name="gate_up",
    )(
        first,
        token,
        *flat,
        pltpu.with_memory_space_constraint(w_gate, pltpu.VMEM),
        pltpu.with_memory_space_constraint(w_up, pltpu.VMEM),
        pltpu.with_memory_space_constraint(w_down, pltpu.HBM),
    )


def kernel_bytes(rows, width):
    return 2 * rows * width + 4 * 2**20


def down_kernel(order, line, start, hidden_ref, down_ref, keep_ref, send_ref):
    experts, _, hidden = down_ref.shape
    groups = len(order)

    @pl.loop(0, keep_ref.shape[1] // hidden)
    def _(step):
        rows = pl.ds(pl.multiple_of((start // hidden + step) * hidden, hidden), hidden)
        weight = down_ref[:, rows, :].reshape(experts * hidden, hidden)
        total = jnp.dot(hidden_ref[...], weight, preferred_element_type=jnp.float32)
        total = total.astype(jnp.bfloat16)
        columns = pl.ds(pl.multiple_of(step * hidden, hidden), hidden)
        for place, entry in enumerate(order):
            rows = pl.ds(place * line, line)
            keep_ref[rows, columns] = total[entry * line:(entry + 1) * line]
            low = (groups + entry) * line
            send_ref[rows, columns] = total[low:low + line]


def down_call(order, line, hidden, w_down, start, columns):
    rows = line * len(order)
    out = jax.ShapeDtypeStruct((rows, columns), jnp.bfloat16)
    whole = pl.BlockSpec(memory_space=pltpu.VMEM)
    return pl.pallas_call(
        functools.partial(down_kernel, order, line, start),
        out_shape=(out, out),
        in_specs=[whole, whole],
        out_specs=(whole, whole),
        compiler_params=pltpu.CompilerParams(vmem_limit_bytes=4 * 2**20),
        cost_estimate=pl.CostEstimate(
            flops=2 * hidden.size * columns,
            bytes_accessed=4 * rows * columns,
            transcendentals=0,
        ),
        name="down",
    )(hidden, pltpu.with_memory_space_constraint(w_down, pltpu.VMEM))


def add(*values):
    total = values[0].astype(jnp.float32)
    for value in values[1:]:
        total = total + value.astype(jnp.float32)
    return total.astype(jnp.bfloat16)


def body(tokens, expert_ids, gate_weights, w_gate, w_up, w_down):
    sects, groups, lanes = (lax.axis_size(a) for a in AXES)
    row_count, width = tokens.shape
    experts = w_gate.shape[0]
    expert_count = sects * groups * experts
    first = lax.axis_index(("sect", "grp")).astype(jnp.int32) * experts

    half = -(-expert_count // 64) * 64
    block = extend(tokens, expert_ids, gate_weights, half)
    entries, w_gate, w_up, token = gather_rows(block, w_gate, w_up)
    hidden, w_down = up_call(first.reshape(1), entries, w_gate, w_up, w_down, token)

    line = lanes * row_count
    results = []
    chunk = width // CHUNKS
    for c in range(CHUNKS):
        bits = bits_of(groups)
        bits = bits if c % 2 else bits[::-1]
        order = [0]
        for bit in bits:
            order = order + [o | bit for o in order]
        keep, send = down_call(order, line, hidden, w_down, c * chunk, chunk)
        value = add(keep, swap(send, "sect", 1))
        for bit in bits[::-1]:
            middle = value.shape[0] // 2
            arrived = swap(value[middle:], "grp", bit)
            value = add(value[:middle], arrived)
        pieces = [value[:row_count]]
        for m in range(1, lanes):
            pieces.append(swap(value[m * row_count:(m + 1) * row_count], "dev", m))
        results.append(add(*pieces))
    return jnp.concatenate(results, axis=1)


def solution(mesh):
    in_specs = (
        P(AXES, None),
        P(AXES, None),
        P(AXES, None),
        P(("sect", "grp"), None, "dev"),
        P(("sect", "grp"), None, "dev"),
        P(("sect", "grp"), "dev", None),
    )
    return jax.shard_map(
        body, mesh=mesh, in_specs=in_specs, out_specs=P(AXES, None), check_vma=False
    )
```

```python
import functools

import jax
import jax.numpy as jnp
from jax import lax
from jax.experimental import pallas as pl
from jax.experimental.pallas import tpu as pltpu
from jax.sharding import PartitionSpec as P

AXES = ("sect", "grp", "dev")
CHUNKS = 2
VMEM_LIMIT = 30 * 2**20


def swap(value, axis, mask):
    return lax.ppermute(value, axis, [(i, i ^ mask) for i in range(lax.axis_size(axis))])


def bits_of(size):
    return [1 << b for b in range(size.bit_length() - 1)]


def vmem_call(kernel, out_shape, name, *operands):
    whole = pl.BlockSpec(memory_space=pltpu.VMEM)
    return pl.pallas_call(
        kernel,
        out_shape=out_shape,
        in_specs=[whole] * len(operands),
        out_specs=jax.tree.map(lambda _: whole, out_shape),
        compiler_params=pltpu.CompilerParams(vmem_limit_bytes=VMEM_LIMIT),
        name=name,
    )(*operands)


def extend_kernel(tokens_hbm, ids_hbm, weights_hbm, out_ref, tokens_ref, ids_ref, weights_ref, sems):
    pairs = ((ids_hbm, ids_ref), (weights_hbm, weights_ref), (tokens_hbm, tokens_ref))
    copies = [pltpu.make_async_copy(a, b, sems.at[i]) for i, (a, b) in enumerate(pairs)]
    for copy in copies:
        copy.start()
    rows, width = tokens_ref.shape
    half = (out_ref.shape[1] - width) // 2
    lane = lax.broadcasted_iota(jnp.int32, (rows, half * 2), 1)
    dense = jnp.zeros((rows, half * 2), jnp.float32)
    for copy in copies:
        copy.wait()
    for k in range(ids_ref.shape[1]):
        mine = lax.rem(lane, half) == ids_ref[:, k:k + 1]
        dense = dense + jnp.where(mine, weights_ref[:, k:k + 1], 0.0)
    high = dense.astype(jnp.bfloat16).astype(jnp.float32)
    out_ref[:, :width] = tokens_ref[...]
    out_ref[:, width:] = jnp.where(lane < half, high, dense - high).astype(jnp.bfloat16)


def extend(tokens, ids, weights, half):
    rows, width = tokens.shape
    return pl.pallas_call(
        extend_kernel,
        out_shape=jax.ShapeDtypeStruct((rows, width + 2 * half), tokens.dtype),
        in_specs=[pl.BlockSpec(memory_space=pl.ANY)] * 3,
        out_specs=pl.BlockSpec(memory_space=pltpu.VMEM),
        scratch_shapes=[pltpu.VMEM(v.shape, v.dtype) for v in (tokens, ids, weights)]
        + [pltpu.SemaphoreType.DMA((3,))],
        compiler_params=pltpu.CompilerParams(vmem_limit_bytes=VMEM_LIMIT),
        name="extend",
    )(*(pltpu.with_memory_space_constraint(v, pltpu.HBM) for v in (tokens, ids, weights)))


def join_kernel(*refs):
    pieces, out_ref = refs[:-1], refs[-1]
    values = [p[...].astype(jnp.float32) for p in pieces]
    out_ref[...] = jnp.concatenate(values, axis=0).astype(out_ref.dtype)


def join(pieces):
    rows, width = pieces[0].shape
    out = jax.ShapeDtypeStruct((rows * len(pieces), width), pieces[0].dtype)
    return vmem_call(join_kernel, out, "join", *pieces)


def halves_kernel(left_ref, right_ref, left_out, right_out):
    half = left_out.shape[1]
    left_out[...] = left_ref[:, :half]
    right_out[...] = right_ref[:, half:]


def halves(left, right):
    rows, width = left.shape
    half = width // 256 * 128
    out = (
        jax.ShapeDtypeStruct((rows, half), left.dtype),
        jax.ShapeDtypeStruct((rows, width - half), left.dtype),
    )
    return vmem_call(halves_kernel, out, "halves", left, right)


def gather_rows(block, w_up):
    lanes, groups, sects = (lax.axis_size(a) for a in ("dev", "grp", "sect"))
    arrived = [swap(block, "dev", m) for m in range(1, lanes)]
    w_up, token = fetch(w_up, block)
    arrived, token = lax.optimization_barrier((arrived, token))
    line = join([block] + arrived)
    if groups == 4:
        by_x, by_y = swap(line, "grp", 1), swap(line, "grp", 2)
        from_x, from_y = halves(by_x, by_y)
        corner = [swap(from_x, "grp", 2), swap(from_y, "grp", 1)]
        entries = [[line], [by_x], [by_y], corner]
    else:
        entries = [[line]]
        for bit in bits_of(groups):
            entries = entries + [[swap(p, "grp", bit) for p in e] for e in entries]
    for bit in bits_of(sects):
        entries = entries + [[swap(p, "sect", bit) for p in e] for e in entries]
    return entries, w_up, token


def down_product(order, line, hidden_ref, down_ref, keep_ref, send_ref, sems, copy_of):
    blocks = sems.shape[0]
    block = keep_ref.shape[1] // blocks
    experts, depth, _ = down_ref.shape
    groups = len(order)

    @pl.loop(0, blocks)
    def _(step):
        columns = pl.ds(pl.multiple_of(step * block, block), block)
        copy_of(step).wait()
        weight = down_ref[:, :, columns].reshape(experts * depth, block)
        total = jnp.dot(hidden_ref[...], weight, preferred_element_type=jnp.float32)
        total = total.astype(jnp.bfloat16)
        for place, entry in enumerate(order):
            rows = pl.ds(place * line, line)
            keep_ref[rows, columns] = total[entry * line:(entry + 1) * line]
            low = (groups + entry) * line
            send_ref[rows, columns] = total[low:low + line]


def down_copy(start, down_hbm, down_ref, sems):
    block = down_ref.shape[2] // sems.shape[0]

    def copy(step):
        at = pl.multiple_of(step * block, block)
        return pltpu.make_async_copy(
            down_hbm.at[:, :, pl.ds(start + at, block)],
            down_ref.at[:, :, pl.ds(at, block)],
            sems.at[step],
        )

    return copy


def up_kernel(layout, width, order, start, token_ref, *refs):
    pieces = refs[: sum(layout)]
    (upw_ref, gate_hbm, down_hbm, hidden_ref, keep_ref, send_ref,
     rows_ref, up_ref, gate_ref, gate_sems, down_ref, sems) = refs[sum(layout):]
    experts, _, hidden = upw_ref.shape
    place = lax.axis_index("sect") * lax.axis_size("grp") + lax.axis_index("grp")
    first = place * experts
    line = pieces[0].shape[0]
    block = min(256, hidden)
    gate_copies = weight_copies(gate_hbm, gate_ref, gate_sems)
    for gate_copy in gate_copies:
        gate_copy.start()
    copy = down_copy(start, down_hbm, down_ref, sems)
    for step in range(sems.shape[0]):
        copy(step).start()

    at = 0
    for entry, count in enumerate(layout):
        left = 0
        for piece in pieces[at:at + count]:
            rows_ref[pl.ds(entry * line, line), pl.ds(left, piece.shape[1])] = piece[...]
            left += piece.shape[1]
        at += count

    for e in range(experts):

        @pl.loop(0, hidden // block)
        def _(step):
            span = pl.ds(pl.multiple_of(step * block, block), block)
            up_ref[e, :, span] = jnp.dot(
                rows_ref[:, :width], upw_ref[e, :, span], preferred_element_type=jnp.float32
            )

    extra = rows_ref[:, width:].astype(jnp.float32)
    lane = lax.broadcasted_iota(jnp.int32, extra.shape, 1)
    parts = gate_sems.shape[1]
    for e in range(experts):
        mine = lax.rem(lane, extra.shape[1] // 2) == first + e
        scale = jnp.sum(jnp.where(mine, extra, 0.0), axis=1, keepdims=True)
        for gate_copy in gate_copies[e * parts:(e + 1) * parts]:
            gate_copy.wait()

        @pl.loop(0, hidden // block)
        def _(step):
            span = pl.ds(pl.multiple_of(step * block, block), block)
            gate = jnp.dot(
                rows_ref[:, :width], gate_ref[e, :, span], preferred_element_type=jnp.float32
            )
            value = gate / (1.0 + jnp.exp(-gate)) * up_ref[e, :, span] * scale
            out = pl.ds(pl.multiple_of(e * hidden + step * block, block), block)
            hidden_ref[:, out] = value.astype(jnp.bfloat16)

    down_product(order, line, hidden_ref, down_ref, keep_ref, send_ref, sems, copy)


def fetch_kernel(after_ref, source_ref, target_ref, token_ref, sems):
    copies = weight_copies(source_ref, target_ref, sems)
    for copy in copies:
        copy.start()
    token_ref[...] = jnp.zeros_like(token_ref)
    for copy in copies:
        copy.wait()


def weight_copies(source_ref, target_ref, sems):
    experts, parts = sems.shape
    depth = source_ref.shape[1] // parts
    return [
        pltpu.make_async_copy(
            source_ref.at[e, pl.ds(p * depth, depth)],
            target_ref.at[e, pl.ds(p * depth, depth)],
            sems.at[e, p],
        )
        for e in range(experts)
        for p in range(parts)
    ]


def fetch(weight, after):
    in_hbm = pl.BlockSpec(memory_space=pl.ANY)
    in_vmem = pl.BlockSpec(memory_space=pltpu.VMEM)
    return pl.pallas_call(
        fetch_kernel,
        out_shape=(
            pltpu.VMEM(weight.shape, weight.dtype),
            jax.ShapeDtypeStruct((8, 128), jnp.float32),
        ),
        in_specs=[in_hbm, in_hbm],
        out_specs=(in_vmem, in_vmem),
        scratch_shapes=[pltpu.SemaphoreType.DMA((weight.shape[0], 4))],
        compiler_params=pltpu.CompilerParams(vmem_limit_bytes=VMEM_LIMIT),
        cost_estimate=pl.CostEstimate(
            flops=0, bytes_accessed=2 * weight.size, transcendentals=0
        ),
        name="fetch",
    )(after, pltpu.with_memory_space_constraint(weight, pltpu.HBM))


def down_scratch(w_down, columns):
    experts, depth, _ = w_down.shape
    block = 512 if columns % 512 == 0 else 128
    return [
        pltpu.VMEM((experts, depth, columns), w_down.dtype),
        pltpu.SemaphoreType.DMA((columns // block,)),
    ]


def up_call(entries, w_gate, w_up, w_down, token, order, start, columns):
    layout = [len(e) for e in entries]
    flat = [p for e in entries for p in e]
    experts, width, hidden = w_up.shape
    line = flat[0].shape[0]
    full = sum(p.shape[1] for p in entries[0])
    rows = line * len(entries)
    whole = pl.BlockSpec(memory_space=pltpu.VMEM)
    anywhere = pl.BlockSpec(memory_space=pl.ANY)
    out = jax.ShapeDtypeStruct((rows // 2, columns), jnp.bfloat16)
    return pl.pallas_call(
        functools.partial(up_kernel, layout, width, order, start),
        out_shape=(jax.ShapeDtypeStruct((rows, experts * hidden), jnp.bfloat16), out, out),
        in_specs=[anywhere] + [whole] * (len(flat) + 1) + [anywhere] * 2,
        out_specs=(whole,) * 3,
        scratch_shapes=[
            pltpu.VMEM((rows, full), jnp.bfloat16),
            pltpu.VMEM((experts, rows, hidden), jnp.float32),
            pltpu.VMEM(w_gate.shape, w_gate.dtype),
            pltpu.SemaphoreType.DMA((experts, 4)),
        ]
        + down_scratch(w_down, columns),
        compiler_params=pltpu.CompilerParams(vmem_limit_bytes=VMEM_LIMIT),
        cost_estimate=pl.CostEstimate(
            flops=4 * rows * experts * width * hidden + 2 * rows * experts * hidden * columns,
            bytes_accessed=2 * experts * hidden * columns,
            transcendentals=rows * experts * hidden,
        ),
        name="gate_up",
    )(
        token,
        *flat,
        pltpu.with_memory_space_constraint(w_up, pltpu.VMEM),
        pltpu.with_memory_space_constraint(w_gate, pltpu.HBM),
        pltpu.with_memory_space_constraint(w_down, pltpu.HBM),
    )


def down_kernel(order, line, start, hidden_ref, down_hbm, keep_ref, send_ref, down_ref, sems):
    copy = down_copy(start, down_hbm, down_ref, sems)
    for step in range(sems.shape[0]):
        copy(step).start()
    down_product(order, line, hidden_ref, down_ref, keep_ref, send_ref, sems, copy)


def down_call(order, line, hidden, w_down, start, columns):
    rows = line * len(order)
    out = jax.ShapeDtypeStruct((rows, columns), jnp.bfloat16)
    whole = pl.BlockSpec(memory_space=pltpu.VMEM)
    return pl.pallas_call(
        functools.partial(down_kernel, order, line, start),
        out_shape=(out, out),
        in_specs=[whole, pl.BlockSpec(memory_space=pl.ANY)],
        out_specs=(whole, whole),
        scratch_shapes=down_scratch(w_down, columns),
        compiler_params=pltpu.CompilerParams(vmem_limit_bytes=VMEM_LIMIT),
        cost_estimate=pl.CostEstimate(
            flops=2 * hidden.size * columns,
            bytes_accessed=2 * hidden.shape[1] * columns,
            transcendentals=0,
        ),
        name="down",
    )(hidden, pltpu.with_memory_space_constraint(w_down, pltpu.HBM))


def add(*values):
    total = values[0].astype(jnp.float32)
    for value in values[1:]:
        total = total + value.astype(jnp.float32)
    return total.astype(jnp.bfloat16)


def body(tokens, expert_ids, gate_weights, w_gate, w_up, w_down):
    sects, groups, lanes = (lax.axis_size(a) for a in AXES)
    row_count, width = tokens.shape
    experts = w_gate.shape[0]
    expert_count = sects * groups * experts

    half = -(-expert_count // 64) * 64
    block = extend(tokens, expert_ids, gate_weights, half)
    entries, w_up, token = gather_rows(block, w_up)

    line = lanes * row_count
    results = []
    chunk = width // CHUNKS
    hidden = None
    for c in range(CHUNKS):
        bits = bits_of(groups)
        bits = bits if c % 2 else bits[::-1]
        order = [0]
        for bit in bits:
            order = order + [o | bit for o in order]
        if c == 0:
            hidden, keep, send = up_call(
                entries, w_gate, w_up, w_down, token, order, 0, chunk
            )
        else:
            keep, send = down_call(order, line, hidden, w_down, c * chunk, chunk)
        value = add(keep, swap(send, "sect", 1))
        for bit in bits[::-1]:
            middle = value.shape[0] // 2
            arrived = swap(value[middle:], "grp", bit)
            value = add(value[:middle], arrived)
        pieces = [value[:row_count]]
        for m in range(1, lanes):
            pieces.append(swap(value[m * row_count:(m + 1) * row_count], "dev", m))
        results.append(add(*pieces))
    return jnp.concatenate(results, axis=1)


def solution(mesh):
    in_specs = (
        P(AXES, None),
        P(AXES, None),
        P(AXES, None),
        P(("sect", "grp"), None, "dev"),
        P(("sect", "grp"), None, "dev"),
        P(("sect", "grp"), "dev", None),
    )
    return jax.shard_map(
        body, mesh=mesh, in_specs=in_specs, out_specs=P(AXES, None), check_vma=False
    )
```

```python
import functools

import jax
import jax.numpy as jnp
from jax import lax
from jax.experimental import pallas as pl
from jax.experimental.pallas import tpu as pltpu
from jax.sharding import PartitionSpec as P

AXES = ("sect", "grp", "dev")
CHUNKS = 2
VMEM_LIMIT = 30 * 2**20


def swap(value, axis, mask):
    return lax.ppermute(value, axis, [(i, i ^ mask) for i in range(lax.axis_size(axis))])


def bits_of(size):
    return [1 << b for b in range(size.bit_length() - 1)]


def vmem_call(kernel, out_shape, name, *operands):
    whole = pl.BlockSpec(memory_space=pltpu.VMEM)
    return pl.pallas_call(
        kernel,
        out_shape=out_shape,
        in_specs=[whole] * len(operands),
        out_specs=jax.tree.map(lambda _: whole, out_shape),
        compiler_params=pltpu.CompilerParams(vmem_limit_bytes=VMEM_LIMIT),
        name=name,
    )(*operands)


def extend_kernel(tokens_hbm, ids_hbm, weights_hbm, out_ref, tokens_ref, ids_ref, weights_ref, sems):
    pairs = ((ids_hbm, ids_ref), (weights_hbm, weights_ref), (tokens_hbm, tokens_ref))
    copies = [pltpu.make_async_copy(a, b, sems.at[i]) for i, (a, b) in enumerate(pairs)]
    for copy in copies:
        copy.start()
    rows, width = tokens_ref.shape
    half = (out_ref.shape[2] - width) // 2
    lane = lax.broadcasted_iota(jnp.int32, (rows, half * 2), 1)
    dense = jnp.zeros((rows, half * 2), jnp.float32)
    for copy in copies:
        copy.wait()
    for k in range(ids_ref.shape[1]):
        mine = lax.rem(lane, half) == ids_ref[:, k:k + 1]
        dense = dense + jnp.where(mine, weights_ref[:, k:k + 1], 0.0)
    high = dense.astype(jnp.bfloat16).astype(jnp.float32)
    extra = jnp.where(lane < half, high, dense - high).astype(jnp.bfloat16)
    for copy in range(out_ref.shape[0]):
        out_ref[copy, :, :width] = tokens_ref[...]
        out_ref[copy, :, width:] = extra


def extend(tokens, ids, weights, half, copies):
    rows, width = tokens.shape
    return pl.pallas_call(
        extend_kernel,
        out_shape=jax.ShapeDtypeStruct((copies, rows, width + 2 * half), tokens.dtype),
        in_specs=[pl.BlockSpec(memory_space=pl.ANY)] * 3,
        out_specs=pl.BlockSpec(memory_space=pltpu.VMEM),
        scratch_shapes=[pltpu.VMEM(v.shape, v.dtype) for v in (tokens, ids, weights)]
        + [pltpu.SemaphoreType.DMA((3,))],
        compiler_params=pltpu.CompilerParams(vmem_limit_bytes=VMEM_LIMIT),
        name="extend",
    )(*(pltpu.with_memory_space_constraint(v, pltpu.HBM) for v in (tokens, ids, weights)))


def join_kernel(pieces_ref, out_ref):
    values = [pieces_ref[i].astype(jnp.float32) for i in range(pieces_ref.shape[0])]
    line = jnp.concatenate(values, axis=0).astype(out_ref.dtype)
    for copy in range(out_ref.shape[0]):
        out_ref[copy] = line


def join(pieces, copies):
    count, rows, width = pieces.shape
    out = jax.ShapeDtypeStruct((copies, count * rows, width), pieces.dtype)
    return vmem_call(join_kernel, out, "join", pieces)


def everywhere(value, axis):
    return lax.all_to_all(value, axis, split_axis=0, concat_axis=0, tiled=True)


def gather_rows(block, w_up):
    groups, sects = lax.axis_size("grp"), lax.axis_size("sect")
    arrived = everywhere(block, "dev")
    w_up, token = fetch(w_up, block)
    arrived, token = lax.optimization_barrier((arrived, token))
    lines = everywhere(join(arrived, groups), "grp")
    entries = [lines]
    for bit in bits_of(sects):
        entries = entries + [swap(e, "sect", bit) for e in entries]
    return entries, w_up, token


def down_product(hidden_ref, down_ref, keep_ref, send_ref, sems, copy_of):
    blocks = sems.shape[0]
    block = keep_ref.shape[1] // blocks
    experts, depth, _ = down_ref.shape
    middle = keep_ref.shape[0]

    @pl.loop(0, blocks)
    def _(step):
        columns = pl.ds(pl.multiple_of(step * block, block), block)
        copy_of(step).wait()
        weight = down_ref[:, :, columns].reshape(experts * depth, block)
        total = jnp.dot(hidden_ref[...], weight, preferred_element_type=jnp.float32)
        total = total.astype(jnp.bfloat16)
        keep_ref[:, columns] = total[:middle]
        send_ref[:, columns] = total[middle:]


def down_copy(start, down_hbm, down_ref, sems):
    block = down_ref.shape[2] // sems.shape[0]

    def copy(step):
        at = pl.multiple_of(step * block, block)
        return pltpu.make_async_copy(
            down_hbm.at[:, :, pl.ds(start + at, block)],
            down_ref.at[:, :, pl.ds(at, block)],
            sems.at[step],
        )

    return copy


def up_kernel(entry_count, width, start, token_ref, *refs):
    entries = refs[:entry_count]
    (upw_ref, gate_hbm, down_hbm, hidden_ref, keep_ref, send_ref,
     rows_ref, up_ref, gate_ref, gate_sems, down_ref, sems) = refs[entry_count:]
    experts, _, hidden = upw_ref.shape
    place = lax.axis_index("sect") * lax.axis_size("grp") + lax.axis_index("grp")
    first = place * experts
    block = min(256, hidden)
    gate_copies = weight_copies(gate_hbm, gate_ref, gate_sems)
    for gate_copy in gate_copies:
        gate_copy.start()
    copy = down_copy(start, down_hbm, down_ref, sems)

    at = 0
    for entry in entries:
        for i in range(entry.shape[0]):
            rows_ref[pl.ds(at, entry.shape[1])] = entry[i]
            at += entry.shape[1]

    for e in range(experts):

        @pl.loop(0, hidden // block)
        def _(step):
            span = pl.ds(pl.multiple_of(step * block, block), block)
            up_ref[e, :, span] = jnp.dot(
                rows_ref[:, :width], upw_ref[e, :, span], preferred_element_type=jnp.float32
            )

    extra = rows_ref[:, width:].astype(jnp.float32)
    lane = lax.broadcasted_iota(jnp.int32, extra.shape, 1)
    parts = gate_sems.shape[1]
    for e in range(experts):
        mine = lax.rem(lane, extra.shape[1] // 2) == first + e
        scale = jnp.sum(jnp.where(mine, extra, 0.0), axis=1, keepdims=True)
        for gate_copy in gate_copies[e * parts:(e + 1) * parts]:
            gate_copy.wait()
        if e == 0:
            for step in range(sems.shape[0]):
                copy(step).start()

        @pl.loop(0, hidden // block)
        def _(step):
            span = pl.ds(pl.multiple_of(step * block, block), block)
            gate = jnp.dot(
                rows_ref[:, :width], gate_ref[e, :, span], preferred_element_type=jnp.float32
            )
            value = gate / (1.0 + jnp.exp(-gate)) * up_ref[e, :, span] * scale
            out = pl.ds(pl.multiple_of(e * hidden + step * block, block), block)
            hidden_ref[:, out] = value.astype(jnp.bfloat16)

    down_product(hidden_ref, down_ref, keep_ref, send_ref, sems, copy)


def fetch_kernel(after_ref, source_ref, target_ref, token_ref, sems):
    copies = weight_copies(source_ref, target_ref, sems)
    for copy in copies:
        copy.start()
    token_ref[...] = jnp.zeros_like(token_ref)
    for copy in copies:
        copy.wait()


def weight_copies(source_ref, target_ref, sems):
    experts, parts = sems.shape
    depth = source_ref.shape[1] // parts
    return [
        pltpu.make_async_copy(
            source_ref.at[e, pl.ds(p * depth, depth)],
            target_ref.at[e, pl.ds(p * depth, depth)],
            sems.at[e, p],
        )
        for e in range(experts)
        for p in range(parts)
    ]


def fetch(weight, after):
    in_hbm = pl.BlockSpec(memory_space=pl.ANY)
    in_vmem = pl.BlockSpec(memory_space=pltpu.VMEM)
    return pl.pallas_call(
        fetch_kernel,
        out_shape=(
            pltpu.VMEM(weight.shape, weight.dtype),
            jax.ShapeDtypeStruct((8, 128), jnp.float32),
        ),
        in_specs=[in_hbm, in_hbm],
        out_specs=(in_vmem, in_vmem),
        scratch_shapes=[pltpu.SemaphoreType.DMA((weight.shape[0], 4))],
        compiler_params=pltpu.CompilerParams(vmem_limit_bytes=VMEM_LIMIT),
        cost_estimate=pl.CostEstimate(
            flops=0, bytes_accessed=2 * weight.size, transcendentals=0
        ),
        name="fetch",
    )(after, pltpu.with_memory_space_constraint(weight, pltpu.HBM))


def down_scratch(w_down, columns):
    experts, depth, _ = w_down.shape
    block = 512 if columns % 512 == 0 else 128
    return [
        pltpu.VMEM((experts, depth, columns), w_down.dtype),
        pltpu.SemaphoreType.DMA((columns // block,)),
    ]


def up_call(entries, w_gate, w_up, w_down, token, start, columns):
    experts, width, hidden = w_up.shape
    groups, line, full = entries[0].shape
    rows = groups * line * len(entries)
    whole = pl.BlockSpec(memory_space=pltpu.VMEM)
    anywhere = pl.BlockSpec(memory_space=pl.ANY)
    out = jax.ShapeDtypeStruct((rows // 2, columns), jnp.bfloat16)
    return pl.pallas_call(
        functools.partial(up_kernel, len(entries), width, start),
        out_shape=(jax.ShapeDtypeStruct((rows, experts * hidden), jnp.bfloat16), out, out),
        in_specs=[anywhere] + [whole] * (len(entries) + 1) + [anywhere] * 2,
        out_specs=(whole,) * 3,
        scratch_shapes=[
            pltpu.VMEM((rows, full), jnp.bfloat16),
            pltpu.VMEM((experts, rows, hidden), jnp.float32),
            pltpu.VMEM(w_gate.shape, w_gate.dtype),
            pltpu.SemaphoreType.DMA((experts, 4)),
        ]
        + down_scratch(w_down, columns),
        compiler_params=pltpu.CompilerParams(vmem_limit_bytes=VMEM_LIMIT),
        cost_estimate=pl.CostEstimate(
            flops=4 * rows * experts * width * hidden + 2 * rows * experts * hidden * columns,
            bytes_accessed=2 * experts * hidden * columns,
            transcendentals=rows * experts * hidden,
        ),
        name="gate_up",
    )(
        token,
        *entries,
        pltpu.with_memory_space_constraint(w_up, pltpu.VMEM),
        pltpu.with_memory_space_constraint(w_gate, pltpu.HBM),
        pltpu.with_memory_space_constraint(w_down, pltpu.HBM),
    )


def down_kernel(start, hidden_ref, down_hbm, keep_ref, send_ref, down_ref, sems):
    copy = down_copy(start, down_hbm, down_ref, sems)
    for step in range(sems.shape[0]):
        copy(step).start()
    down_product(hidden_ref, down_ref, keep_ref, send_ref, sems, copy)


def down_call(hidden, w_down, start, columns):
    rows = hidden.shape[0] // 2
    out = jax.ShapeDtypeStruct((rows, columns), jnp.bfloat16)
    whole = pl.BlockSpec(memory_space=pltpu.VMEM)
    return pl.pallas_call(
        functools.partial(down_kernel, start),
        out_shape=(out, out),
        in_specs=[whole, pl.BlockSpec(memory_space=pl.ANY)],
        out_specs=(whole, whole),
        scratch_shapes=down_scratch(w_down, columns),
        compiler_params=pltpu.CompilerParams(vmem_limit_bytes=VMEM_LIMIT),
        cost_estimate=pl.CostEstimate(
            flops=2 * hidden.size * columns,
            bytes_accessed=2 * hidden.shape[1] * columns,
            transcendentals=0,
        ),
        name="down",
    )(hidden, pltpu.with_memory_space_constraint(w_down, pltpu.HBM))


def add(*values):
    total = values[0].astype(jnp.float32)
    for value in values[1:]:
        total = total + value.astype(jnp.float32)
    return total.astype(jnp.bfloat16)


def body(tokens, expert_ids, gate_weights, w_gate, w_up, w_down):
    sects, groups, lanes = (lax.axis_size(a) for a in AXES)
    row_count, width = tokens.shape
    experts = w_gate.shape[0]
    expert_count = sects * groups * experts

    half = -(-expert_count // 64) * 64
    block = extend(tokens, expert_ids, gate_weights, half, lanes)
    entries, w_up, token = gather_rows(block, w_up)

    chunk = width // CHUNKS
    sums = []
    for c in range(CHUNKS):
        if c == 0:
            hidden, keep, send = up_call(entries, w_gate, w_up, w_down, token, 0, chunk)
        else:
            keep, send = down_call(hidden, w_down, c * chunk, chunk)
        sums.append(add(keep, swap(send, "sect", 1)))
    line = lanes * row_count
    arrived = everywhere(jnp.concatenate(sums, axis=1), "grp").reshape(groups, line, width)
    value = add(*(arrived[g] for g in range(groups)))
    arrived = everywhere(value.reshape(lanes, row_count, width), "dev")
    return add(*(arrived[d] for d in range(lanes)))


def solution(mesh):
    in_specs = (
        P(AXES, None),
        P(AXES, None),
        P(AXES, None),
        P(("sect", "grp"), None, "dev"),
        P(("sect", "grp"), None, "dev"),
        P(("sect", "grp"), "dev", None),
    )
    return jax.shard_map(
        body, mesh=mesh, in_specs=in_specs, out_specs=P(AXES, None), check_vma=False
    )
```

```python
import functools

import jax
import jax.numpy as jnp
from jax import lax
from jax.experimental import pallas as pl
from jax.experimental.pallas import tpu as pltpu
from jax.sharding import PartitionSpec as P

AXES = ("sect", "grp", "dev")
CHUNKS = 2
VMEM_LIMIT = 30 * 2**20


def swap(value, axis, mask):
    return lax.ppermute(value, axis, [(i, i ^ mask) for i in range(lax.axis_size(axis))])


def bits_of(size):
    return [1 << b for b in range(size.bit_length() - 1)]


def vmem_call(kernel, out_shape, name, *operands):
    whole = pl.BlockSpec(memory_space=pltpu.VMEM)
    return pl.pallas_call(
        kernel,
        out_shape=out_shape,
        in_specs=[whole] * len(operands),
        out_specs=jax.tree.map(lambda _: whole, out_shape),
        compiler_params=pltpu.CompilerParams(vmem_limit_bytes=VMEM_LIMIT),
        name=name,
    )(*operands)


def extend_kernel(tokens_hbm, ids_hbm, weights_hbm, out_ref, tokens_ref, ids_ref, weights_ref, sems):
    pairs = ((ids_hbm, ids_ref), (weights_hbm, weights_ref), (tokens_hbm, tokens_ref))
    copies = [pltpu.make_async_copy(a, b, sems.at[i]) for i, (a, b) in enumerate(pairs)]
    for copy in copies:
        copy.start()
    rows, width = tokens_ref.shape
    half = (out_ref.shape[1] - width) // 2
    lane = lax.broadcasted_iota(jnp.int32, (rows, half * 2), 1)
    dense = jnp.zeros((rows, half * 2), jnp.float32)
    for copy in copies:
        copy.wait()
    for k in range(ids_ref.shape[1]):
        mine = lax.rem(lane, half) == ids_ref[:, k:k + 1]
        dense = dense + jnp.where(mine, weights_ref[:, k:k + 1], 0.0)
    high = dense.astype(jnp.bfloat16).astype(jnp.float32)
    out_ref[:, :width] = tokens_ref[...]
    out_ref[:, width:] = jnp.where(lane < half, high, dense - high).astype(jnp.bfloat16)


def extend(tokens, ids, weights, half):
    rows, width = tokens.shape
    return pl.pallas_call(
        extend_kernel,
        out_shape=jax.ShapeDtypeStruct((rows, width + 2 * half), tokens.dtype),
        in_specs=[pl.BlockSpec(memory_space=pl.ANY)] * 3,
        out_specs=pl.BlockSpec(memory_space=pltpu.VMEM),
        scratch_shapes=[pltpu.VMEM(v.shape, v.dtype) for v in (tokens, ids, weights)]
        + [pltpu.SemaphoreType.DMA((3,))],
        compiler_params=pltpu.CompilerParams(vmem_limit_bytes=VMEM_LIMIT),
        name="extend",
    )(*(pltpu.with_memory_space_constraint(v, pltpu.HBM) for v in (tokens, ids, weights)))


def stack_kernel(*refs):
    pieces, out_ref = refs[:-1], refs[-1]
    values = [p[...].astype(jnp.float32) for p in pieces]
    out_ref[...] = jnp.concatenate(values, axis=0).astype(out_ref.dtype)


def stack(*pieces):
    rows = sum(p.shape[0] for p in pieces)
    out = jax.ShapeDtypeStruct((rows, pieces[0].shape[1]), pieces[0].dtype)
    return vmem_call(stack_kernel, out, "stack", *pieces)


def halves_kernel(left_ref, right_ref, left_out, right_out):
    half = left_out.shape[1]
    left_out[...] = left_ref[:, :half]
    right_out[...] = right_ref[:, half:]


def halves(left, right):
    rows, width = left.shape
    half = width // 256 * 128
    out = (
        jax.ShapeDtypeStruct((rows, half), left.dtype),
        jax.ShapeDtypeStruct((rows, width - half), left.dtype),
    )
    return vmem_call(halves_kernel, out, "halves", left, right)


def gather_kernel(by_x_ref, by_y_ref, left_ref, right_ref, out_ref):
    line, half = left_ref.shape
    out_ref[:line] = by_x_ref[...]
    out_ref[line:2 * line] = by_y_ref[...]
    out_ref[2 * line:, :half] = left_ref[...]
    out_ref[2 * line:, half:] = right_ref[...]


def gather_rows(block, w_up):
    lanes, groups, sects = (lax.axis_size(a) for a in ("dev", "grp", "sect"))
    line, weights, token = block, [], block
    experts = list(range(w_up.shape[0]))
    for bit in bits_of(lanes)[::-1]:
        arrived = swap(line, "dev", bit)
        if experts:
            weight, token = fetch(w_up, experts.pop(0), token)
            weights.append(weight)
            arrived, token = lax.optimization_barrier((arrived, token))
        line = stack(line, arrived)
    while experts:
        weight, token = fetch(w_up, experts.pop(0), token)
        weights.append(weight)
    if groups == 4:
        by_x, by_y, mine = swap(line, "grp", 1), swap(line, "grp", 2), swap(line, "sect", 1)
        by_x, by_y, mine = lax.optimization_barrier((by_x, by_y, mine))
        from_x, from_y = halves(by_x, by_y)
        left, right = swap(from_x, "grp", 2), swap(from_y, "grp", 1)
        out = jax.ShapeDtypeStruct((3 * line.shape[0], line.shape[1]), line.dtype)
        rest = vmem_call(gather_kernel, out, "gather", by_x, by_y, left, right)
        entries = [line, rest, mine, swap(rest, "sect", 1)]
    else:
        entries = [line]
        for bit in bits_of(groups):
            entries = entries + [swap(e, "grp", bit) for e in entries]
        for bit in bits_of(sects):
            entries = entries + [swap(e, "sect", bit) for e in entries]
    return entries, weights, token


def down_product(order, hidden_ref, down_ref, keep_ref, send_ref, sems, copy_of):
    blocks = sems.shape[0]
    block = keep_ref.shape[1] // blocks
    experts, depth, _ = down_ref.shape
    groups = len(order)
    line = keep_ref.shape[0] // groups

    @pl.loop(0, blocks)
    def _(step):
        columns = pl.ds(pl.multiple_of(step * block, block), block)
        copy_of(step).wait()
        weight = down_ref[:, :, columns].reshape(experts * depth, block)
        total = jnp.dot(hidden_ref[...], weight, preferred_element_type=jnp.float32)
        total = total.astype(jnp.bfloat16)
        for place, entry in enumerate(order):
            rows = pl.ds(place * line, line)
            keep_ref[rows, columns] = total[entry * line:(entry + 1) * line]
            low = (groups + entry) * line
            send_ref[rows, columns] = total[low:low + line]


def down_copy(start, down_hbm, down_ref, sems):
    block = down_ref.shape[2] // sems.shape[0]

    def copy(step):
        at = pl.multiple_of(step * block, block)
        return pltpu.make_async_copy(
            down_hbm.at[:, :, pl.ds(start + at, block)],
            down_ref.at[:, :, pl.ds(at, block)],
            sems.at[step],
        )

    return copy


def up_kernel(counts, width, order, start, token_ref, *refs):
    pieces, up_refs = refs[:counts[0]], refs[counts[0]:sum(counts)]
    (gate_hbm, down_hbm, hidden_ref, keep_ref, send_ref,
     rows_ref, up_ref, gate_ref, gate_sems, down_ref, sems) = refs[sum(counts):]
    experts, _, hidden = gate_ref.shape
    place = lax.axis_index("sect") * lax.axis_size("grp") + lax.axis_index("grp")
    first = place * experts
    block = min(256, hidden)
    gate_copies = weight_copies(gate_hbm, gate_ref, gate_sems)
    for gate_copy in gate_copies:
        gate_copy.start()
    copy = down_copy(start, down_hbm, down_ref, sems)

    at = 0
    for piece in pieces:
        rows_ref[pl.ds(at, piece.shape[0])] = piece[...]
        at += piece.shape[0]

    for e in range(experts):

        @pl.loop(0, hidden // block)
        def _(step):
            span = pl.ds(pl.multiple_of(step * block, block), block)
            up_ref[e, :, span] = jnp.dot(
                rows_ref[:, :width], up_refs[e][0, :, span], preferred_element_type=jnp.float32
            )

    extra = rows_ref[:, width:].astype(jnp.float32)
    lane = lax.broadcasted_iota(jnp.int32, extra.shape, 1)
    parts = gate_sems.shape[1]
    for e in range(experts):
        mine = lax.rem(lane, extra.shape[1] // 2) == first + e
        scale = jnp.sum(jnp.where(mine, extra, 0.0), axis=1, keepdims=True)
        for gate_copy in gate_copies[e * parts:(e + 1) * parts]:
            gate_copy.wait()
        if e == 0:
            for step in range(sems.shape[0]):
                copy(step).start()

        @pl.loop(0, hidden // block)
        def _(step):
            span = pl.ds(pl.multiple_of(step * block, block), block)
            gate = jnp.dot(
                rows_ref[:, :width], gate_ref[e, :, span], preferred_element_type=jnp.float32
            )
            value = gate / (1.0 + jnp.exp(-gate)) * up_ref[e, :, span] * scale
            out = pl.ds(pl.multiple_of(e * hidden + step * block, block), block)
            hidden_ref[:, out] = value.astype(jnp.bfloat16)

    down_product(order, hidden_ref, down_ref, keep_ref, send_ref, sems, copy)


def fetch_kernel(expert, after_ref, source_ref, target_ref, token_ref, sems):
    copies = weight_copies(source_ref.at[pl.ds(expert, 1)], target_ref, sems)
    for copy in copies:
        copy.start()
    token_ref[...] = jnp.zeros_like(token_ref)
    for copy in copies:
        copy.wait()


def weight_copies(source_ref, target_ref, sems):
    experts, parts = sems.shape
    depth = source_ref.shape[1] // parts
    return [
        pltpu.make_async_copy(
            source_ref.at[e, pl.ds(p * depth, depth)],
            target_ref.at[e, pl.ds(p * depth, depth)],
            sems.at[e, p],
        )
        for e in range(experts)
        for p in range(parts)
    ]


def fetch(weight, expert, after):
    in_hbm = pl.BlockSpec(memory_space=pl.ANY)
    in_vmem = pl.BlockSpec(memory_space=pltpu.VMEM)
    return pl.pallas_call(
        functools.partial(fetch_kernel, expert),
        out_shape=(
            pltpu.VMEM((1, *weight.shape[1:]), weight.dtype),
            jax.ShapeDtypeStruct((8, 128), jnp.float32),
        ),
        in_specs=[in_hbm, in_hbm],
        out_specs=(in_vmem, in_vmem),
        scratch_shapes=[pltpu.SemaphoreType.DMA((1, 8))],
        compiler_params=pltpu.CompilerParams(vmem_limit_bytes=VMEM_LIMIT),
        cost_estimate=pl.CostEstimate(
            flops=0, bytes_accessed=2 * weight.size // weight.shape[0], transcendentals=0
        ),
        name="fetch",
    )(after, pltpu.with_memory_space_constraint(weight, pltpu.HBM))


def down_scratch(w_down, columns):
    experts, depth, _ = w_down.shape
    block = 512 if columns % 512 == 0 else 128
    return [
        pltpu.VMEM((experts, depth, columns), w_down.dtype),
        pltpu.SemaphoreType.DMA((columns // block,)),
    ]


def up_call(entries, w_gate, w_ups, w_down, token, order, start, columns):
    experts, width, hidden = w_gate.shape
    full = entries[0].shape[1]
    rows = sum(e.shape[0] for e in entries)
    counts = (len(entries), len(w_ups))
    whole = pl.BlockSpec(memory_space=pltpu.VMEM)
    anywhere = pl.BlockSpec(memory_space=pl.ANY)
    out = jax.ShapeDtypeStruct((rows // 2, columns), jnp.bfloat16)
    return pl.pallas_call(
        functools.partial(up_kernel, counts, width, order, start),
        out_shape=(jax.ShapeDtypeStruct((rows, experts * hidden), jnp.bfloat16), out, out),
        in_specs=[anywhere] + [whole] * sum(counts) + [anywhere] * 2,
        out_specs=(whole,) * 3,
        scratch_shapes=[
            pltpu.VMEM((rows, full), jnp.bfloat16),
            pltpu.VMEM((experts, rows, hidden), jnp.float32),
            pltpu.VMEM(w_gate.shape, w_gate.dtype),
            pltpu.SemaphoreType.DMA((experts, 4)),
        ]
        + down_scratch(w_down, columns),
        compiler_params=pltpu.CompilerParams(vmem_limit_bytes=VMEM_LIMIT),
        cost_estimate=pl.CostEstimate(
            flops=4 * rows * experts * width * hidden + 2 * rows * experts * hidden * columns,
            bytes_accessed=2 * experts * hidden * columns,
            transcendentals=rows * experts * hidden,
        ),
        name="gate_up",
    )(
        token,
        *entries,
        *(pltpu.with_memory_space_constraint(w, pltpu.VMEM) for w in w_ups),
        pltpu.with_memory_space_constraint(w_gate, pltpu.HBM),
        pltpu.with_memory_space_constraint(w_down, pltpu.HBM),
    )


def down_kernel(order, start, hidden_ref, down_hbm, keep_ref, send_ref, down_ref, sems):
    copy = down_copy(start, down_hbm, down_ref, sems)
    for step in range(sems.shape[0]):
        copy(step).start()
    down_product(order, hidden_ref, down_ref, keep_ref, send_ref, sems, copy)


def down_call(order, hidden, w_down, start, columns):
    rows = hidden.shape[0] // 2
    out = jax.ShapeDtypeStruct((rows, columns), jnp.bfloat16)
    whole = pl.BlockSpec(memory_space=pltpu.VMEM)
    return pl.pallas_call(
        functools.partial(down_kernel, order, start),
        out_shape=(out, out),
        in_specs=[whole, pl.BlockSpec(memory_space=pl.ANY)],
        out_specs=(whole, whole),
        scratch_shapes=down_scratch(w_down, columns),
        compiler_params=pltpu.CompilerParams(vmem_limit_bytes=VMEM_LIMIT),
        cost_estimate=pl.CostEstimate(
            flops=2 * hidden.size * columns,
            bytes_accessed=2 * hidden.shape[1] * columns,
            transcendentals=0,
        ),
        name="down",
    )(hidden, pltpu.with_memory_space_constraint(w_down, pltpu.HBM))


def add(*values):
    total = values[0].astype(jnp.float32)
    for value in values[1:]:
        total = total + value.astype(jnp.float32)
    return total.astype(jnp.bfloat16)


def body(tokens, expert_ids, gate_weights, w_gate, w_up, w_down):
    sects, groups, lanes = (lax.axis_size(a) for a in AXES)
    row_count, width = tokens.shape
    experts = w_gate.shape[0]
    expert_count = sects * groups * experts

    half = -(-expert_count // 64) * 64
    block = extend(tokens, expert_ids, gate_weights, half)
    entries, w_ups, token = gather_rows(block, w_up)

    results = []
    chunk = width // CHUNKS
    hidden = None
    for c in range(CHUNKS):
        bits = bits_of(groups)
        bits = bits if c % 2 else bits[::-1]
        order = [0]
        for bit in bits:
            order = order + [o | bit for o in order]
        if c == 0:
            hidden, keep, send = up_call(
                entries, w_gate, w_ups, w_down, token, order, 0, chunk
            )
        else:
            keep, send = down_call(order, hidden, w_down, c * chunk, chunk)
        value = add(keep, swap(send, "sect", 1))
        for bit in bits[::-1]:
            middle = value.shape[0] // 2
            arrived = swap(value[middle:], "grp", bit)
            value = add(value[:middle], arrived)
        results.append(value)
    value = jnp.concatenate(results, axis=1)
    for bit in bits_of(lanes):
        middle = value.shape[0] // 2
        value = add(value[:middle], swap(value[middle:], "dev", bit))
    return value


def solution(mesh):
    in_specs = (
        P(AXES, None),
        P(AXES, None),
        P(AXES, None),
        P(("sect", "grp"), None, "dev"),
        P(("sect", "grp"), None, "dev"),
        P(("sect", "grp"), "dev", None),
    )
    return jax.shard_map(
        body, mesh=mesh, in_specs=in_specs, out_specs=P(AXES, None), check_vma=False
    )
```

```python
import functools

import jax
import jax.numpy as jnp
from jax import lax
from jax.experimental import pallas as pl
from jax.experimental.pallas import tpu as pltpu
from jax.sharding import PartitionSpec as P

AXES = ("sect", "grp", "dev")
VMEM_LIMIT = 20 * 2**20


def rounds_of():
    sects, groups, lanes = (lax.axis_size(a) for a in AXES)
    near = [1 << b for b in range(lanes.bit_length() - 1)][::-1]
    far = [lanes << b for b in range(groups.bit_length() - 1)][::-1]
    orders = [near + far, far[-1:] + near + far[:-1]]
    return [orders[s % 2] for s in range(sects)]


def swap(value, masks):
    count = lax.axis_size(("grp", "dev"))
    pairs = [
        (s * count + i, s * count + (i ^ mask)) for s, mask in enumerate(masks) for i in range(count)
    ]
    return lax.ppermute(value, AXES, pairs)


def swap_core(value):
    return lax.ppermute(value, "sect", [(0, 1), (1, 0)])


def vmem_call(kernel, out_shape, name, *operands):
    whole = pl.BlockSpec(memory_space=pltpu.VMEM)
    return pl.pallas_call(
        kernel,
        out_shape=out_shape,
        in_specs=[whole] * len(operands),
        out_specs=jax.tree.map(lambda _: whole, out_shape),
        compiler_params=pltpu.CompilerParams(vmem_limit_bytes=VMEM_LIMIT),
        name=name,
    )(*operands)


def extend_kernel(tokens_hbm, ids_hbm, weights_hbm, out_ref, tokens_ref, ids_ref, weights_ref, sems):
    pairs = ((ids_hbm, ids_ref), (weights_hbm, weights_ref), (tokens_hbm, tokens_ref))
    copies = [pltpu.make_async_copy(a, b, sems.at[i]) for i, (a, b) in enumerate(pairs)]
    for copy in copies:
        copy.start()
    rows, width = tokens_ref.shape
    half = (out_ref.shape[1] - width) // 2
    lane = lax.broadcasted_iota(jnp.int32, (rows, half * 2), 1)
    dense = jnp.zeros((rows, half * 2), jnp.float32)
    for copy in copies:
        copy.wait()
    for k in range(ids_ref.shape[1]):
        mine = lax.rem(lane, half) == ids_ref[:, k:k + 1]
        dense = dense + jnp.where(mine, weights_ref[:, k:k + 1], 0.0)
    high = dense.astype(jnp.bfloat16).astype(jnp.float32)
    out_ref[:, :width] = tokens_ref[...]
    out_ref[:, width:] = jnp.where(lane < half, high, dense - high).astype(jnp.bfloat16)


def extend(tokens, ids, weights, half):
    rows, width = tokens.shape
    return pl.pallas_call(
        extend_kernel,
        out_shape=jax.ShapeDtypeStruct((rows, width + 2 * half), tokens.dtype),
        in_specs=[pl.BlockSpec(memory_space=pl.ANY)] * 3,
        out_specs=pl.BlockSpec(memory_space=pltpu.VMEM),
        scratch_shapes=[pltpu.VMEM(v.shape, v.dtype) for v in (tokens, ids, weights)]
        + [pltpu.SemaphoreType.DMA((3,))],
        compiler_params=pltpu.CompilerParams(vmem_limit_bytes=VMEM_LIMIT),
        name="extend",
    )(*(pltpu.with_memory_space_constraint(v, pltpu.HBM) for v in (tokens, ids, weights)))


def stack_kernel(*refs):
    pieces, out_ref = refs[:-1], refs[-1]
    values = [p[...].astype(jnp.float32) for p in pieces]
    out_ref[...] = jnp.concatenate(values, axis=0).astype(out_ref.dtype)


def stack(*pieces):
    rows = sum(p.shape[0] for p in pieces)
    out = jax.ShapeDtypeStruct((rows, pieces[0].shape[1]), pieces[0].dtype)
    return vmem_call(stack_kernel, out, "stack", *pieces)


def gather_rows(block, w_up):
    line, weights, token = block, [], block
    rounds = list(zip(*rounds_of()))
    experts = w_up.shape[0]
    for number, masks in enumerate(rounds):
        arrived = swap(line, masks)
        expert = number - len(rounds) + experts
        if expert >= 0:
            weight, token = fetch(w_up, expert, token)
            weights.append(weight)
            arrived, token = lax.optimization_barrier((arrived, token))
        line = stack(line, arrived)
    return [line, swap_core(line)], weights, token


def down_copy(expert, block, down_hbm, target_ref, sems):
    hidden = down_hbm.shape[1]
    span = pl.ds(pl.multiple_of(block * hidden, hidden), hidden)
    return pltpu.make_async_copy(
        down_hbm.at[expert, :, span], target_ref.at[expert, span], sems.at[expert, block]
    )


def expert_kernel(counts, width, token_ref, *refs):
    pieces, up_refs = refs[:counts[0]], refs[counts[0]:sum(counts)]
    (gate_hbm, down_hbm, keep_ref, send_ref,
     rows_ref, up_ref, hidden_ref, gate_ref, gate_sems, sems) = refs[sum(counts):]
    experts, _, hidden = gate_ref.shape
    place = lax.axis_index("sect") * lax.axis_size("grp") + lax.axis_index("grp")
    first = place * experts
    block = min(256, hidden)
    gate_copies = weight_copies(gate_hbm, gate_ref, gate_sems)
    for gate_copy in gate_copies:
        gate_copy.start()

    at = 0
    for piece in pieces:
        rows_ref[pl.ds(at, piece.shape[0])] = piece[...]
        at += piece.shape[0]

    for e in range(experts):

        @pl.loop(0, hidden // block)
        def _(step):
            span = pl.ds(pl.multiple_of(step * block, block), block)
            up_ref[e, :, span] = jnp.dot(
                rows_ref[:, :width], up_refs[e][0, :, span], preferred_element_type=jnp.float32
            )

    extra = rows_ref[:, width:].astype(jnp.float32)
    lane = lax.broadcasted_iota(jnp.int32, extra.shape, 1)
    parts = gate_sems.shape[1]
    for e in range(experts):
        mine = lax.rem(lane, extra.shape[1] // 2) == first + e
        scale = jnp.sum(jnp.where(mine, extra, 0.0), axis=1, keepdims=True)
        for gate_copy in gate_copies[e * parts:(e + 1) * parts]:
            gate_copy.wait()

        @pl.loop(0, hidden // block)
        def _(step):
            span = pl.ds(pl.multiple_of(step * block, block), block)
            gate = jnp.dot(
                rows_ref[:, :width], gate_ref[e, :, span], preferred_element_type=jnp.float32
            )
            value = gate / (1.0 + jnp.exp(-gate)) * up_ref[e, :, span] * scale
            out = pl.ds(pl.multiple_of(e * hidden + step * block, block), block)
            hidden_ref[:, out] = value.astype(jnp.bfloat16)

        for step in range(width // hidden):
            down_copy(e, step, down_hbm, gate_ref, sems).start()

    middle = keep_ref.shape[0]

    @pl.loop(0, width // hidden)
    def _(step):
        for e in range(experts):
            down_copy(e, step, down_hbm, gate_ref, sems).wait()
        span = pl.ds(pl.multiple_of(step * hidden, hidden), hidden)
        weight = gate_ref[:, span, :].reshape(experts * hidden, hidden)
        total = jnp.dot(hidden_ref[...], weight, preferred_element_type=jnp.float32)
        total = total.astype(jnp.bfloat16)
        keep_ref[:, span] = total[:middle]
        send_ref[:, span] = total[middle:]


def fetch_kernel(expert, after_ref, source_ref, target_ref, token_ref, sems):
    copies = weight_copies(source_ref.at[pl.ds(expert, 1)], target_ref, sems)
    for copy in copies:
        copy.start()
    token_ref[...] = jnp.zeros_like(token_ref)
    for copy in copies:
        copy.wait()


def weight_copies(source_ref, target_ref, sems):
    experts, parts = sems.shape
    depth = source_ref.shape[1] // parts
    return [
        pltpu.make_async_copy(
            source_ref.at[e, pl.ds(p * depth, depth)],
            target_ref.at[e, pl.ds(p * depth, depth)],
            sems.at[e, p],
        )
        for e in range(experts)
        for p in range(parts)
    ]


def fetch(weight, expert, after):
    in_hbm = pl.BlockSpec(memory_space=pl.ANY)
    in_vmem = pl.BlockSpec(memory_space=pltpu.VMEM)
    return pl.pallas_call(
        functools.partial(fetch_kernel, expert),
        out_shape=(
            pltpu.VMEM((1, *weight.shape[1:]), weight.dtype),
            jax.ShapeDtypeStruct((8, 128), jnp.float32),
        ),
        in_specs=[in_hbm, in_hbm],
        out_specs=(in_vmem, in_vmem),
        scratch_shapes=[pltpu.SemaphoreType.DMA((1, 8))],
        compiler_params=pltpu.CompilerParams(vmem_limit_bytes=VMEM_LIMIT),
        cost_estimate=pl.CostEstimate(
            flops=0, bytes_accessed=2 * weight.size // weight.shape[0], transcendentals=0
        ),
        name="fetch",
    )(after, pltpu.with_memory_space_constraint(weight, pltpu.HBM))


def expert_call(entries, w_gate, w_ups, w_down, token):
    experts, width, hidden = w_gate.shape
    full = entries[0].shape[1]
    rows = sum(e.shape[0] for e in entries)
    counts = (len(entries), len(w_ups))
    whole = pl.BlockSpec(memory_space=pltpu.VMEM)
    anywhere = pl.BlockSpec(memory_space=pl.ANY)
    out = jax.ShapeDtypeStruct((rows // 2, width), jnp.bfloat16)
    return pl.pallas_call(
        functools.partial(expert_kernel, counts, width),
        out_shape=(out, out),
        in_specs=[anywhere] + [whole] * sum(counts) + [anywhere] * 2,
        out_specs=(whole,) * 2,
        scratch_shapes=[
            pltpu.VMEM((rows, full), jnp.bfloat16),
            pltpu.VMEM((experts, rows, hidden), jnp.float32),
            pltpu.VMEM((rows, experts * hidden), jnp.bfloat16),
            pltpu.VMEM(w_gate.shape, w_gate.dtype),
            pltpu.SemaphoreType.DMA((experts, 4)),
            pltpu.SemaphoreType.DMA((experts, width // hidden)),
        ],
        compiler_params=pltpu.CompilerParams(vmem_limit_bytes=VMEM_LIMIT),
        cost_estimate=pl.CostEstimate(
            flops=6 * rows * experts * width * hidden,
            bytes_accessed=2 * (w_gate.size + w_down.size),
            transcendentals=rows * experts * hidden,
        ),
        name="experts",
    )(
        token,
        *entries,
        *(pltpu.with_memory_space_constraint(w, pltpu.VMEM) for w in w_ups),
        pltpu.with_memory_space_constraint(w_gate, pltpu.HBM),
        pltpu.with_memory_space_constraint(w_down, pltpu.HBM),
    )


def add(*values):
    total = values[0].astype(jnp.float32)
    for value in values[1:]:
        total = total + value.astype(jnp.float32)
    return total.astype(jnp.bfloat16)


def body(tokens, expert_ids, gate_weights, w_gate, w_up, w_down):
    sects, groups, lanes = (lax.axis_size(a) for a in AXES)
    row_count, width = tokens.shape
    experts = w_gate.shape[0]
    expert_count = sects * groups * experts

    half = -(-expert_count // 64) * 64
    block = extend(tokens, expert_ids, gate_weights, half)
    entries, w_ups, token = gather_rows(block, w_up)

    results = []
    keep, send = expert_call(entries, w_gate, w_ups, w_down, token)
    value = add(keep, swap_core(send))
    for masks in list(zip(*rounds_of()))[::-1]:
        middle = value.shape[0] // 2
        value = add(value[:middle], swap(value[middle:], masks))
    return value


def solution(mesh):
    in_specs = (
        P(AXES, None),
        P(AXES, None),
        P(AXES, None),
        P(("sect", "grp"), None, "dev"),
        P(("sect", "grp"), None, "dev"),
        P(("sect", "grp"), "dev", None),
    )
    return jax.shard_map(
        body, mesh=mesh, in_specs=in_specs, out_specs=P(AXES, None), check_vma=False
    )
```

```python
import functools

import jax
import jax.numpy as jnp
from jax import lax
from jax.experimental import pallas as pl
from jax.experimental.pallas import tpu as pltpu
from jax.sharding import PartitionSpec as P

AXES = ("sect", "grp", "dev")
VMEM_LIMIT = 20 * 2**20


def rounds_of():
    sects, groups, _ = (lax.axis_size(a) for a in AXES)
    bits = [1 << b for b in range(groups.bit_length() - 1)]
    orders = [bits[::-1], bits]
    return list(zip(*(orders[s % 2] for s in range(sects))))


def swap(value, masks):
    count = lax.axis_size("grp")
    pairs = [
        (s * count + i, s * count + (i ^ mask)) for s, mask in enumerate(masks) for i in range(count)
    ]
    return lax.ppermute(value, ("sect", "grp"), pairs)


def swap_line(value, mask):
    return lax.ppermute(value, "dev", [(i, i ^ mask) for i in range(lax.axis_size("dev"))])


def swap_core(value):
    return lax.ppermute(value, "sect", [(0, 1), (1, 0)])


def vmem_call(kernel, out_shape, name, *operands):
    whole = pl.BlockSpec(memory_space=pltpu.VMEM)
    return pl.pallas_call(
        kernel,
        out_shape=out_shape,
        in_specs=[whole] * len(operands),
        out_specs=jax.tree.map(lambda _: whole, out_shape),
        compiler_params=pltpu.CompilerParams(vmem_limit_bytes=VMEM_LIMIT),
        name=name,
    )(*operands)


def extend_kernel(tokens_hbm, ids_hbm, weights_hbm, out_ref, tokens_ref, ids_ref, weights_ref, sems):
    pairs = ((ids_hbm, ids_ref), (weights_hbm, weights_ref), (tokens_hbm, tokens_ref))
    copies = [pltpu.make_async_copy(a, b, sems.at[i]) for i, (a, b) in enumerate(pairs)]
    for copy in copies:
        copy.start()
    rows, width = tokens_ref.shape
    half = (out_ref.shape[1] - width) // 2
    lane = lax.broadcasted_iota(jnp.int32, (rows, half * 2), 1)
    dense = jnp.zeros((rows, half * 2), jnp.float32)
    for copy in copies:
        copy.wait()
    for k in range(ids_ref.shape[1]):
        mine = lax.rem(lane, half) == ids_ref[:, k:k + 1]
        dense = dense + jnp.where(mine, weights_ref[:, k:k + 1], 0.0)
    high = dense.astype(jnp.bfloat16).astype(jnp.float32)
    out_ref[:, :width] = tokens_ref[...]
    out_ref[:, width:] = jnp.where(lane < half, high, dense - high).astype(jnp.bfloat16)


def extend(tokens, ids, weights, half):
    rows, width = tokens.shape
    return pl.pallas_call(
        extend_kernel,
        out_shape=jax.ShapeDtypeStruct((rows, width + 2 * half), tokens.dtype),
        in_specs=[pl.BlockSpec(memory_space=pl.ANY)] * 3,
        out_specs=pl.BlockSpec(memory_space=pltpu.VMEM),
        scratch_shapes=[pltpu.VMEM(v.shape, v.dtype) for v in (tokens, ids, weights)]
        + [pltpu.SemaphoreType.DMA((3,))],
        compiler_params=pltpu.CompilerParams(vmem_limit_bytes=VMEM_LIMIT),
        name="extend",
    )(*(pltpu.with_memory_space_constraint(v, pltpu.HBM) for v in (tokens, ids, weights)))


def stack_kernel(*refs):
    pieces, out_ref = refs[:-1], refs[-1]
    values = [p[...].astype(jnp.float32) for p in pieces]
    out_ref[...] = jnp.concatenate(values, axis=0).astype(out_ref.dtype)


def stack(*pieces):
    rows = sum(p.shape[0] for p in pieces)
    out = jax.ShapeDtypeStruct((rows, pieces[0].shape[1]), pieces[0].dtype)
    return vmem_call(stack_kernel, out, "stack", *pieces)


def gather_rows(block, w_up, w_gate):
    wanted = [(w_up, e) for e in range(w_up.shape[0])] + [(w_gate, 0)]
    weights, token = [], block

    def meanwhile(arrived, token):
        if wanted:
            weight, token = fetch(*wanted.pop(0), token)
            weights.append(weight)
            arrived, token = lax.optimization_barrier((arrived, token))
        return arrived, token

    arrived = [swap_line(block, m) for m in range(1, lax.axis_size("dev"))]
    arrived, token = meanwhile(arrived, token)
    line = stack(block, *arrived)
    for masks in rounds_of():
        arrived, token = meanwhile(swap(line, masks), token)
        line = stack(line, arrived)
    while wanted:
        _, token = meanwhile(line, token)
    return [line, swap_core(line)], weights, token


def down_copy(expert, block, down_hbm, target_ref, sems):
    hidden = down_hbm.shape[1]
    span = pl.ds(pl.multiple_of(block * hidden, hidden), hidden)
    return pltpu.make_async_copy(
        down_hbm.at[expert, :, span], target_ref.at[expert, span], sems.at[expert, block]
    )


def expert_kernel(counts, width, token_ref, *refs):
    pieces, up_refs = refs[:counts[0]], refs[counts[0]:sum(counts) - 1]
    first_gate_ref = refs[sum(counts) - 1]
    (gate_hbm, down_hbm, keep_ref, send_ref,
     rows_ref, up_ref, hidden_ref, scratch_ref, gate_sems, sems) = refs[sum(counts):]
    experts, _, hidden = scratch_ref.shape
    place = lax.axis_index("sect") * lax.axis_size("grp") + lax.axis_index("grp")
    first = place * experts
    block = min(256, hidden)
    for e in range(1, experts):
        for copy in weight_copies(gate_hbm, scratch_ref, gate_sems, e):
            copy.start()

    at = 0
    for piece in pieces:
        rows_ref[pl.ds(at, piece.shape[0])] = piece[...]
        at += piece.shape[0]

    for e in range(experts):

        @pl.loop(0, hidden // block)
        def _(step):
            span = pl.ds(pl.multiple_of(step * block, block), block)
            up_ref[e, :, span] = jnp.dot(
                rows_ref[:, :width], up_refs[e][0, :, span], preferred_element_type=jnp.float32
            )

        if e == 0:
            for step in range(width // hidden):
                down_copy(0, step, down_hbm, scratch_ref, sems).start()

    extra = rows_ref[:, width:].astype(jnp.float32)
    lane = lax.broadcasted_iota(jnp.int32, extra.shape, 1)
    for e in range(experts):
        mine = lax.rem(lane, extra.shape[1] // 2) == first + e
        scale = jnp.sum(jnp.where(mine, extra, 0.0), axis=1, keepdims=True)
        if e > 0:
            for copy in weight_copies(gate_hbm, scratch_ref, gate_sems, e):
                copy.wait()
        gate_ref = first_gate_ref.at[0] if e == 0 else scratch_ref.at[e]

        @pl.loop(0, hidden // block)
        def _(step):
            span = pl.ds(pl.multiple_of(step * block, block), block)
            gate = jnp.dot(
                rows_ref[:, :width], gate_ref[:, span], preferred_element_type=jnp.float32
            )
            value = gate / (1.0 + jnp.exp(-gate)) * up_ref[e, :, span] * scale
            out = pl.ds(pl.multiple_of(e * hidden + step * block, block), block)
            hidden_ref[:, out] = value.astype(jnp.bfloat16)

        if e > 0:
            for step in range(width // hidden):
                down_copy(e, step, down_hbm, scratch_ref, sems).start()

    middle = keep_ref.shape[0]

    @pl.loop(0, width // hidden)
    def _(step):
        for e in range(experts):
            down_copy(e, step, down_hbm, scratch_ref, sems).wait()
        span = pl.ds(pl.multiple_of(step * hidden, hidden), hidden)
        weight = scratch_ref[:, span, :].reshape(experts * hidden, hidden)
        total = jnp.dot(hidden_ref[...], weight, preferred_element_type=jnp.float32)
        total = total.astype(jnp.bfloat16)
        keep_ref[:, span] = total[:middle]
        send_ref[:, span] = total[middle:]


def fetch_kernel(expert, after_ref, source_ref, target_ref, token_ref, sems):
    copies = weight_copies(source_ref.at[pl.ds(expert, 1)], target_ref, sems, 0)
    for copy in copies:
        copy.start()
    token_ref[...] = jnp.zeros_like(token_ref)
    for copy in copies:
        copy.wait()


def weight_copies(source_ref, target_ref, sems, expert):
    parts = sems.shape[1]
    depth = source_ref.shape[1] // parts
    return [
        pltpu.make_async_copy(
            source_ref.at[expert, pl.ds(p * depth, depth)],
            target_ref.at[expert, pl.ds(p * depth, depth)],
            sems.at[expert, p],
        )
        for p in range(parts)
    ]


def fetch(weight, expert, after):
    in_hbm = pl.BlockSpec(memory_space=pl.ANY)
    in_vmem = pl.BlockSpec(memory_space=pltpu.VMEM)
    return pl.pallas_call(
        functools.partial(fetch_kernel, expert),
        out_shape=(
            pltpu.VMEM((1, *weight.shape[1:]), weight.dtype),
            jax.ShapeDtypeStruct((8, 128), jnp.float32),
        ),
        in_specs=[in_hbm, in_hbm],
        out_specs=(in_vmem, in_vmem),
        scratch_shapes=[pltpu.SemaphoreType.DMA((1, 8))],
        compiler_params=pltpu.CompilerParams(vmem_limit_bytes=VMEM_LIMIT),
        cost_estimate=pl.CostEstimate(
            flops=0, bytes_accessed=2 * weight.size // weight.shape[0], transcendentals=0
        ),
        name="fetch",
    )(after, pltpu.with_memory_space_constraint(weight, pltpu.HBM))


def expert_call(entries, w_gate, held, w_down, token):
    experts, width, hidden = w_gate.shape
    full = entries[0].shape[1]
    rows = sum(e.shape[0] for e in entries)
    counts = (len(entries), len(held))
    whole = pl.BlockSpec(memory_space=pltpu.VMEM)
    anywhere = pl.BlockSpec(memory_space=pl.ANY)
    out = jax.ShapeDtypeStruct((rows // 2, width), jnp.bfloat16)
    return pl.pallas_call(
        functools.partial(expert_kernel, counts, width),
        out_shape=(out, out),
        in_specs=[anywhere] + [whole] * sum(counts) + [anywhere] * 2,
        out_specs=(whole,) * 2,
        scratch_shapes=[
            pltpu.VMEM((rows, full), jnp.bfloat16),
            pltpu.VMEM((experts, rows, hidden), jnp.float32),
            pltpu.VMEM((rows, experts * hidden), jnp.bfloat16),
            pltpu.VMEM(w_gate.shape, w_gate.dtype),
            pltpu.SemaphoreType.DMA((experts, 4)),
            pltpu.SemaphoreType.DMA((experts, width // hidden)),
        ],
        compiler_params=pltpu.CompilerParams(vmem_limit_bytes=VMEM_LIMIT),
        cost_estimate=pl.CostEstimate(
            flops=6 * rows * experts * width * hidden,
            bytes_accessed=2 * (w_gate.size + w_down.size),
            transcendentals=rows * experts * hidden,
        ),
        name="experts",
    )(
        token,
        *entries,
        *(pltpu.with_memory_space_constraint(w, pltpu.VMEM) for w in held),
        pltpu.with_memory_space_constraint(w_gate, pltpu.HBM),
        pltpu.with_memory_space_constraint(w_down, pltpu.HBM),
    )


def add(*values):
    total = values[0].astype(jnp.float32)
    for value in values[1:]:
        total = total + value.astype(jnp.float32)
    return total.astype(jnp.bfloat16)


def body(tokens, expert_ids, gate_weights, w_gate, w_up, w_down):
    sects, groups, lanes = (lax.axis_size(a) for a in AXES)
    row_count, width = tokens.shape
    experts = w_gate.shape[0]
    expert_count = sects * groups * experts

    half = -(-expert_count // 64) * 64
    block = extend(tokens, expert_ids, gate_weights, half)
    entries, held, token = gather_rows(block, w_up, w_gate)

    results = []
    keep, send = expert_call(entries, w_gate, held, w_down, token)
    value = add(keep, swap_core(send))
    for masks in rounds_of()[::-1]:
        middle = value.shape[0] // 2
        value = add(value[:middle], swap(value[middle:], masks))
    own = [value[m * row_count:(m + 1) * row_count] for m in range(lanes)]
    return add(own[0], *(swap_line(own[m], m) for m in range(1, lanes)))


def solution(mesh):
    in_specs = (
        P(AXES, None),
        P(AXES, None),
        P(AXES, None),
        P(("sect", "grp"), None, "dev"),
        P(("sect", "grp"), None, "dev"),
        P(("sect", "grp"), "dev", None),
    )
    return jax.shard_map(
        body, mesh=mesh, in_specs=in_specs, out_specs=P(AXES, None), check_vma=False
    )
```

```python
import functools

import jax
import jax.numpy as jnp
from jax import lax
from jax.experimental import pallas as pl
from jax.experimental.pallas import tpu as pltpu
from jax.sharding import PartitionSpec as P

AXES = ("sect", "grp", "dev")
VMEM_LIMIT = 10 * 2**20


def rounds_of():
    sects, groups, _ = (lax.axis_size(a) for a in AXES)
    bits = [1 << b for b in range(groups.bit_length() - 1)]
    orders = [bits[::-1], bits]
    return list(zip(*(orders[s % 2] for s in range(sects))))


def swap(value, masks):
    count = lax.axis_size("grp")
    pairs = [
        (s * count + i, s * count + (i ^ mask)) for s, mask in enumerate(masks) for i in range(count)
    ]
    return lax.ppermute(value, ("sect", "grp"), pairs)


def swap_line(value, mask):
    return lax.ppermute(value, "dev", [(i, i ^ mask) for i in range(lax.axis_size("dev"))])


def swap_core(value):
    return lax.ppermute(value, "sect", [(0, 1), (1, 0)])


def vmem_call(kernel, out_shape, name, *operands):
    whole = pl.BlockSpec(memory_space=pltpu.VMEM)
    return pl.pallas_call(
        kernel,
        out_shape=out_shape,
        in_specs=[whole] * len(operands),
        out_specs=jax.tree.map(lambda _: whole, out_shape),
        compiler_params=pltpu.CompilerParams(vmem_limit_bytes=VMEM_LIMIT),
        name=name,
    )(*operands)


def extend_kernel(tokens_hbm, ids_hbm, weights_hbm, out_ref, tokens_ref, ids_ref, weights_ref, sems):
    pairs = ((ids_hbm, ids_ref), (weights_hbm, weights_ref), (tokens_hbm, tokens_ref))
    copies = [pltpu.make_async_copy(a, b, sems.at[i]) for i, (a, b) in enumerate(pairs)]
    for copy in copies:
        copy.start()
    rows, width = tokens_ref.shape
    half = (out_ref.shape[1] - width) // 2
    lane = lax.broadcasted_iota(jnp.int32, (rows, half * 2), 1)
    dense = jnp.zeros((rows, half * 2), jnp.float32)
    for copy in copies:
        copy.wait()
    for k in range(ids_ref.shape[1]):
        mine = lax.rem(lane, half) == ids_ref[:, k:k + 1]
        dense = dense + jnp.where(mine, weights_ref[:, k:k + 1], 0.0)
    high = dense.astype(jnp.bfloat16).astype(jnp.float32)
    out_ref[:, :width] = tokens_ref[...]
    out_ref[:, width:] = jnp.where(lane < half, high, dense - high).astype(jnp.bfloat16)


def extend(tokens, ids, weights, half):
    rows, width = tokens.shape
    return pl.pallas_call(
        extend_kernel,
        out_shape=jax.ShapeDtypeStruct((rows, width + 2 * half), tokens.dtype),
        in_specs=[pl.BlockSpec(memory_space=pl.ANY)] * 3,
        out_specs=pl.BlockSpec(memory_space=pltpu.VMEM),
        scratch_shapes=[pltpu.VMEM(v.shape, v.dtype) for v in (tokens, ids, weights)]
        + [pltpu.SemaphoreType.DMA((3,))],
        compiler_params=pltpu.CompilerParams(vmem_limit_bytes=VMEM_LIMIT),
        name="extend",
    )(*(pltpu.with_memory_space_constraint(v, pltpu.HBM) for v in (tokens, ids, weights)))


def stack_kernel(*refs):
    pieces, out_ref = refs[:-1], refs[-1]
    values = [p[...].astype(jnp.float32) for p in pieces]
    out_ref[...] = jnp.concatenate(values, axis=0).astype(out_ref.dtype)


def stack(*pieces):
    rows = sum(p.shape[0] for p in pieces)
    out = jax.ShapeDtypeStruct((rows, pieces[0].shape[1]), pieces[0].dtype)
    return vmem_call(stack_kernel, out, "stack", *pieces)


def gather_rows(block, w_up, w_gate):
    wanted = [(w_up, e) for e in range(w_up.shape[0])] + [(w_gate, 0)]
    weights, token = [], block

    def meanwhile(arrived, token):
        if wanted:
            weight, token = fetch(*wanted.pop(0), token)
            weights.append(weight)
            arrived, token = lax.optimization_barrier((arrived, token))
        return arrived, token

    arrived = [swap_line(block, m) for m in range(1, lax.axis_size("dev"))]
    arrived, token = meanwhile(arrived, token)
    line = stack(block, *arrived)
    rounds = rounds_of()
    for masks in rounds[:-1]:
        arrived, token = meanwhile(swap(line, masks), token)
        line = stack(line, arrived)
    last = swap(line, rounds[-1])
    mine, token = meanwhile(line, token)
    last, other, token = lax.optimization_barrier((last, swap_core(mine), token))
    while wanted:
        _, token = meanwhile(line, token)
    return [line, last, other, swap_core(last)], weights, token


def down_copy(expert, block, down_hbm, target_ref, sems):
    hidden = down_hbm.shape[1]
    span = pl.ds(pl.multiple_of(block * hidden, hidden), hidden)
    return pltpu.make_async_copy(
        down_hbm.at[expert, :, span], target_ref.at[expert, span], sems.at[expert, block]
    )


def down_block(step, hidden_ref, weights_ref, keep_ref, send_ref, first):
    experts, _, hidden = weights_ref.shape
    middle = keep_ref.shape[0]
    rows = pl.ds(pl.multiple_of((first + step) * hidden, hidden), hidden)
    weight = weights_ref[:, rows, :].reshape(experts * hidden, hidden)
    total = jnp.dot(hidden_ref[...], weight, preferred_element_type=jnp.float32)
    total = total.astype(jnp.bfloat16)
    span = pl.ds(pl.multiple_of(step * hidden, hidden), hidden)
    keep_ref[:, span] = total[:middle]
    send_ref[:, span] = total[middle:]


def expert_kernel(counts, width, token_ref, *refs):
    pieces, up_refs = refs[:counts[0]], refs[counts[0]:sum(counts) - 1]
    first_gate_ref = refs[sum(counts) - 1]
    (gate_hbm, down_hbm, hidden_ref, keep_ref, send_ref, weights_ref,
     rows_ref, up_ref, gate_sems, sems) = refs[sum(counts):]
    experts, _, hidden = weights_ref.shape
    place = lax.axis_index("sect") * lax.axis_size("grp") + lax.axis_index("grp")
    first = place * experts
    block = min(256, hidden)
    blocks = width // hidden
    for e in range(1, experts):
        for copy in weight_copies(gate_hbm, weights_ref, gate_sems, e):
            copy.start()

    at = 0
    for piece in pieces:
        rows_ref[pl.ds(at, piece.shape[0])] = piece[...]
        at += piece.shape[0]

    for e in range(experts):

        @pl.loop(0, hidden // block, unroll=True)
        def _(step):
            span = pl.ds(pl.multiple_of(step * block, block), block)
            up_ref[e, :, span] = jnp.dot(
                rows_ref[:, :width], up_refs[e][0, :, span], preferred_element_type=jnp.float32
            )

        if e == 0:
            for step in range(blocks):
                down_copy(0, step, down_hbm, weights_ref, sems).start()

    extra = rows_ref[:, width:].astype(jnp.float32)
    lane = lax.broadcasted_iota(jnp.int32, extra.shape, 1)
    for e in range(experts):
        mine = lax.rem(lane, extra.shape[1] // 2) == first + e
        scale = jnp.sum(jnp.where(mine, extra, 0.0), axis=1, keepdims=True)
        if e > 0:
            for copy in weight_copies(gate_hbm, weights_ref, gate_sems, e):
                copy.wait()
        gate_ref = first_gate_ref.at[0] if e == 0 else weights_ref.at[e]

        @pl.loop(0, hidden // block, unroll=True)
        def _(step):
            span = pl.ds(pl.multiple_of(step * block, block), block)
            gate = jnp.dot(
                rows_ref[:, :width], gate_ref[:, span], preferred_element_type=jnp.float32
            )
            value = gate / (1.0 + jnp.exp(-gate)) * up_ref[e, :, span] * scale
            out = pl.ds(pl.multiple_of(e * hidden + step * block, block), block)
            hidden_ref[:, out] = value.astype(jnp.bfloat16)

        if e > 0:
            for step in range(blocks):
                down_copy(e, step, down_hbm, weights_ref, sems).start()

    @pl.loop(0, blocks // 2)
    def _(step):
        for e in range(experts):
            down_copy(e, step, down_hbm, weights_ref, sems).wait()
        down_block(step, hidden_ref, weights_ref, keep_ref, send_ref, 0)

    for step in range(blocks // 2, blocks):
        for e in range(experts):
            down_copy(e, step, down_hbm, weights_ref, sems).wait()


def down_kernel(first, hidden_ref, weights_ref, keep_ref, send_ref):
    @pl.loop(0, keep_ref.shape[1] // weights_ref.shape[2], unroll=True)
    def _(step):
        down_block(step, hidden_ref, weights_ref, keep_ref, send_ref, first)


def fetch_kernel(expert, after_ref, source_ref, target_ref, token_ref, sems):
    copies = weight_copies(source_ref.at[pl.ds(expert, 1)], target_ref, sems, 0)
    for copy in copies:
        copy.start()
    token_ref[...] = jnp.zeros_like(token_ref)
    for copy in copies:
        copy.wait()


def weight_copies(source_ref, target_ref, sems, expert):
    parts = sems.shape[1]
    depth = source_ref.shape[1] // parts
    return [
        pltpu.make_async_copy(
            source_ref.at[expert, pl.ds(p * depth, depth)],
            target_ref.at[expert, pl.ds(p * depth, depth)],
            sems.at[expert, p],
        )
        for p in range(parts)
    ]


def fetch(weight, expert, after):
    in_hbm = pl.BlockSpec(memory_space=pl.ANY)
    in_vmem = pl.BlockSpec(memory_space=pltpu.VMEM)
    return pl.pallas_call(
        functools.partial(fetch_kernel, expert),
        out_shape=(
            pltpu.VMEM((1, *weight.shape[1:]), weight.dtype),
            jax.ShapeDtypeStruct((8, 128), jnp.float32),
        ),
        in_specs=[in_hbm, in_hbm],
        out_specs=(in_vmem, in_vmem),
        scratch_shapes=[pltpu.SemaphoreType.DMA((1, 8))],
        compiler_params=pltpu.CompilerParams(vmem_limit_bytes=VMEM_LIMIT),
        cost_estimate=pl.CostEstimate(
            flops=0, bytes_accessed=2 * weight.size // weight.shape[0], transcendentals=0
        ),
        name="fetch",
    )(after, pltpu.with_memory_space_constraint(weight, pltpu.HBM))


def expert_call(entries, w_gate, held, w_down, token):
    experts, width, hidden = w_gate.shape
    full = entries[0].shape[1]
    rows = sum(e.shape[0] for e in entries)
    counts = (len(entries), len(held))
    blocks = width // hidden
    whole = pl.BlockSpec(memory_space=pltpu.VMEM)
    anywhere = pl.BlockSpec(memory_space=pl.ANY)
    columns = (blocks // 2 * hidden, (blocks - blocks // 2) * hidden)
    outs = [jax.ShapeDtypeStruct((rows // 2, c), jnp.bfloat16) for c in columns]
    hiddens, keep, send, weights = pl.pallas_call(
        functools.partial(expert_kernel, counts, width),
        out_shape=(
            jax.ShapeDtypeStruct((rows, experts * hidden), jnp.bfloat16),
            outs[0],
            outs[0],
            pltpu.VMEM(w_gate.shape, w_gate.dtype),
        ),
        in_specs=[anywhere] + [whole] * sum(counts) + [anywhere] * 2,
        out_specs=(whole,) * 4,
        scratch_shapes=[
            pltpu.VMEM((rows, full), jnp.bfloat16),
            pltpu.VMEM((experts, rows, hidden), jnp.float32),
            pltpu.SemaphoreType.DMA((experts, 4)),
            pltpu.SemaphoreType.DMA((experts, blocks)),
        ],
        compiler_params=pltpu.CompilerParams(vmem_limit_bytes=VMEM_LIMIT),
        cost_estimate=pl.CostEstimate(
            flops=5 * rows * experts * width * hidden,
            bytes_accessed=2 * (w_gate.size + w_down.size),
            transcendentals=rows * experts * hidden,
        ),
        name="experts",
    )(
        token,
        *entries,
        *(pltpu.with_memory_space_constraint(w, pltpu.VMEM) for w in held),
        pltpu.with_memory_space_constraint(w_gate, pltpu.HBM),
        pltpu.with_memory_space_constraint(w_down, pltpu.HBM),
    )
    later = pl.pallas_call(
        functools.partial(down_kernel, blocks // 2),
        out_shape=(outs[1], outs[1]),
        in_specs=[whole, whole],
        out_specs=(whole, whole),
        compiler_params=pltpu.CompilerParams(vmem_limit_bytes=VMEM_LIMIT),
        cost_estimate=pl.CostEstimate(
            flops=rows * experts * width * hidden,
            bytes_accessed=2 * rows * columns[1],
            transcendentals=0,
        ),
        name="down",
    )(hiddens, pltpu.with_memory_space_constraint(weights, pltpu.VMEM))
    return (keep, send), later


def add(*values):
    total = values[0].astype(jnp.float32)
    for value in values[1:]:
        total = total + value.astype(jnp.float32)
    return total.astype(jnp.bfloat16)


def body(tokens, expert_ids, gate_weights, w_gate, w_up, w_down):
    sects, groups, lanes = (lax.axis_size(a) for a in AXES)
    row_count, width = tokens.shape
    experts = w_gate.shape[0]
    expert_count = sects * groups * experts

    half = -(-expert_count // 64) * 64
    block = extend(tokens, expert_ids, gate_weights, half)
    entries, held, token = gather_rows(block, w_up, w_gate)

    results = []
    halves = []
    for keep, send in expert_call(entries, w_gate, held, w_down, token):
        value = add(keep, swap_core(send))
        for masks in rounds_of()[::-1]:
            middle = value.shape[0] // 2
            value = add(value[:middle], swap(value[middle:], masks))
        halves.append(value)
    value = jnp.concatenate(halves, axis=1)
    own = [value[m * row_count:(m + 1) * row_count] for m in range(lanes)]
    return add(own[0], *(swap_line(own[m], m) for m in range(1, lanes)))


def solution(mesh):
    in_specs = (
        P(AXES, None),
        P(AXES, None),
        P(AXES, None),
        P(("sect", "grp"), None, "dev"),
        P(("sect", "grp"), None, "dev"),
        P(("sect", "grp"), "dev", None),
    )
    return jax.shard_map(
        body, mesh=mesh, in_specs=in_specs, out_specs=P(AXES, None), check_vma=False
    )
```

```python
import functools

import jax
import jax.numpy as jnp
from jax import lax
from jax.experimental import pallas as pl
from jax.experimental.pallas import tpu as pltpu
from jax.sharding import PartitionSpec as P

AXES = ("sect", "grp", "dev")
VMEM_LIMIT = 12 * 2**20


def rounds_of():
    sects, groups, _ = (lax.axis_size(a) for a in AXES)
    bits = [1 << b for b in range(groups.bit_length() - 1)]
    orders = [bits[::-1], bits]
    return list(zip(*(orders[s % 2] for s in range(sects))))


def swap(value, masks):
    count = lax.axis_size("grp")
    pairs = [
        (s * count + i, s * count + (i ^ mask)) for s, mask in enumerate(masks) for i in range(count)
    ]
    return lax.ppermute(value, ("sect", "grp"), pairs)


def swap_line(value, mask):
    return lax.ppermute(value, "dev", [(i, i ^ mask) for i in range(lax.axis_size("dev"))])


def swap_core(value):
    return lax.ppermute(value, "sect", [(0, 1), (1, 0)])


def vmem_call(kernel, out_shape, name, *operands):
    whole = pl.BlockSpec(memory_space=pltpu.VMEM)
    return pl.pallas_call(
        kernel,
        out_shape=out_shape,
        in_specs=[whole] * len(operands),
        out_specs=jax.tree.map(lambda _: whole, out_shape),
        compiler_params=pltpu.CompilerParams(vmem_limit_bytes=VMEM_LIMIT),
        name=name,
    )(*operands)


def extend_kernel(tokens_hbm, ids_hbm, weights_hbm, out_ref, tokens_ref, ids_ref, weights_ref, sems):
    pairs = ((ids_hbm, ids_ref), (weights_hbm, weights_ref), (tokens_hbm, tokens_ref))
    copies = [pltpu.make_async_copy(a, b, sems.at[i]) for i, (a, b) in enumerate(pairs)]
    for copy in copies:
        copy.start()
    rows, width = tokens_ref.shape
    half = (out_ref.shape[1] - width) // 2
    lane = lax.broadcasted_iota(jnp.int32, (rows, half * 2), 1)
    dense = jnp.zeros((rows, half * 2), jnp.float32)
    for copy in copies:
        copy.wait()
    for k in range(ids_ref.shape[1]):
        mine = lax.rem(lane, half) == ids_ref[:, k:k + 1]
        dense = dense + jnp.where(mine, weights_ref[:, k:k + 1], 0.0)
    high = dense.astype(jnp.bfloat16).astype(jnp.float32)
    out_ref[:, :width] = tokens_ref[...]
    out_ref[:, width:] = jnp.where(lane < half, high, dense - high).astype(jnp.bfloat16)


def extend(tokens, ids, weights, half):
    rows, width = tokens.shape
    return pl.pallas_call(
        extend_kernel,
        out_shape=jax.ShapeDtypeStruct((rows, width + 2 * half), tokens.dtype),
        in_specs=[pl.BlockSpec(memory_space=pl.ANY)] * 3,
        out_specs=pl.BlockSpec(memory_space=pltpu.VMEM),
        scratch_shapes=[pltpu.VMEM(v.shape, v.dtype) for v in (tokens, ids, weights)]
        + [pltpu.SemaphoreType.DMA((3,))],
        compiler_params=pltpu.CompilerParams(vmem_limit_bytes=VMEM_LIMIT),
        name="extend",
    )(*(pltpu.with_memory_space_constraint(v, pltpu.HBM) for v in (tokens, ids, weights)))


def stack_kernel(*refs):
    pieces, out_ref = refs[:-1], refs[-1]
    values = [p[...].astype(jnp.float32) for p in pieces]
    out_ref[...] = jnp.concatenate(values, axis=0).astype(out_ref.dtype)


def stack(*pieces):
    rows = sum(p.shape[0] for p in pieces)
    out = jax.ShapeDtypeStruct((rows, pieces[0].shape[1]), pieces[0].dtype)
    return vmem_call(stack_kernel, out, "stack", *pieces)


def gather_rows(block, w_up, w_gate):
    wanted = [(w, e) for w in (w_gate, w_up) for e in range(w.shape[0])]
    weights, token = [], block

    def meanwhile(arrived, token):
        if wanted:
            weight, token = fetch(*wanted.pop(0), token)
            weights.append(weight)
            arrived, token = lax.optimization_barrier((arrived, token))
        return arrived, token

    arrived = [swap_line(block, m) for m in range(1, lax.axis_size("dev"))]
    arrived, token = meanwhile(arrived, token)
    line = stack(block, *arrived)
    rounds = rounds_of()
    for masks in rounds[:-1]:
        arrived, token = meanwhile(swap(line, masks), token)
        line = stack(line, arrived)
    last = swap(line, rounds[-1])
    mine, token = meanwhile(line, token)
    other = swap_core(mine)
    while wanted:
        weight, token = fetch(*wanted.pop(0), token)
        weights.append(weight)
    last, other, token = lax.optimization_barrier((last, other, token))
    return [line, last, other, swap_core(last)], weights, token


def down_copy(expert, block, down_hbm, target_ref, sems):
    hidden = down_hbm.shape[1]
    span = pl.ds(block * hidden, hidden)
    return pltpu.make_async_copy(
        down_hbm.at[expert, :, span], target_ref.at[0, span], sems.at[expert, block]
    )


def down_block(block, at, hidden_ref, down_refs, keep_ref, send_ref):
    hidden = down_refs[0].shape[2]
    middle = keep_ref.shape[0]
    rows = pl.ds(block * hidden, hidden)
    weight = jnp.concatenate([ref[0, rows, :] for ref in down_refs], axis=0)
    total = jnp.dot(hidden_ref[...], weight, preferred_element_type=jnp.float32)
    total = total.astype(jnp.bfloat16)
    span = pl.ds(at * hidden, hidden)
    keep_ref[:, span] = total[:middle]
    send_ref[:, span] = total[middle:]


def expert_kernel(entry_count, experts, width, token_ref, *refs):
    pieces, refs = refs[:entry_count], refs[entry_count:]
    gate_refs, up_refs, refs = refs[:experts], refs[experts:2 * experts], refs[2 * experts:]
    down_hbm, hidden_ref, keep_ref, send_ref = refs[:4]
    down_refs, (rows_ref, value_ref, sems) = refs[4:4 + experts], refs[4 + experts:]
    hidden = gate_refs[0].shape[2]
    place = lax.axis_index("sect") * lax.axis_size("grp") + lax.axis_index("grp")
    first = place * experts
    block = min(256, hidden)
    blocks = width // hidden

    at = 0
    for piece in pieces:
        rows_ref[pl.ds(at, piece.shape[0])] = piece[...]
        at += piece.shape[0]

    for e in range(experts):
        for step in range(hidden // block):
            span = pl.ds(step * block, block)
            gate = jnp.dot(
                rows_ref[:, :width], gate_refs[e][0, :, span], preferred_element_type=jnp.float32
            )
            value_ref[e, :, span] = gate / (1.0 + jnp.exp(-gate))
        for step in range(blocks // 2):
            down_copy(e, step, down_hbm, down_refs[e], sems).start()

    for step in range(blocks // 2, blocks):
        for e in range(experts):
            down_copy(e, step, down_hbm, down_refs[e], sems).start()

    extra = rows_ref[:, width:].astype(jnp.float32)
    lane = lax.broadcasted_iota(jnp.int32, extra.shape, 1)
    for e in range(experts):
        mine = lax.rem(lane, extra.shape[1] // 2) == first + e
        scale = jnp.sum(jnp.where(mine, extra, 0.0), axis=1, keepdims=True)
        for step in range(hidden // block):
            span = pl.ds(step * block, block)
            up = jnp.dot(
                rows_ref[:, :width], up_refs[e][0, :, span], preferred_element_type=jnp.float32
            )
            value = value_ref[e, :, span] * up * scale
            hidden_ref[:, pl.ds(e * hidden + step * block, block)] = value.astype(jnp.bfloat16)

    for step in range(blocks // 2):
        for e in range(experts):
            down_copy(e, step, down_hbm, down_refs[e], sems).wait()
        down_block(step, step, hidden_ref, down_refs, keep_ref, send_ref)

    for step in range(blocks // 2, blocks):
        for e in range(experts):
            down_copy(e, step, down_hbm, down_refs[e], sems).wait()


def down_kernel(first, hidden_ref, *refs):
    *down_refs, keep_ref, send_ref = refs
    for step in range(keep_ref.shape[1] // down_refs[0].shape[2]):
        down_block(first + step, step, hidden_ref, down_refs, keep_ref, send_ref)


def fetch_kernel(expert, after_ref, source_ref, target_ref, token_ref, sems):
    copies = weight_copies(source_ref.at[pl.ds(expert, 1)], target_ref, sems, 0)
    for copy in copies:
        copy.start()
    token_ref[...] = jnp.zeros_like(token_ref)
    for copy in copies:
        copy.wait()


def weight_copies(source_ref, target_ref, sems, expert):
    parts = sems.shape[1]
    depth = source_ref.shape[1] // parts
    return [
        pltpu.make_async_copy(
            source_ref.at[expert, pl.ds(p * depth, depth)],
            target_ref.at[expert, pl.ds(p * depth, depth)],
            sems.at[expert, p],
        )
        for p in range(parts)
    ]


def fetch(weight, expert, after):
    in_hbm = pl.BlockSpec(memory_space=pl.ANY)
    in_vmem = pl.BlockSpec(memory_space=pltpu.VMEM)
    return pl.pallas_call(
        functools.partial(fetch_kernel, expert),
        out_shape=(
            pltpu.VMEM((1, *weight.shape[1:]), weight.dtype),
            jax.ShapeDtypeStruct((8, 128), jnp.float32),
        ),
        in_specs=[in_hbm, in_hbm],
        out_specs=(in_vmem, in_vmem),
        scratch_shapes=[pltpu.SemaphoreType.DMA((1, 8))],
        compiler_params=pltpu.CompilerParams(vmem_limit_bytes=VMEM_LIMIT),
        cost_estimate=pl.CostEstimate(
            flops=0, bytes_accessed=2 * weight.size // weight.shape[0], transcendentals=0
        ),
        name="fetch",
    )(after, pltpu.with_memory_space_constraint(weight, pltpu.HBM))


def in_vmem(values):
    return [pltpu.with_memory_space_constraint(v, pltpu.VMEM) for v in values]


def expert_call(entries, held, w_down, token):
    experts, hidden, width = w_down.shape
    full = entries[0].shape[1]
    rows = sum(e.shape[0] for e in entries)
    blocks = width // hidden
    whole = pl.BlockSpec(memory_space=pltpu.VMEM)
    anywhere = pl.BlockSpec(memory_space=pl.ANY)
    columns = (blocks // 2 * hidden, (blocks - blocks // 2) * hidden)
    outs = [jax.ShapeDtypeStruct((rows // 2, c), jnp.bfloat16) for c in columns]
    hiddens, keep, send, *down = pl.pallas_call(
        functools.partial(expert_kernel, len(entries), experts, width),
        out_shape=(
            jax.ShapeDtypeStruct((rows, experts * hidden), jnp.bfloat16),
            outs[0],
            outs[0],
            *(pltpu.VMEM(w.shape, w.dtype) for w in held[:experts]),
        ),
        in_specs=[anywhere] + [whole] * (len(entries) + len(held)) + [anywhere],
        out_specs=(whole,) * (3 + experts),
        input_output_aliases={1 + len(entries) + e: 3 + e for e in range(experts)},
        scratch_shapes=[
            pltpu.VMEM((rows, full), jnp.bfloat16),
            pltpu.VMEM((experts, rows, hidden), jnp.float32),
            pltpu.SemaphoreType.DMA((experts, blocks)),
        ],
        compiler_params=pltpu.CompilerParams(vmem_limit_bytes=VMEM_LIMIT),
        cost_estimate=pl.CostEstimate(
            flops=5 * rows * w_down.size,
            bytes_accessed=2 * w_down.size,
            transcendentals=rows * experts * hidden,
        ),
        name="experts",
    )(
        token,
        *entries,
        *in_vmem(held),
        pltpu.with_memory_space_constraint(w_down, pltpu.HBM),
    )
    later = pl.pallas_call(
        functools.partial(down_kernel, blocks // 2),
        out_shape=(outs[1], outs[1]),
        in_specs=[whole] * (1 + experts),
        out_specs=(whole, whole),
        compiler_params=pltpu.CompilerParams(vmem_limit_bytes=VMEM_LIMIT),
        cost_estimate=pl.CostEstimate(
            flops=rows * w_down.size,
            bytes_accessed=2 * rows * columns[1],
            transcendentals=0,
        ),
        name="down",
    )(hiddens, *in_vmem(down))
    return (keep, send), later


def add(*values):
    total = values[0].astype(jnp.float32)
    for value in values[1:]:
        total = total + value.astype(jnp.float32)
    return total.astype(jnp.bfloat16)


def body(tokens, expert_ids, gate_weights, w_gate, w_up, w_down):
    sects, groups, lanes = (lax.axis_size(a) for a in AXES)
    row_count, width = tokens.shape
    experts = w_gate.shape[0]
    expert_count = sects * groups * experts

    half = -(-expert_count // 64) * 64
    block = extend(tokens, expert_ids, gate_weights, half)
    entries, held, token = gather_rows(block, w_up, w_gate)

    results = []
    halves = []
    for keep, send in expert_call(entries, held, w_down, token):
        value = add(keep, swap_core(send))
        for masks in rounds_of()[::-1]:
            middle = value.shape[0] // 2
            value = add(value[:middle], swap(value[middle:], masks))
        halves.append(value)
    value = jnp.concatenate(halves, axis=1)
    own = [value[m * row_count:(m + 1) * row_count] for m in range(lanes)]
    return add(own[0], *(swap_line(own[m], m) for m in range(1, lanes)))


def solution(mesh):
    in_specs = (
        P(AXES, None),
        P(AXES, None),
        P(AXES, None),
        P(("sect", "grp"), None, "dev"),
        P(("sect", "grp"), None, "dev"),
        P(("sect", "grp"), "dev", None),
    )
    return jax.shard_map(
        body, mesh=mesh, in_specs=in_specs, out_specs=P(AXES, None), check_vma=False
    )
```

```python
import functools

import jax
import jax.numpy as jnp
from jax import lax
from jax.experimental import pallas as pl
from jax.experimental.pallas import tpu as pltpu
from jax.sharding import PartitionSpec as P

AXES = ("sect", "grp", "dev")
VMEM_LIMIT = 16 * 2**20


def rounds_of():
    sects, groups, _ = (lax.axis_size(a) for a in AXES)
    bits = [1 << b for b in range(groups.bit_length() - 1)]
    orders = [bits[::-1], bits]
    return list(zip(*(orders[s % 2] for s in range(sects))))


def swap(value, masks):
    count = lax.axis_size("grp")
    pairs = [
        (s * count + i, s * count + (i ^ mask)) for s, mask in enumerate(masks) for i in range(count)
    ]
    return lax.ppermute(value, ("sect", "grp"), pairs)


def line_masks():
    sects, _, lanes = (lax.axis_size(a) for a in AXES)
    near = list(range(1, lanes))
    orders = [near[-1:] + near[:-1], near]
    return list(zip(*(orders[s % 2] for s in range(sects))))


def swap_line(value, masks):
    lanes = lax.axis_size("dev")
    pairs = [
        (s * lanes + i, s * lanes + (i ^ mask)) for s, mask in enumerate(masks) for i in range(lanes)
    ]
    return lax.ppermute(value, ("sect", "dev"), pairs)


def swap_core(value):
    return lax.ppermute(value, "sect", [(0, 1), (1, 0)])


def vmem_call(kernel, out_shape, name, *operands):
    whole = pl.BlockSpec(memory_space=pltpu.VMEM)
    return pl.pallas_call(
        kernel,
        out_shape=out_shape,
        in_specs=[whole] * len(operands),
        out_specs=jax.tree.map(lambda _: whole, out_shape),
        compiler_params=pltpu.CompilerParams(vmem_limit_bytes=VMEM_LIMIT),
        name=name,
    )(*operands)


def extend_kernel(tokens_hbm, ids_hbm, weights_hbm, out_ref, tokens_ref, ids_ref, weights_ref, sems):
    pairs = ((ids_hbm, ids_ref), (weights_hbm, weights_ref), (tokens_hbm, tokens_ref))
    copies = [pltpu.make_async_copy(a, b, sems.at[i]) for i, (a, b) in enumerate(pairs)]
    for copy in copies:
        copy.start()
    rows, width = tokens_ref.shape
    half = (out_ref.shape[1] - width) // 2
    lane = lax.broadcasted_iota(jnp.int32, (rows, half * 2), 1)
    dense = jnp.zeros((rows, half * 2), jnp.float32)
    for copy in copies:
        copy.wait()
    for k in range(ids_ref.shape[1]):
        mine = lax.rem(lane, half) == ids_ref[:, k:k + 1]
        dense = dense + jnp.where(mine, weights_ref[:, k:k + 1], 0.0)
    high = dense.astype(jnp.bfloat16).astype(jnp.float32)
    out_ref[:, :width] = tokens_ref[...]
    out_ref[:, width:] = jnp.where(lane < half, high, dense - high).astype(jnp.bfloat16)


def extend(tokens, ids, weights, half):
    rows, width = tokens.shape
    return pl.pallas_call(
        extend_kernel,
        out_shape=jax.ShapeDtypeStruct((rows, width + 2 * half), tokens.dtype),
        in_specs=[pl.BlockSpec(memory_space=pl.ANY)] * 3,
        out_specs=pl.BlockSpec(memory_space=pltpu.VMEM),
        scratch_shapes=[pltpu.VMEM(v.shape, v.dtype) for v in (tokens, ids, weights)]
        + [pltpu.SemaphoreType.DMA((3,))],
        compiler_params=pltpu.CompilerParams(vmem_limit_bytes=VMEM_LIMIT),
        name="extend",
    )(*(pltpu.with_memory_space_constraint(v, pltpu.HBM) for v in (tokens, ids, weights)))


def stack_kernel(*refs):
    pieces, out_ref = refs[:-1], refs[-1]
    values = [p[...].astype(jnp.float32) for p in pieces]
    out_ref[...] = jnp.concatenate(values, axis=0).astype(out_ref.dtype)


def stack(*pieces):
    rows = sum(p.shape[0] for p in pieces)
    out = jax.ShapeDtypeStruct((rows, pieces[0].shape[1]), pieces[0].dtype)
    return vmem_call(stack_kernel, out, "stack", *pieces)


def gather_rows(block, w_up, w_gate):
    wanted = [(w, e) for w in (w_gate, w_up) for e in range(w.shape[0])]
    weights, token = [], block

    def meanwhile(arrived, token):
        if wanted:
            weight, token = fetch(*wanted.pop(0), token)
            weights.append(weight)
            arrived, token = lax.optimization_barrier((arrived, token))
        return arrived, token

    arrived = [swap_line(block, masks) for masks in line_masks()]
    arrived, token = meanwhile(arrived, token)
    line = stack(block, *arrived)
    rounds = rounds_of()
    for masks in rounds[:-1]:
        arrived, token = meanwhile(swap(line, masks), token)
        line = stack(line, arrived)
    last = swap(line, rounds[-1])
    mine, token = meanwhile(line, token)
    other = swap_core(mine)
    while wanted:
        weight, token = fetch(*wanted.pop(0), token)
        weights.append(weight)
    last, other, token = lax.optimization_barrier((last, other, token))
    return [line, last, other, swap_core(last)], weights, token


def down_copy(expert, block, at, down_hbm, target_ref, sems):
    hidden = down_hbm.shape[1]
    return pltpu.make_async_copy(
        down_hbm.at[expert, :, pl.ds(block * hidden, hidden)],
        target_ref.at[pl.ds(at * hidden, hidden)],
        sems.at[expert, block],
    )


def down_block(at, hidden_ref, down_refs, keep_ref, send_ref):
    hidden = down_refs[0].shape[1]
    middle = keep_ref.shape[0]
    weight = jnp.concatenate([ref[pl.ds(at * hidden, hidden), :] for ref in down_refs], axis=0)
    total = jnp.dot(hidden_ref[...], weight, preferred_element_type=jnp.float32)
    total = total.astype(jnp.bfloat16)
    span = pl.ds(at * hidden, hidden)
    keep_ref[:, span] = total[:middle]
    send_ref[:, span] = total[middle:]


def expert_kernel(entry_count, experts, width, token_ref, *refs):
    pieces, refs = refs[:entry_count], refs[entry_count:]
    gate_refs, up_refs, refs = refs[:experts], refs[experts:2 * experts], refs[2 * experts:]
    down_hbm, hidden_ref, keep_ref, send_ref = refs[:4]
    down_refs, (rows_ref, value_ref, early_ref, sems) = refs[4:4 + experts], refs[4 + experts:]
    hidden = gate_refs[0].shape[2]
    place = lax.axis_index("sect") * lax.axis_size("grp") + lax.axis_index("grp")
    first = place * experts
    block = min(256, hidden)
    blocks = width // hidden

    early = [
        down_copy(e, step, step, down_hbm, early_ref.at[e], sems)
        for step in range(blocks // 2)
        for e in range(experts)
    ]
    late = [
        [
            down_copy(e, step, step - blocks // 2, down_hbm, down_refs[e].at[0], sems)
            for step in range(blocks // 2, blocks)
        ]
        for e in range(experts)
    ]
    for copy in early:
        copy.start()

    at = 0
    for piece in pieces:
        rows_ref[pl.ds(at, piece.shape[0])] = piece[...]
        at += piece.shape[0]

    for e in range(experts):
        for step in range(hidden // block):
            span = pl.ds(step * block, block)
            gate = jnp.dot(
                rows_ref[:, :width], gate_refs[e][0, :, span], preferred_element_type=jnp.float32
            )
            value_ref[e, :, span] = gate / (1.0 + jnp.exp(-gate))
        for copy in late[e]:
            copy.start()

    extra = rows_ref[:, width:].astype(jnp.float32)
    lane = lax.broadcasted_iota(jnp.int32, extra.shape, 1)
    for e in range(experts):
        mine = lax.rem(lane, extra.shape[1] // 2) == first + e
        scale = jnp.sum(jnp.where(mine, extra, 0.0), axis=1, keepdims=True)
        for step in range(hidden // block):
            span = pl.ds(step * block, block)
            up = jnp.dot(
                rows_ref[:, :width], up_refs[e][0, :, span], preferred_element_type=jnp.float32
            )
            value = value_ref[e, :, span] * up * scale
            hidden_ref[:, pl.ds(e * hidden + step * block, block)] = value.astype(jnp.bfloat16)

    for step in range(blocks // 2):
        for copy in early[step * experts:(step + 1) * experts]:
            copy.wait()
        down_block(step, hidden_ref, [early_ref.at[e] for e in range(experts)], keep_ref, send_ref)

    for copies in late:
        for copy in copies:
            copy.wait()


def down_kernel(hidden_ref, *refs):
    *down_refs, keep_ref, send_ref = refs
    for step in range(keep_ref.shape[1] // down_refs[0].shape[2]):
        down_block(step, hidden_ref, [ref.at[0] for ref in down_refs], keep_ref, send_ref)


def fetch_kernel(expert, after_ref, source_ref, target_ref, token_ref, sems):
    copies = weight_copies(source_ref.at[pl.ds(expert, 1)], target_ref, sems, 0)
    for copy in copies:
        copy.start()
    token_ref[...] = jnp.zeros_like(token_ref)
    for copy in copies:
        copy.wait()


def weight_copies(source_ref, target_ref, sems, expert):
    parts = sems.shape[1]
    depth = source_ref.shape[1] // parts
    return [
        pltpu.make_async_copy(
            source_ref.at[expert, pl.ds(p * depth, depth)],
            target_ref.at[expert, pl.ds(p * depth, depth)],
            sems.at[expert, p],
        )
        for p in range(parts)
    ]


def fetch(weight, expert, after):
    in_hbm = pl.BlockSpec(memory_space=pl.ANY)
    in_vmem = pl.BlockSpec(memory_space=pltpu.VMEM)
    return pl.pallas_call(
        functools.partial(fetch_kernel, expert),
        out_shape=(
            pltpu.VMEM((1, *weight.shape[1:]), weight.dtype),
            jax.ShapeDtypeStruct((8, 128), jnp.float32),
        ),
        in_specs=[in_hbm, in_hbm],
        out_specs=(in_vmem, in_vmem),
        scratch_shapes=[pltpu.SemaphoreType.DMA((1, 8))],
        compiler_params=pltpu.CompilerParams(vmem_limit_bytes=VMEM_LIMIT),
        cost_estimate=pl.CostEstimate(
            flops=0, bytes_accessed=2 * weight.size // weight.shape[0], transcendentals=0
        ),
        name="fetch",
    )(after, pltpu.with_memory_space_constraint(weight, pltpu.HBM))


def in_vmem(values):
    return [pltpu.with_memory_space_constraint(v, pltpu.VMEM) for v in values]


def expert_call(entries, held, w_down, token):
    experts, hidden, width = w_down.shape
    full = entries[0].shape[1]
    rows = sum(e.shape[0] for e in entries)
    blocks = width // hidden
    whole = pl.BlockSpec(memory_space=pltpu.VMEM)
    anywhere = pl.BlockSpec(memory_space=pl.ANY)
    columns = (blocks // 2 * hidden, (blocks - blocks // 2) * hidden)
    outs = [jax.ShapeDtypeStruct((rows // 2, c), jnp.bfloat16) for c in columns]
    hiddens, keep, send, *down = pl.pallas_call(
        functools.partial(expert_kernel, len(entries), experts, width),
        out_shape=(
            jax.ShapeDtypeStruct((rows, experts * hidden), jnp.bfloat16),
            outs[0],
            outs[0],
            *(pltpu.VMEM(w.shape, w.dtype) for w in held[:experts]),
        ),
        in_specs=[anywhere] + [whole] * (len(entries) + len(held)) + [anywhere],
        out_specs=(whole,) * (3 + experts),
        input_output_aliases={1 + len(entries) + e: 3 + e for e in range(experts)},
        scratch_shapes=[
            pltpu.VMEM((rows, full), jnp.bfloat16),
            pltpu.VMEM((experts, rows, hidden), jnp.float32),
            pltpu.VMEM((experts, columns[0], hidden), w_down.dtype),
            pltpu.SemaphoreType.DMA((experts, blocks)),
        ],
        compiler_params=pltpu.CompilerParams(vmem_limit_bytes=VMEM_LIMIT),
        cost_estimate=pl.CostEstimate(
            flops=5 * rows * w_down.size,
            bytes_accessed=2 * w_down.size,
            transcendentals=rows * experts * hidden,
        ),
        name="experts",
    )(
        token,
        *entries,
        *in_vmem(held),
        pltpu.with_memory_space_constraint(w_down, pltpu.HBM),
    )
    later = pl.pallas_call(
        down_kernel,
        out_shape=(outs[1], outs[1]),
        in_specs=[whole] * (1 + experts),
        out_specs=(whole, whole),
        compiler_params=pltpu.CompilerParams(vmem_limit_bytes=VMEM_LIMIT),
        cost_estimate=pl.CostEstimate(
            flops=rows * w_down.size,
            bytes_accessed=2 * rows * columns[1],
            transcendentals=0,
        ),
        name="down",
    )(hiddens, *in_vmem(down))
    return (keep, send), later


def add(*values):
    total = values[0].astype(jnp.float32)
    for value in values[1:]:
        total = total + value.astype(jnp.float32)
    return total.astype(jnp.bfloat16)


def body(tokens, expert_ids, gate_weights, w_gate, w_up, w_down):
    sects, groups, lanes = (lax.axis_size(a) for a in AXES)
    row_count, width = tokens.shape
    experts = w_gate.shape[0]
    expert_count = sects * groups * experts

    half = -(-expert_count // 64) * 64
    block = extend(tokens, expert_ids, gate_weights, half)
    entries, held, token = gather_rows(block, w_up, w_gate)

    results = []
    halves = []
    for keep, send in expert_call(entries, held, w_down, token):
        value = add(keep, swap_core(send))
        for masks in rounds_of()[::-1]:
            middle = value.shape[0] // 2
            value = add(value[:middle], swap(value[middle:], masks))
        halves.append(value)
    value = jnp.concatenate(halves, axis=1)
    own = [value[m * row_count:(m + 1) * row_count] for m in range(lanes)]
    return add(own[0], *(swap_line(o, masks) for o, masks in zip(own[1:], line_masks())))


def solution(mesh):
    in_specs = (
        P(AXES, None),
        P(AXES, None),
        P(AXES, None),
        P(("sect", "grp"), None, "dev"),
        P(("sect", "grp"), None, "dev"),
        P(("sect", "grp"), "dev", None),
    )
    return jax.shard_map(
        body, mesh=mesh, in_specs=in_specs, out_specs=P(AXES, None), check_vma=False
    )
```

```python
import functools

import jax
import jax.numpy as jnp
from jax import lax
from jax.experimental import pallas as pl
from jax.experimental.pallas import tpu as pltpu
from jax.sharding import PartitionSpec as P

AXES = ("sect", "grp", "dev")
VMEM_LIMIT = 10 * 2**20


def rounds_of():
    sects, groups, _ = (lax.axis_size(a) for a in AXES)
    bits = [1 << b for b in range(groups.bit_length() - 1)]
    orders = [bits[::-1], bits]
    return list(zip(*(orders[s % 2] for s in range(sects))))


def swap(value, masks):
    count = lax.axis_size("grp")
    pairs = [
        (s * count + i, s * count + (i ^ mask)) for s, mask in enumerate(masks) for i in range(count)
    ]
    return lax.ppermute(value, ("sect", "grp"), pairs)


def line_orders():
    lanes = lax.axis_size("dev")
    near = list(range(1, lanes))
    orders = [[0] + near[-1:] + near[:-1], [0] + near]
    return [orders[s % 2] for s in range(lax.axis_size("sect"))]


def swap_line(value, masks):
    lanes = lax.axis_size("dev")
    pairs = [
        (s * lanes + i, s * lanes + (i ^ mask)) for s, mask in enumerate(masks) for i in range(lanes)
    ]
    return lax.ppermute(value, ("sect", "dev"), pairs)


def swap_core(value):
    return lax.ppermute(value, "sect", [(0, 1), (1, 0)])


def vmem_call(kernel, out_shape, name, *operands):
    whole = pl.BlockSpec(memory_space=pltpu.VMEM)
    return pl.pallas_call(
        kernel,
        out_shape=out_shape,
        in_specs=[whole] * len(operands),
        out_specs=jax.tree.map(lambda _: whole, out_shape),
        compiler_params=pltpu.CompilerParams(vmem_limit_bytes=VMEM_LIMIT),
        name=name,
    )(*operands)


def extend_kernel(tokens_hbm, ids_hbm, weights_hbm, out_ref, tokens_ref, ids_ref, weights_ref, sems):
    pairs = ((ids_hbm, ids_ref), (weights_hbm, weights_ref), (tokens_hbm, tokens_ref))
    copies = [pltpu.make_async_copy(a, b, sems.at[i]) for i, (a, b) in enumerate(pairs)]
    for copy in copies:
        copy.start()
    rows, width = tokens_ref.shape
    half = (out_ref.shape[1] - width) // 2
    lane = lax.broadcasted_iota(jnp.int32, (rows, half * 2), 1)
    dense = jnp.zeros((rows, half * 2), jnp.float32)
    for copy in copies:
        copy.wait()
    for k in range(ids_ref.shape[1]):
        mine = lax.rem(lane, half) == ids_ref[:, k:k + 1]
        dense = dense + jnp.where(mine, weights_ref[:, k:k + 1], 0.0)
    high = dense.astype(jnp.bfloat16).astype(jnp.float32)
    out_ref[:, :width] = tokens_ref[...]
    out_ref[:, width:] = jnp.where(lane < half, high, dense - high).astype(jnp.bfloat16)


def extend(tokens, ids, weights, half):
    rows, width = tokens.shape
    return pl.pallas_call(
        extend_kernel,
        out_shape=jax.ShapeDtypeStruct((rows, width + 2 * half), tokens.dtype),
        in_specs=[pl.BlockSpec(memory_space=pl.ANY)] * 3,
        out_specs=pl.BlockSpec(memory_space=pltpu.VMEM),
        scratch_shapes=[pltpu.VMEM(v.shape, v.dtype) for v in (tokens, ids, weights)]
        + [pltpu.SemaphoreType.DMA((3,))],
        compiler_params=pltpu.CompilerParams(vmem_limit_bytes=VMEM_LIMIT),
        name="extend",
    )(*(pltpu.with_memory_space_constraint(v, pltpu.HBM) for v in (tokens, ids, weights)))


def stack_kernel(orders, *refs):
    pieces, out_ref = refs[:-1], refs[-1]
    for core, order in enumerate(orders):

        @pl.when(lax.axis_index("sect") == core)
        def _():
            values = [pieces[i][...].astype(jnp.float32) for i in order]
            out_ref[...] = jnp.concatenate(values, axis=0).astype(out_ref.dtype)


def stack(pieces, orders=None):
    rows = sum(p.shape[0] for p in pieces)
    out = jax.ShapeDtypeStruct((rows, pieces[0].shape[1]), pieces[0].dtype)
    if orders is None:
        orders = [range(len(pieces))] * lax.axis_size("sect")
    return vmem_call(functools.partial(stack_kernel, orders), out, "stack", *pieces)


def gather_rows(block, w_gate, w_up, w_down):
    experts, sects, lanes = w_gate.shape[0], lax.axis_size("sect"), lax.axis_size("dev")
    early = early_columns(w_down)
    gates, ups, downs = ([(w, e, w.shape[2]) for e in range(experts)] for w in (w_gate, w_up, w_down))
    downs = [(w, e, early) for w, e, _ in downs]
    held, token = {}, block

    def fetch_next(wanted, token):
        weight, expert, columns = wanted.pop(0)
        held[id(weight), expert], token = fetch(weight, expert, columns, token)
        return token

    arrived = [swap_line(block, (m,) * sects) for m in range(1, lanes)]
    token = fetch_next(gates, token)
    arrived, token = lax.optimization_barrier((arrived, token))
    line = stack([block, *arrived], line_orders())
    rounds = rounds_of()
    for number, masks in enumerate(rounds[:-1]):
        arrived = swap(line, masks)
        if gates:
            token = fetch_next(gates, token)
            if len(downs) > 1:
                token = fetch_next(downs, token)
        arrived, token = lax.optimization_barrier((arrived, token))
        line = stack([line, arrived])
    last = swap(line, rounds[-1])
    token = fetch_next(gates if gates else ups, token)
    mine, token = lax.optimization_barrier((line, token))
    other = swap_core(mine)
    while gates or ups:
        token = fetch_next(gates if gates else ups, token)
    last, other, token = lax.optimization_barrier((last, other, token))
    last_other = swap_core(last)
    while downs:
        token = fetch_next(downs, token)
    last_other, token = lax.optimization_barrier((last_other, token))
    weights = [held[id(w), e] for w in (w_gate, w_up, w_down) for e in range(experts)]
    return [line, last, other, last_other], weights, token


def early_columns(w_down):
    _, hidden, width = w_down.shape
    return width // hidden // 2 * hidden


def down_copy(expert, block, at, down_hbm, target_ref, sems):
    hidden = down_hbm.shape[1]
    return pltpu.make_async_copy(
        down_hbm.at[expert, :, pl.ds(block * hidden, hidden)],
        target_ref.at[pl.ds(at * hidden, hidden)],
        sems.at[expert, block],
    )


def down_block(at, hidden_ref, weights, keep_ref, send_ref):
    hidden = weights[0].shape[1]
    middle = keep_ref.shape[0]
    weight = jnp.concatenate(weights, axis=0)
    total = jnp.dot(hidden_ref[...], weight, preferred_element_type=jnp.float32)
    total = total.astype(jnp.bfloat16)
    span = pl.ds(at * hidden, hidden)
    keep_ref[:, span] = total[:middle]
    send_ref[:, span] = total[middle:]


def expert_kernel(entry_count, experts, width, token_ref, *refs):
    pieces, refs = refs[:entry_count], refs[entry_count:]
    gate_refs, up_refs, early_refs, refs = (
        refs[:experts], refs[experts:2 * experts], refs[2 * experts:3 * experts], refs[3 * experts:]
    )
    down_hbm, hidden_ref, keep_ref, send_ref = refs[:4]
    down_refs, (rows_ref, value_ref, sems) = refs[4:4 + experts], refs[4 + experts:]
    hidden = gate_refs[0].shape[2]
    place = lax.axis_index("sect") * lax.axis_size("grp") + lax.axis_index("grp")
    first = place * experts
    block = min(256, hidden)
    blocks = width // hidden

    late = [
        [
            down_copy(e, step, step - blocks // 2, down_hbm, down_refs[e].at[0], sems)
            for step in range(blocks // 2, blocks)
        ]
        for e in range(experts)
    ]

    at = 0
    for piece in pieces:
        rows_ref[pl.ds(at, piece.shape[0])] = piece[...]
        at += piece.shape[0]

    for e in range(experts):
        for step in range(hidden // block):
            span = pl.ds(step * block, block)
            gate = jnp.dot(
                rows_ref[:, :width], gate_refs[e][0, :, span], preferred_element_type=jnp.float32
            )
            value_ref[e, :, span] = gate / (1.0 + jnp.exp(-gate))
        for copy in late[e]:
            copy.start()

    extra = rows_ref[:, width:].astype(jnp.float32)
    lane = lax.broadcasted_iota(jnp.int32, extra.shape, 1)
    for e in range(experts):
        mine = lax.rem(lane, extra.shape[1] // 2) == first + e
        scale = jnp.sum(jnp.where(mine, extra, 0.0), axis=1, keepdims=True)
        for step in range(hidden // block):
            span = pl.ds(step * block, block)
            up = jnp.dot(
                rows_ref[:, :width], up_refs[e][0, :, span], preferred_element_type=jnp.float32
            )
            value = value_ref[e, :, span] * up * scale
            hidden_ref[:, pl.ds(e * hidden + step * block, block)] = value.astype(jnp.bfloat16)

    for step in range(blocks // 2):
        span = pl.ds(step * hidden, hidden)
        down_block(step, hidden_ref, [ref[0, :, span] for ref in early_refs], keep_ref, send_ref)

    for copies in late:
        for copy in copies:
            copy.wait()


def down_kernel(hidden_ref, *refs):
    *down_refs, keep_ref, send_ref = refs
    hidden = down_refs[0].shape[2]
    for step in range(keep_ref.shape[1] // hidden):
        span = pl.ds(step * hidden, hidden)
        down_block(step, hidden_ref, [ref[0, span, :] for ref in down_refs], keep_ref, send_ref)


def fetch_kernel(expert, after_ref, source_ref, target_ref, token_ref, sems):
    columns = pl.ds(0, target_ref.shape[2])
    copies = weight_copies(source_ref.at[pl.ds(expert, 1), :, columns], target_ref, sems, 0)
    for copy in copies:
        copy.start()
    token_ref[...] = jnp.zeros_like(token_ref)
    for copy in copies:
        copy.wait()


def weight_copies(source_ref, target_ref, sems, expert):
    parts = sems.shape[1]
    depth = source_ref.shape[1] // parts
    return [
        pltpu.make_async_copy(
            source_ref.at[expert, pl.ds(p * depth, depth)],
            target_ref.at[expert, pl.ds(p * depth, depth)],
            sems.at[expert, p],
        )
        for p in range(parts)
    ]


def fetch(weight, expert, columns, after):
    in_hbm = pl.BlockSpec(memory_space=pl.ANY)
    in_vmem = pl.BlockSpec(memory_space=pltpu.VMEM)
    return pl.pallas_call(
        functools.partial(fetch_kernel, expert),
        out_shape=(
            pltpu.VMEM((1, weight.shape[1], columns), weight.dtype),
            jax.ShapeDtypeStruct((8, 128), jnp.float32),
        ),
        in_specs=[in_hbm, in_hbm],
        out_specs=(in_vmem, in_vmem),
        scratch_shapes=[pltpu.SemaphoreType.DMA((1, 8))],
        compiler_params=pltpu.CompilerParams(vmem_limit_bytes=VMEM_LIMIT),
        cost_estimate=pl.CostEstimate(
            flops=0, bytes_accessed=2 * weight.shape[1] * columns, transcendentals=0
        ),
        name="fetch",
    )(after, pltpu.with_memory_space_constraint(weight, pltpu.HBM))


def in_vmem(values):
    return [pltpu.with_memory_space_constraint(v, pltpu.VMEM) for v in values]


def expert_call(entries, held, w_down, token):
    experts, hidden, width = w_down.shape
    full = entries[0].shape[1]
    rows = sum(e.shape[0] for e in entries)
    blocks = width // hidden
    whole = pl.BlockSpec(memory_space=pltpu.VMEM)
    anywhere = pl.BlockSpec(memory_space=pl.ANY)
    columns = (early_columns(w_down), width - early_columns(w_down))
    outs = [jax.ShapeDtypeStruct((rows // 2, c), jnp.bfloat16) for c in columns]
    hiddens, keep, send, *down = pl.pallas_call(
        functools.partial(expert_kernel, len(entries), experts, width),
        out_shape=(
            jax.ShapeDtypeStruct((rows, experts * hidden), jnp.bfloat16),
            outs[0],
            outs[0],
            *(pltpu.VMEM(w.shape, w.dtype) for w in held[:experts]),
        ),
        in_specs=[anywhere] + [whole] * (len(entries) + len(held)) + [anywhere],
        out_specs=(whole,) * (3 + experts),
        input_output_aliases={1 + len(entries) + e: 3 + e for e in range(experts)},
        scratch_shapes=[
            pltpu.VMEM((rows, full), jnp.bfloat16),
            pltpu.VMEM((experts, rows, hidden), jnp.float32),
            pltpu.SemaphoreType.DMA((experts, blocks)),
        ],
        compiler_params=pltpu.CompilerParams(vmem_limit_bytes=VMEM_LIMIT),
        cost_estimate=pl.CostEstimate(
            flops=5 * rows * w_down.size,
            bytes_accessed=2 * w_down.size,
            transcendentals=rows * experts * hidden,
        ),
        name="experts",
    )(
        token,
        *entries,
        *in_vmem(held),
        pltpu.with_memory_space_constraint(w_down, pltpu.HBM),
    )
    later = pl.pallas_call(
        down_kernel,
        out_shape=(outs[1], outs[1]),
        in_specs=[whole] * (1 + experts),
        out_specs=(whole, whole),
        compiler_params=pltpu.CompilerParams(vmem_limit_bytes=VMEM_LIMIT),
        cost_estimate=pl.CostEstimate(
            flops=rows * w_down.size,
            bytes_accessed=2 * rows * columns[1],
            transcendentals=0,
        ),
        name="down",
    )(hiddens, *in_vmem(down))
    return (keep, send), later


def add(*values):
    total = values[0].astype(jnp.float32)
    for value in values[1:]:
        total = total + value.astype(jnp.float32)
    return total.astype(jnp.bfloat16)


def body(tokens, expert_ids, gate_weights, w_gate, w_up, w_down):
    sects, groups, lanes = (lax.axis_size(a) for a in AXES)
    row_count, width = tokens.shape
    experts = w_gate.shape[0]
    expert_count = sects * groups * experts

    half = -(-expert_count // 64) * 64
    block = extend(tokens, expert_ids, gate_weights, half)
    entries, held, token = gather_rows(block, w_gate, w_up, w_down)

    results = []
    halves = []
    for keep, send in expert_call(entries, held, w_down, token):
        value = add(keep, swap_core(send))
        for masks in rounds_of()[::-1]:
            middle = value.shape[0] // 2
            value = add(value[:middle], swap(value[middle:], masks))
        halves.append(value)
    value = jnp.concatenate(halves, axis=1)
    own = [value[m * row_count:(m + 1) * row_count] for m in range(lanes)]
    masks = list(zip(*line_orders()))
    return add(own[0], *(swap_line(own[i], masks[i]) for i in range(1, lanes)))


def solution(mesh):
    in_specs = (
        P(AXES, None),
        P(AXES, None),
        P(AXES, None),
        P(("sect", "grp"), None, "dev"),
        P(("sect", "grp"), None, "dev"),
        P(("sect", "grp"), "dev", None),
    )
    return jax.shard_map(
        body, mesh=mesh, in_specs=in_specs, out_specs=P(AXES, None), check_vma=False
    )
```

```python
import functools

import jax
import jax.numpy as jnp
from jax import lax
from jax.experimental import pallas as pl
from jax.experimental.pallas import tpu as pltpu
from jax.sharding import PartitionSpec as P

AXES = ("sect", "grp", "dev")
VMEM_LIMIT = 10 * 2**20


def rounds_of():
    sects, groups, _ = (lax.axis_size(a) for a in AXES)
    bits = [1 << b for b in range(groups.bit_length() - 1)]
    orders = [bits[::-1], bits]
    return list(zip(*(orders[s % 2] for s in range(sects))))


def swap(value, masks):
    count = lax.axis_size("grp")
    pairs = [
        (s * count + i, s * count + (i ^ mask)) for s, mask in enumerate(masks) for i in range(count)
    ]
    return lax.ppermute(value, ("sect", "grp"), pairs)


def line_orders():
    lanes = lax.axis_size("dev")
    near = list(range(1, lanes))
    orders = [[0] + near[-1:] + near[:-1], [0] + near]
    return [orders[s % 2] for s in range(lax.axis_size("sect"))]


def swap_line(value, masks):
    lanes = lax.axis_size("dev")
    pairs = [
        (s * lanes + i, s * lanes + (i ^ mask)) for s, mask in enumerate(masks) for i in range(lanes)
    ]
    return lax.ppermute(value, ("sect", "dev"), pairs)


def swap_core(value):
    return lax.ppermute(value, "sect", [(0, 1), (1, 0)])


def vmem_call(kernel, out_shape, name, *operands):
    whole = pl.BlockSpec(memory_space=pltpu.VMEM)
    return pl.pallas_call(
        kernel,
        out_shape=out_shape,
        in_specs=[whole] * len(operands),
        out_specs=jax.tree.map(lambda _: whole, out_shape),
        compiler_params=pltpu.CompilerParams(vmem_limit_bytes=VMEM_LIMIT),
        name=name,
    )(*operands)


def extend_kernel(tokens_hbm, ids_hbm, weights_hbm, out_ref, tokens_ref, ids_ref, weights_ref, sems):
    pairs = ((ids_hbm, ids_ref), (weights_hbm, weights_ref), (tokens_hbm, tokens_ref))
    copies = [pltpu.make_async_copy(a, b, sems.at[i]) for i, (a, b) in enumerate(pairs)]
    for copy in copies:
        copy.start()
    rows, width = tokens_ref.shape
    half = (out_ref.shape[1] - width) // 2
    lane = lax.broadcasted_iota(jnp.int32, (rows, half * 2), 1)
    dense = jnp.zeros((rows, half * 2), jnp.float32)
    for copy in copies:
        copy.wait()
    for k in range(ids_ref.shape[1]):
        mine = lax.rem(lane, half) == ids_ref[:, k:k + 1]
        dense = dense + jnp.where(mine, weights_ref[:, k:k + 1], 0.0)
    high = dense.astype(jnp.bfloat16).astype(jnp.float32)
    out_ref[:, :width] = tokens_ref[...]
    out_ref[:, width:] = jnp.where(lane < half, high, dense - high).astype(jnp.bfloat16)


def extend(tokens, ids, weights, half):
    rows, width = tokens.shape
    return pl.pallas_call(
        extend_kernel,
        out_shape=jax.ShapeDtypeStruct((rows, width + 2 * half), tokens.dtype),
        in_specs=[pl.BlockSpec(memory_space=pl.ANY)] * 3,
        out_specs=pl.BlockSpec(memory_space=pltpu.VMEM),
        scratch_shapes=[pltpu.VMEM(v.shape, v.dtype) for v in (tokens, ids, weights)]
        + [pltpu.SemaphoreType.DMA((3,))],
        compiler_params=pltpu.CompilerParams(vmem_limit_bytes=VMEM_LIMIT),
        name="extend",
    )(*(pltpu.with_memory_space_constraint(v, pltpu.HBM) for v in (tokens, ids, weights)))


def stack_kernel(orders, *refs):
    pieces, out_ref = refs[:-1], refs[-1]
    for core, order in enumerate(orders):

        @pl.when(lax.axis_index("sect") == core)
        def _():
            values = [pieces[i][...].astype(jnp.float32) for i in order]
            out_ref[...] = jnp.concatenate(values, axis=0).astype(out_ref.dtype)


def stack(pieces, orders=None):
    rows = sum(p.shape[0] for p in pieces)
    out = jax.ShapeDtypeStruct((rows, pieces[0].shape[1]), pieces[0].dtype)
    if orders is None:
        orders = [range(len(pieces))] * lax.axis_size("sect")
    return vmem_call(functools.partial(stack_kernel, orders), out, "stack", *pieces)


def gather_rows(block, w_gate, w_up, w_down):
    experts, sects, lanes = w_gate.shape[0], lax.axis_size("sect"), lax.axis_size("dev")
    half, early = w_down.shape[1] // 2, early_columns(w_down)
    whole = [(w, e, 0, w.shape[1], w.shape[2]) for w in (w_gate, w_up) for e in range(experts)]
    parts = [(w_down, e, r, half, early) for e in range(experts) for r in (0, half)]
    held, token = {}, block

    def fetch_next(wholes, part, token):
        wanted = [whole.pop(0) for _ in range(min(wholes, len(whole)))] + parts[:part]
        del parts[:part]
        if not wanted:
            return token
        *arrays, token = fetch(wanted, token)
        for (weight, expert, row, _, _), array in zip(wanted, arrays):
            held[id(weight), expert, row] = array
        return token

    arrived = [swap_line(block, (m,) * sects) for m in range(1, lanes)]
    token = fetch_next(1, 1, token)
    arrived, token = lax.optimization_barrier((arrived, token))
    line = stack([block, *arrived], line_orders())
    rounds = rounds_of()
    for masks in rounds[:-1]:
        arrived = swap(line, masks)
        token = fetch_next(1, 1, token)
        arrived, token = lax.optimization_barrier((arrived, token))
        line = stack([line, arrived])
    last = swap(line, rounds[-1])
    token = fetch_next(1, 1, token)
    mine, token = lax.optimization_barrier((line, token))
    other = swap_core(mine)
    token = fetch_next(len(whole), 0, token)
    last, other, token = lax.optimization_barrier((last, other, token))
    last_other = swap_core(last)
    token = fetch_next(0, len(parts), token)
    last_other, token = lax.optimization_barrier((last_other, token))
    weights = [held[id(w), e, 0] for w in (w_gate, w_up) for e in range(experts)]
    weights += [held[id(w_down), e, r] for e in range(experts) for r in (0, half)]
    return [line, last, other, last_other], weights, token


def early_columns(w_down):
    _, hidden, width = w_down.shape
    return width // hidden // 2 * hidden


def down_copy(expert, block, at, down_hbm, target_ref, sems):
    hidden = down_hbm.shape[1]
    return pltpu.make_async_copy(
        down_hbm.at[expert, :, pl.ds(block * hidden, hidden)],
        target_ref.at[pl.ds(at * hidden, hidden)],
        sems.at[expert, block],
    )


def down_block(at, hidden_ref, weights, keep_ref, send_ref):
    hidden = weights[0].shape[1]
    middle = keep_ref.shape[0]
    weight = jnp.concatenate(weights, axis=0)
    total = jnp.dot(hidden_ref[...], weight, preferred_element_type=jnp.float32)
    total = total.astype(jnp.bfloat16)
    span = pl.ds(at * hidden, hidden)
    keep_ref[:, span] = total[:middle]
    send_ref[:, span] = total[middle:]


def expert_kernel(entry_count, experts, width, token_ref, *refs):
    pieces, refs = refs[:entry_count], refs[entry_count:]
    gate_refs, up_refs, early_refs, refs = (
        refs[:experts], refs[experts:2 * experts], refs[2 * experts:4 * experts], refs[4 * experts:]
    )
    down_hbm, hidden_ref, keep_ref, send_ref = refs[:4]
    down_refs, (rows_ref, value_ref, sems) = refs[4:4 + experts], refs[4 + experts:]
    hidden = gate_refs[0].shape[2]
    place = lax.axis_index("sect") * lax.axis_size("grp") + lax.axis_index("grp")
    first = place * experts
    block = min(512, hidden)
    blocks = width // hidden

    late = [
        [
            down_copy(e, step, step - blocks // 2, down_hbm, down_refs[e].at[0], sems)
            for step in range(blocks // 2, blocks)
        ]
        for e in range(experts)
    ]

    at = 0
    for piece in pieces:
        rows_ref[pl.ds(at, piece.shape[0])] = piece[...]
        at += piece.shape[0]

    for e in range(experts):
        for step in range(hidden // block):
            span = pl.ds(step * block, block)
            gate = jnp.dot(
                rows_ref[:, :width], gate_refs[e][0, :, span], preferred_element_type=jnp.float32
            )
            value_ref[e, :, span] = gate / (1.0 + jnp.exp(-gate))
        for copy in late[e]:
            copy.start()

    extra = rows_ref[:, width:].astype(jnp.float32)
    lane = lax.broadcasted_iota(jnp.int32, extra.shape, 1)
    for e in range(experts):
        mine = lax.rem(lane, extra.shape[1] // 2) == first + e
        scale = jnp.sum(jnp.where(mine, extra, 0.0), axis=1, keepdims=True)
        for step in range(hidden // block):
            span = pl.ds(step * block, block)
            up = jnp.dot(
                rows_ref[:, :width], up_refs[e][0, :, span], preferred_element_type=jnp.float32
            )
            value = value_ref[e, :, span] * up * scale
            hidden_ref[:, pl.ds(e * hidden + step * block, block)] = value.astype(jnp.bfloat16)

    for step in range(blocks // 2):
        span = pl.ds(step * hidden, hidden)
        down_block(step, hidden_ref, [ref[0, :, span] for ref in early_refs], keep_ref, send_ref)

    for copies in late:
        for copy in copies:
            copy.wait()


def down_kernel(hidden_ref, *refs):
    *down_refs, keep_ref, send_ref = refs
    hidden = down_refs[0].shape[2]
    for step in range(keep_ref.shape[1] // hidden):
        span = pl.ds(step * hidden, hidden)
        down_block(step, hidden_ref, [ref[0, span, :] for ref in down_refs], keep_ref, send_ref)


def fetch_kernel(wanted, after_ref, *refs):
    count = len(wanted)
    sources, targets, (token_ref, sems) = refs[:count], refs[count:2 * count], refs[2 * count:]
    copies = []
    for i, (_, expert, first, rows, columns) in enumerate(wanted):
        depth = rows // sems.shape[1]
        copies += [
            pltpu.make_async_copy(
                sources[i].at[expert, pl.ds(first + p * depth, depth), pl.ds(0, columns)],
                targets[i].at[0, pl.ds(p * depth, depth)],
                sems.at[i, p],
            )
            for p in range(sems.shape[1])
        ]
    for copy in copies:
        copy.start()
    token_ref[...] = jnp.zeros_like(token_ref)
    for copy in copies:
        copy.wait()


def fetch(wanted, after):
    in_hbm = pl.BlockSpec(memory_space=pl.ANY)
    whole = pl.BlockSpec(memory_space=pltpu.VMEM)
    return pl.pallas_call(
        functools.partial(fetch_kernel, [(None, *w[1:]) for w in wanted]),
        out_shape=(
            *(pltpu.VMEM((1, rows, columns), w.dtype) for w, _, _, rows, columns in wanted),
            jax.ShapeDtypeStruct((8, 128), jnp.float32),
        ),
        in_specs=[in_hbm] * (1 + len(wanted)),
        out_specs=(whole,) * (1 + len(wanted)),
        scratch_shapes=[pltpu.SemaphoreType.DMA((len(wanted), 8))],
        compiler_params=pltpu.CompilerParams(vmem_limit_bytes=VMEM_LIMIT),
        cost_estimate=pl.CostEstimate(
            flops=0,
            bytes_accessed=2 * sum(rows * columns for _, _, _, rows, columns in wanted),
            transcendentals=0,
        ),
        name="fetch",
    )(after, *(pltpu.with_memory_space_constraint(w[0], pltpu.HBM) for w in wanted))


def in_vmem(values):
    return [pltpu.with_memory_space_constraint(v, pltpu.VMEM) for v in values]


def expert_call(entries, held, w_down, token):
    experts, hidden, width = w_down.shape
    full = entries[0].shape[1]
    rows = sum(e.shape[0] for e in entries)
    blocks = width // hidden
    whole = pl.BlockSpec(memory_space=pltpu.VMEM)
    anywhere = pl.BlockSpec(memory_space=pl.ANY)
    columns = (early_columns(w_down), width - early_columns(w_down))
    outs = [jax.ShapeDtypeStruct((rows // 2, c), jnp.bfloat16) for c in columns]
    hiddens, keep, send, *down = pl.pallas_call(
        functools.partial(expert_kernel, len(entries), experts, width),
        out_shape=(
            jax.ShapeDtypeStruct((rows, experts * hidden), jnp.bfloat16),
            outs[0],
            outs[0],
            *(pltpu.VMEM(w.shape, w.dtype) for w in held[:experts]),
        ),
        in_specs=[anywhere] + [whole] * (len(entries) + len(held)) + [anywhere],
        out_specs=(whole,) * (3 + experts),
        input_output_aliases={1 + len(entries) + e: 3 + e for e in range(experts)},
        scratch_shapes=[
            pltpu.VMEM((rows, full), jnp.bfloat16),
            pltpu.VMEM((experts, rows, hidden), jnp.float32),
            pltpu.SemaphoreType.DMA((experts, blocks)),
        ],
        compiler_params=pltpu.CompilerParams(vmem_limit_bytes=VMEM_LIMIT),
        cost_estimate=pl.CostEstimate(
            flops=5 * rows * w_down.size,
            bytes_accessed=2 * w_down.size,
            transcendentals=rows * experts * hidden,
        ),
        name="experts",
    )(
        token,
        *entries,
        *in_vmem(held),
        pltpu.with_memory_space_constraint(w_down, pltpu.HBM),
    )
    later = pl.pallas_call(
        down_kernel,
        out_shape=(outs[1], outs[1]),
        in_specs=[whole] * (1 + experts),
        out_specs=(whole, whole),
        compiler_params=pltpu.CompilerParams(vmem_limit_bytes=VMEM_LIMIT),
        cost_estimate=pl.CostEstimate(
            flops=rows * w_down.size,
            bytes_accessed=2 * rows * columns[1],
            transcendentals=0,
        ),
        name="down",
    )(hiddens, *in_vmem(down))
    return (keep, send), later


def add(*values):
    total = values[0].astype(jnp.float32)
    for value in values[1:]:
        total = total + value.astype(jnp.float32)
    return total.astype(jnp.bfloat16)


def body(tokens, expert_ids, gate_weights, w_gate, w_up, w_down):
    sects, groups, lanes = (lax.axis_size(a) for a in AXES)
    row_count, width = tokens.shape
    experts = w_gate.shape[0]
    expert_count = sects * groups * experts

    half = -(-expert_count // 64) * 64
    block = extend(tokens, expert_ids, gate_weights, half)
    entries, held, token = gather_rows(block, w_gate, w_up, w_down)

    results = []
    halves = []
    for keep, send in expert_call(entries, held, w_down, token):
        value = add(keep, swap_core(send))
        for masks in rounds_of()[::-1]:
            middle = value.shape[0] // 2
            value = add(value[:middle], swap(value[middle:], masks))
        halves.append(value)
    value = jnp.concatenate(halves, axis=1)
    own = [value[m * row_count:(m + 1) * row_count] for m in range(lanes)]
    masks = list(zip(*line_orders()))
    return add(own[0], *(swap_line(own[i], masks[i]) for i in range(1, lanes)))


def solution(mesh):
    in_specs = (
        P(AXES, None),
        P(AXES, None),
        P(AXES, None),
        P(("sect", "grp"), None, "dev"),
        P(("sect", "grp"), None, "dev"),
        P(("sect", "grp"), "dev", None),
    )
    return jax.shard_map(
        body, mesh=mesh, in_specs=in_specs, out_specs=P(AXES, None), check_vma=False
    )
```

```python
import functools

import jax
import jax.numpy as jnp
from jax import lax
from jax.experimental import pallas as pl
from jax.experimental.pallas import tpu as pltpu
from jax.sharding import PartitionSpec as P

AXES = ("sect", "grp", "dev")
VMEM_LIMIT = 10 * 2**20


def rounds_of():
    sects, groups, _ = (lax.axis_size(a) for a in AXES)
    bits = [1 << b for b in range(groups.bit_length() - 1)]
    orders = [bits[::-1], bits]
    return list(zip(*(orders[s % 2] for s in range(sects))))


def swap(value, masks):
    count = lax.axis_size("grp")
    pairs = [
        (s * count + i, s * count + (i ^ mask)) for s, mask in enumerate(masks) for i in range(count)
    ]
    return lax.ppermute(value, ("sect", "grp"), pairs)


def line_orders():
    lanes = lax.axis_size("dev")
    near = list(range(1, lanes))
    orders = [[0] + near[-1:] + near[:-1], [0] + near]
    return [orders[s % 2] for s in range(lax.axis_size("sect"))]


def swap_line(value, masks):
    lanes = lax.axis_size("dev")
    pairs = [
        (s * lanes + i, s * lanes + (i ^ mask)) for s, mask in enumerate(masks) for i in range(lanes)
    ]
    return lax.ppermute(value, ("sect", "dev"), pairs)


def swap_core(value):
    return lax.ppermute(value, "sect", [(0, 1), (1, 0)])


def vmem_call(kernel, out_shape, name, *operands):
    whole = pl.BlockSpec(memory_space=pltpu.VMEM)
    return pl.pallas_call(
        kernel,
        out_shape=out_shape,
        in_specs=[whole] * len(operands),
        out_specs=jax.tree.map(lambda _: whole, out_shape),
        compiler_params=pltpu.CompilerParams(vmem_limit_bytes=VMEM_LIMIT),
        name=name,
    )(*operands)


def extend_kernel(tokens_hbm, ids_hbm, weights_hbm, out_ref, tokens_ref, ids_ref, weights_ref, sems):
    pairs = ((ids_hbm, ids_ref), (weights_hbm, weights_ref), (tokens_hbm, tokens_ref))
    copies = [pltpu.make_async_copy(a, b, sems.at[i]) for i, (a, b) in enumerate(pairs)]
    for copy in copies:
        copy.start()
    rows, width = tokens_ref.shape
    half = (out_ref.shape[1] - width) // 2
    lane = lax.broadcasted_iota(jnp.int32, (rows, half * 2), 1)
    dense = jnp.zeros((rows, half * 2), jnp.float32)
    for copy in copies:
        copy.wait()
    for k in range(ids_ref.shape[1]):
        mine = lax.rem(lane, half) == ids_ref[:, k:k + 1]
        dense = dense + jnp.where(mine, weights_ref[:, k:k + 1], 0.0)
    high = dense.astype(jnp.bfloat16).astype(jnp.float32)
    out_ref[:, :width] = tokens_ref[...]
    out_ref[:, width:] = jnp.where(lane < half, high, dense - high).astype(jnp.bfloat16)


def extend(tokens, ids, weights, half):
    rows, width = tokens.shape
    return pl.pallas_call(
        extend_kernel,
        out_shape=jax.ShapeDtypeStruct((rows, width + 2 * half), tokens.dtype),
        in_specs=[pl.BlockSpec(memory_space=pl.ANY)] * 3,
        out_specs=pl.BlockSpec(memory_space=pltpu.VMEM),
        scratch_shapes=[pltpu.VMEM(v.shape, v.dtype) for v in (tokens, ids, weights)]
        + [pltpu.SemaphoreType.DMA((3,))],
        compiler_params=pltpu.CompilerParams(vmem_limit_bytes=VMEM_LIMIT),
        name="extend",
    )(*(pltpu.with_memory_space_constraint(v, pltpu.HBM) for v in (tokens, ids, weights)))


def stack_kernel(orders, *refs):
    pieces, out_ref = refs[:-1], refs[-1]
    for core, order in enumerate(orders):

        @pl.when(lax.axis_index("sect") == core)
        def _():
            values = [pieces[i][...].astype(jnp.float32) for i in order]
            out_ref[...] = jnp.concatenate(values, axis=0).astype(out_ref.dtype)


def stack(pieces, orders=None):
    rows = sum(p.shape[0] for p in pieces)
    out = jax.ShapeDtypeStruct((rows, pieces[0].shape[1]), pieces[0].dtype)
    if orders is None:
        orders = [range(len(pieces))] * lax.axis_size("sect")
    return vmem_call(functools.partial(stack_kernel, orders), out, "stack", *pieces)


def gather_rows(block, w_gate, w_up, w_down):
    experts, sects, lanes = w_gate.shape[0], lax.axis_size("sect"), lax.axis_size("dev")
    half, early = w_down.shape[1] // 2, early_columns(w_down)
    whole = [(w, e, 0, w.shape[1], w.shape[2]) for w in (w_gate, w_up) for e in range(experts)]
    parts = [(w_down, e, r, half, early) for e in range(experts) for r in (0, half)]
    held, token = {}, block

    def fetch_next(wholes, part, token):
        wanted = [whole.pop(0) for _ in range(min(wholes, len(whole)))] + parts[:part]
        del parts[:part]
        if not wanted:
            return token
        *arrays, token = fetch(wanted, token)
        for (weight, expert, row, _, _), array in zip(wanted, arrays):
            held[id(weight), expert, row] = array
        return token

    arrived = [swap_line(block, (m,) * sects) for m in range(1, lanes)]
    token = fetch_next(1, 1, token)
    arrived, token = lax.optimization_barrier((arrived, token))
    line = stack([block, *arrived], line_orders())
    rounds = rounds_of()
    for masks in rounds[:-1]:
        arrived = swap(line, masks)
        token = fetch_next(1, 1, token)
        arrived, token = lax.optimization_barrier((arrived, token))
        line = stack([line, arrived])
    last = swap(line, rounds[-1])
    token = fetch_next(1, 1, token)
    mine, token = lax.optimization_barrier((line, token))
    other = swap_core(mine)
    token = fetch_next(len(whole), 0, token)
    last, other, token = lax.optimization_barrier((last, other, token))
    last_other = swap_core(last)
    token = fetch_next(0, len(parts), token)
    last_other, token = lax.optimization_barrier((last_other, token))
    weights = [held[id(w), e, 0] for w in (w_gate, w_up) for e in range(experts)]
    weights += [held[id(w_down), e, r] for e in range(experts) for r in (0, half)]
    return [line, last, other, last_other], weights, token


def early_columns(w_down):
    _, hidden, width = w_down.shape
    return width // hidden // 2 * hidden


def down_copy(expert, block, at, down_hbm, target_ref, sems):
    hidden = down_hbm.shape[1]
    return pltpu.make_async_copy(
        down_hbm.at[expert, :, pl.ds(block * hidden, hidden)],
        target_ref.at[pl.ds(at * hidden, hidden)],
        sems.at[expert, block],
    )


def down_block(at, hidden_ref, weights, keep_ref, send_ref):
    hidden = weights[0].shape[1]
    middle = keep_ref.shape[0]
    weight = jnp.concatenate(weights, axis=0)
    total = jnp.dot(hidden_ref[...], weight, preferred_element_type=jnp.float32)
    total = total.astype(jnp.bfloat16)
    span = pl.ds(at * hidden, hidden)
    keep_ref[:, span] = total[:middle]
    send_ref[:, span] = total[middle:]


def expert_kernel(entry_count, experts, width, token_ref, *refs):
    pieces, refs = refs[:entry_count], refs[entry_count:]
    gate_refs, up_refs, early_refs, refs = (
        refs[:experts], refs[experts:2 * experts], refs[2 * experts:4 * experts], refs[4 * experts:]
    )
    down_hbm, hidden_ref, keep_ref, send_ref = refs[:4]
    down_refs, (rows_ref, value_ref, sems) = refs[4:4 + experts], refs[4 + experts:]
    hidden = gate_refs[0].shape[2]
    place = lax.axis_index("sect") * lax.axis_size("grp") + lax.axis_index("grp")
    first = place * experts
    block = min(256, hidden)
    blocks = width // hidden

    late = [
        [
            down_copy(e, step, step - blocks // 2, down_hbm, down_refs[e].at[0], sems)
            for step in range(blocks // 2, blocks)
        ]
        for e in range(experts)
    ]

    at = 0
    for piece in pieces:
        rows_ref[pl.ds(at, piece.shape[0])] = piece[...]
        at += piece.shape[0]

    for e in range(experts):

        @pl.loop(0, hidden // block)
        def _(step):
            span = pl.ds(pl.multiple_of(step * block, block), block)
            gate = jnp.dot(
                rows_ref[:, :width], gate_refs[e][0, :, span], preferred_element_type=jnp.float32
            )
            value_ref[e, :, span] = gate / (1.0 + jnp.exp(-gate))

        for copy in late[e]:
            copy.start()

    extra = rows_ref[:, width:].astype(jnp.float32)
    lane = lax.broadcasted_iota(jnp.int32, extra.shape, 1)
    for e in range(experts):
        mine = lax.rem(lane, extra.shape[1] // 2) == first + e
        scale = jnp.sum(jnp.where(mine, extra, 0.0), axis=1, keepdims=True)

        @pl.loop(0, hidden // block)
        def _(step):
            span = pl.ds(pl.multiple_of(step * block, block), block)
            up = jnp.dot(
                rows_ref[:, :width], up_refs[e][0, :, span], preferred_element_type=jnp.float32
            )
            value = value_ref[e, :, span] * up * scale
            out = pl.ds(pl.multiple_of(e * hidden + step * block, block), block)
            hidden_ref[:, out] = value.astype(jnp.bfloat16)

    for step in range(blocks // 2):
        span = pl.ds(step * hidden, hidden)
        down_block(step, hidden_ref, [ref[0, :, span] for ref in early_refs], keep_ref, send_ref)

    for copies in late:
        for copy in copies:
            copy.wait()


def down_kernel(hidden_ref, *refs):
    *down_refs, keep_ref, send_ref = refs
    hidden = down_refs[0].shape[2]
    for step in range(keep_ref.shape[1] // hidden):
        span = pl.ds(step * hidden, hidden)
        down_block(step, hidden_ref, [ref[0, span, :] for ref in down_refs], keep_ref, send_ref)


def fetch_kernel(wanted, after_ref, *refs):
    count = len(wanted)
    sources, targets, (token_ref, sems) = refs[:count], refs[count:2 * count], refs[2 * count:]
    copies = []
    for i, (_, expert, first, rows, columns) in enumerate(wanted):
        depth = rows // sems.shape[1]
        copies += [
            pltpu.make_async_copy(
                sources[i].at[expert, pl.ds(first + p * depth, depth), pl.ds(0, columns)],
                targets[i].at[0, pl.ds(p * depth, depth)],
                sems.at[i, p],
            )
            for p in range(sems.shape[1])
        ]
    for copy in copies:
        copy.start()
    token_ref[...] = jnp.zeros_like(token_ref)
    for copy in copies:
        copy.wait()


def fetch(wanted, after):
    in_hbm = pl.BlockSpec(memory_space=pl.ANY)
    whole = pl.BlockSpec(memory_space=pltpu.VMEM)
    return pl.pallas_call(
        functools.partial(fetch_kernel, [(None, *w[1:]) for w in wanted]),
        out_shape=(
            *(pltpu.VMEM((1, rows, columns), w.dtype) for w, _, _, rows, columns in wanted),
            jax.ShapeDtypeStruct((8, 128), jnp.float32),
        ),
        in_specs=[in_hbm] * (1 + len(wanted)),
        out_specs=(whole,) * (1 + len(wanted)),
        scratch_shapes=[pltpu.SemaphoreType.DMA((len(wanted), 8))],
        compiler_params=pltpu.CompilerParams(vmem_limit_bytes=VMEM_LIMIT),
        cost_estimate=pl.CostEstimate(
            flops=0,
            bytes_accessed=2 * sum(rows * columns for _, _, _, rows, columns in wanted),
            transcendentals=0,
        ),
        name="fetch",
    )(after, *(pltpu.with_memory_space_constraint(w[0], pltpu.HBM) for w in wanted))


def in_vmem(values):
    return [pltpu.with_memory_space_constraint(v, pltpu.VMEM) for v in values]


def expert_call(entries, held, w_down, token):
    experts, hidden, width = w_down.shape
    full = entries[0].shape[1]
    rows = sum(e.shape[0] for e in entries)
    blocks = width // hidden
    whole = pl.BlockSpec(memory_space=pltpu.VMEM)
    anywhere = pl.BlockSpec(memory_space=pl.ANY)
    columns = (early_columns(w_down), width - early_columns(w_down))
    outs = [jax.ShapeDtypeStruct((rows // 2, c), jnp.bfloat16) for c in columns]
    hiddens, keep, send, *down = pl.pallas_call(
        functools.partial(expert_kernel, len(entries), experts, width),
        out_shape=(
            jax.ShapeDtypeStruct((rows, experts * hidden), jnp.bfloat16),
            outs[0],
            outs[0],
            *(pltpu.VMEM(w.shape, w.dtype) for w in held[:experts]),
        ),
        in_specs=[anywhere] + [whole] * (len(entries) + len(held)) + [anywhere],
        out_specs=(whole,) * (3 + experts),
        input_output_aliases={1 + len(entries) + e: 3 + e for e in range(experts)},
        scratch_shapes=[
            pltpu.VMEM((rows, full), jnp.bfloat16),
            pltpu.VMEM((experts, rows, hidden), jnp.float32),
            pltpu.SemaphoreType.DMA((experts, blocks)),
        ],
        compiler_params=pltpu.CompilerParams(vmem_limit_bytes=VMEM_LIMIT),
        cost_estimate=pl.CostEstimate(
            flops=5 * rows * w_down.size,
            bytes_accessed=2 * w_down.size,
            transcendentals=rows * experts * hidden,
        ),
        name="experts",
    )(
        token,
        *entries,
        *in_vmem(held),
        pltpu.with_memory_space_constraint(w_down, pltpu.HBM),
    )
    later = pl.pallas_call(
        down_kernel,
        out_shape=(outs[1], outs[1]),
        in_specs=[whole] * (1 + experts),
        out_specs=(whole, whole),
        compiler_params=pltpu.CompilerParams(vmem_limit_bytes=VMEM_LIMIT),
        cost_estimate=pl.CostEstimate(
            flops=rows * w_down.size,
            bytes_accessed=2 * rows * columns[1],
            transcendentals=0,
        ),
        name="down",
    )(hiddens, *in_vmem(down))
    return (keep, send), later


def add(*values):
    total = values[0].astype(jnp.float32)
    for value in values[1:]:
        total = total + value.astype(jnp.float32)
    return total.astype(jnp.bfloat16)


def body(tokens, expert_ids, gate_weights, w_gate, w_up, w_down):
    sects, groups, lanes = (lax.axis_size(a) for a in AXES)
    row_count, width = tokens.shape
    experts = w_gate.shape[0]
    expert_count = sects * groups * experts

    half = -(-expert_count // 64) * 64
    block = extend(tokens, expert_ids, gate_weights, half)
    entries, held, token = gather_rows(block, w_gate, w_up, w_down)

    results = []
    halves = []
    for keep, send in expert_call(entries, held, w_down, token):
        value = add(keep, swap_core(send))
        for masks in rounds_of()[::-1]:
            middle = value.shape[0] // 2
            value = add(value[:middle], swap(value[middle:], masks))
        halves.append(value)
    value = jnp.concatenate(halves, axis=1)
    own = [value[m * row_count:(m + 1) * row_count] for m in range(lanes)]
    masks = list(zip(*line_orders()))
    return add(own[0], *(swap_line(own[i], masks[i]) for i in range(1, lanes)))


def solution(mesh):
    in_specs = (
        P(AXES, None),
        P(AXES, None),
        P(AXES, None),
        P(("sect", "grp"), None, "dev"),
        P(("sect", "grp"), None, "dev"),
        P(("sect", "grp"), "dev", None),
    )
    return jax.shard_map(
        body, mesh=mesh, in_specs=in_specs, out_specs=P(AXES, None), check_vma=False
    )
```

```python
import functools

import jax
import jax.numpy as jnp
from jax import lax
from jax.experimental import pallas as pl
from jax.experimental.pallas import tpu as pltpu
from jax.sharding import PartitionSpec as P

AXES = ("sect", "grp", "dev")
VMEM_LIMIT = 14 * 2**20


def rounds_of():
    sects, groups, _ = (lax.axis_size(a) for a in AXES)
    bits = [1 << b for b in range(groups.bit_length() - 1)]
    orders = [bits[::-1], bits]
    return list(zip(*(orders[s % 2] for s in range(sects))))


def swap(value, masks):
    count = lax.axis_size("grp")
    pairs = [
        (s * count + i, s * count + (i ^ mask)) for s, mask in enumerate(masks) for i in range(count)
    ]
    return lax.ppermute(value, ("sect", "grp"), pairs)


def line_orders():
    lanes = lax.axis_size("dev")
    near = list(range(1, lanes))
    orders = [[0] + near[-1:] + near[:-1], [0] + near]
    return [orders[s % 2] for s in range(lax.axis_size("sect"))]


def swap_line(value, masks):
    lanes = lax.axis_size("dev")
    pairs = [
        (s * lanes + i, s * lanes + (i ^ mask)) for s, mask in enumerate(masks) for i in range(lanes)
    ]
    return lax.ppermute(value, ("sect", "dev"), pairs)


def swap_core(value):
    return lax.ppermute(value, "sect", [(0, 1), (1, 0)])


def vmem_call(kernel, out_shape, name, *operands):
    whole = pl.BlockSpec(memory_space=pltpu.VMEM)
    return pl.pallas_call(
        kernel,
        out_shape=out_shape,
        in_specs=[whole] * len(operands),
        out_specs=jax.tree.map(lambda _: whole, out_shape),
        compiler_params=pltpu.CompilerParams(vmem_limit_bytes=VMEM_LIMIT),
        name=name,
    )(*operands)


def extend_kernel(tokens_hbm, ids_hbm, weights_hbm, out_ref, tokens_ref, ids_ref, weights_ref, sems):
    pairs = ((ids_hbm, ids_ref), (weights_hbm, weights_ref), (tokens_hbm, tokens_ref))
    copies = [pltpu.make_async_copy(a, b, sems.at[i]) for i, (a, b) in enumerate(pairs)]
    for copy in copies:
        copy.start()
    rows, width = tokens_ref.shape
    half = (out_ref.shape[1] - width) // 2
    lane = lax.broadcasted_iota(jnp.int32, (rows, half * 2), 1)
    dense = jnp.zeros((rows, half * 2), jnp.float32)
    for copy in copies:
        copy.wait()
    for k in range(ids_ref.shape[1]):
        mine = lax.rem(lane, half) == ids_ref[:, k:k + 1]
        dense = dense + jnp.where(mine, weights_ref[:, k:k + 1], 0.0)
    high = dense.astype(jnp.bfloat16).astype(jnp.float32)
    out_ref[:, :width] = tokens_ref[...]
    out_ref[:, width:] = jnp.where(lane < half, high, dense - high).astype(jnp.bfloat16)


def extend(tokens, ids, weights, half):
    rows, width = tokens.shape
    return pl.pallas_call(
        extend_kernel,
        out_shape=jax.ShapeDtypeStruct((rows, width + 2 * half), tokens.dtype),
        in_specs=[pl.BlockSpec(memory_space=pl.ANY)] * 3,
        out_specs=pl.BlockSpec(memory_space=pltpu.VMEM),
        scratch_shapes=[pltpu.VMEM(v.shape, v.dtype) for v in (tokens, ids, weights)]
        + [pltpu.SemaphoreType.DMA((3,))],
        compiler_params=pltpu.CompilerParams(vmem_limit_bytes=VMEM_LIMIT),
        name="extend",
    )(*(pltpu.with_memory_space_constraint(v, pltpu.HBM) for v in (tokens, ids, weights)))


def stack_kernel(orders, *refs):
    pieces, out_ref = refs[:-1], refs[-1]
    for core, order in enumerate(orders):

        @pl.when(lax.axis_index("sect") == core)
        def _():
            values = [pieces[i][...].astype(jnp.float32) for i in order]
            out_ref[...] = jnp.concatenate(values, axis=0).astype(out_ref.dtype)


def stack(pieces, orders=None):
    rows = sum(p.shape[0] for p in pieces)
    out = jax.ShapeDtypeStruct((rows, pieces[0].shape[1]), pieces[0].dtype)
    if orders is None:
        orders = [range(len(pieces))] * lax.axis_size("sect")
    return vmem_call(functools.partial(stack_kernel, orders), out, "stack", *pieces)


def gather_rows(block, w_gate, w_up, w_down):
    experts, sects, lanes = w_gate.shape[0], lax.axis_size("sect"), lax.axis_size("dev")
    half, early = w_down.shape[1] // 2, early_columns(w_down)
    whole = [(w, e, 0, w.shape[1], w.shape[2]) for w in (w_gate, w_up) for e in range(experts)]
    whole = whole[:-1]
    parts = [(w_down, e, r, half, early) for e in range(experts) for r in (0, half)]
    held, token = {}, block

    def fetch_next(wholes, part, token):
        wanted = [whole.pop(0) for _ in range(min(wholes, len(whole)))] + parts[:part]
        del parts[:part]
        if not wanted:
            return token
        *arrays, token = fetch(wanted, token)
        for (weight, expert, row, _, _), array in zip(wanted, arrays):
            held[id(weight), expert, row] = array
        return token

    arrived = [swap_line(block, (m,) * sects) for m in range(1, lanes)]
    token = fetch_next(0, 2, token)
    arrived, token = lax.optimization_barrier((arrived, token))
    line = stack([block, *arrived], line_orders())
    rounds = rounds_of()
    for masks in rounds[:-1]:
        arrived = swap(line, masks)
        token = fetch_next(1, 1, token)
        arrived, token = lax.optimization_barrier((arrived, token))
        line = stack([line, arrived])
    last = swap(line, rounds[-1])
    token = fetch_next(1, 0, token)
    mine, token = lax.optimization_barrier((line, token))
    other = swap_core(mine)
    token = fetch_next(len(whole), 0, token)
    last, other, token = lax.optimization_barrier((last, other, token))
    last_other = swap_core(last)
    token = fetch_next(0, len(parts), token)
    last_other, token = lax.optimization_barrier((last_other, token))
    weights = [held[id(w_gate), e, 0] for e in range(experts)]
    weights += [held[id(w_up), e, 0] for e in range(experts - 1)]
    weights += [held[id(w_down), e, r] for e in range(experts) for r in (0, half)]
    return [line, last, other, last_other], weights, token


def early_columns(w_down):
    _, hidden, width = w_down.shape
    return width // hidden // 2 * hidden


def down_copy(expert, block, at, down_hbm, target_ref, sems):
    hidden = down_hbm.shape[1]
    return pltpu.make_async_copy(
        down_hbm.at[expert, :, pl.ds(block * hidden, hidden)],
        target_ref.at[pl.ds(at * hidden, hidden)],
        sems.at[expert, block],
    )


def down_block(span, hidden_ref, weights, keep_ref, send_ref):
    middle = keep_ref.shape[0]
    weight = jnp.concatenate(weights, axis=0)
    total = jnp.dot(hidden_ref[...], weight, preferred_element_type=jnp.float32)
    total = total.astype(jnp.bfloat16)
    keep_ref[:, span] = total[:middle]
    send_ref[:, span] = total[middle:]


def expert_kernel(entry_count, experts, width, token_ref, *refs):
    pieces, refs = refs[:entry_count], refs[entry_count:]
    gate_refs, up_refs, refs = refs[:experts], refs[experts:2 * experts - 1], refs[2 * experts - 1:]
    early_refs, refs = refs[:2 * experts], refs[2 * experts:]
    up_hbm, down_hbm, hidden_ref, keep_ref, send_ref = refs[:5]
    down_refs, (rows_ref, value_ref, last_up_ref, up_sems, sems) = refs[5:5 + experts], refs[5 + experts:]
    up_refs = [*up_refs, last_up_ref]
    hidden = gate_refs[0].shape[2]
    place = lax.axis_index("sect") * lax.axis_size("grp") + lax.axis_index("grp")
    first = place * experts
    block = min(256, hidden)
    blocks = width // hidden

    late = [
        [
            down_copy(e, step, step - blocks // 2, down_hbm, down_refs[e].at[0], sems)
            for step in range(blocks // 2, blocks)
        ]
        for e in range(experts)
    ]

    depth = width // up_sems.shape[0]
    up_copies = [
        pltpu.make_async_copy(
            up_hbm.at[experts - 1, pl.ds(p * depth, depth)],
            last_up_ref.at[0, pl.ds(p * depth, depth)],
            up_sems.at[p],
        )
        for p in range(up_sems.shape[0])
    ]
    for copy in up_copies:
        copy.start()

    at = 0
    for piece in pieces:
        rows_ref[pl.ds(at, piece.shape[0])] = piece[...]
        at += piece.shape[0]

    for e in range(experts):

        @pl.loop(0, hidden // block)
        def _(step):
            span = pl.ds(pl.multiple_of(step * block, block), block)
            gate = jnp.dot(
                rows_ref[:, :width], gate_refs[e][0, :, span], preferred_element_type=jnp.float32
            )
            value_ref[e, :, span] = gate / (1.0 + jnp.exp(-gate))

        for copy in late[e]:
            copy.start()

    extra = rows_ref[:, width:].astype(jnp.float32)
    lane = lax.broadcasted_iota(jnp.int32, extra.shape, 1)
    for e in range(experts):
        mine = lax.rem(lane, extra.shape[1] // 2) == first + e
        scale = jnp.sum(jnp.where(mine, extra, 0.0), axis=1, keepdims=True)
        if e == experts - 1:
            for copy in up_copies:
                copy.wait()

        @pl.loop(0, hidden // block)
        def _(step):
            span = pl.ds(pl.multiple_of(step * block, block), block)
            up = jnp.dot(
                rows_ref[:, :width], up_refs[e][0, :, span], preferred_element_type=jnp.float32
            )
            value = value_ref[e, :, span] * up * scale
            out = pl.ds(pl.multiple_of(e * hidden + step * block, block), block)
            hidden_ref[:, out] = value.astype(jnp.bfloat16)

    part = keep_ref.shape[1] // 2

    @pl.loop(0, 2)
    def _(step):
        span = pl.ds(pl.multiple_of(step * part, 128), part)
        down_block(span, hidden_ref, [ref[0, :, span] for ref in early_refs], keep_ref, send_ref)

    for copies in late:
        for copy in copies:
            copy.wait()


def down_kernel(hidden_ref, *refs):
    *down_refs, keep_ref, send_ref = refs
    hidden = down_refs[0].shape[2]
    for step in range(keep_ref.shape[1] // hidden):
        span = pl.ds(step * hidden, hidden)
        down_block(span, hidden_ref, [ref[0, span, :] for ref in down_refs], keep_ref, send_ref)


def fetch_kernel(wanted, after_ref, *refs):
    count = len(wanted)
    sources, targets, (token_ref, sems) = refs[:count], refs[count:2 * count], refs[2 * count:]
    copies = []
    for i, (_, expert, first, rows, columns) in enumerate(wanted):
        depth = rows // sems.shape[1]
        copies += [
            pltpu.make_async_copy(
                sources[i].at[expert, pl.ds(first + p * depth, depth), pl.ds(0, columns)],
                targets[i].at[0, pl.ds(p * depth, depth)],
                sems.at[i, p],
            )
            for p in range(sems.shape[1])
        ]
    for copy in copies:
        copy.start()
    token_ref[...] = jnp.zeros_like(token_ref)
    for copy in copies:
        copy.wait()


def fetch(wanted, after):
    in_hbm = pl.BlockSpec(memory_space=pl.ANY)
    whole = pl.BlockSpec(memory_space=pltpu.VMEM)
    return pl.pallas_call(
        functools.partial(fetch_kernel, [(None, *w[1:]) for w in wanted]),
        out_shape=(
            *(pltpu.VMEM((1, rows, columns), w.dtype) for w, _, _, rows, columns in wanted),
            jax.ShapeDtypeStruct((8, 128), jnp.float32),
        ),
        in_specs=[in_hbm] * (1 + len(wanted)),
        out_specs=(whole,) * (1 + len(wanted)),
        scratch_shapes=[pltpu.SemaphoreType.DMA((len(wanted), 8))],
        compiler_params=pltpu.CompilerParams(vmem_limit_bytes=VMEM_LIMIT),
        cost_estimate=pl.CostEstimate(
            flops=0,
            bytes_accessed=2 * sum(rows * columns for _, _, _, rows, columns in wanted),
            transcendentals=0,
        ),
        name="fetch",
    )(after, *(pltpu.with_memory_space_constraint(w[0], pltpu.HBM) for w in wanted))


def in_vmem(values):
    return [pltpu.with_memory_space_constraint(v, pltpu.VMEM) for v in values]


def expert_call(entries, held, w_up, w_down, token):
    experts, hidden, width = w_down.shape
    full = entries[0].shape[1]
    rows = sum(e.shape[0] for e in entries)
    blocks = width // hidden
    whole = pl.BlockSpec(memory_space=pltpu.VMEM)
    anywhere = pl.BlockSpec(memory_space=pl.ANY)
    columns = (early_columns(w_down), width - early_columns(w_down))
    outs = [jax.ShapeDtypeStruct((rows // 2, c), jnp.bfloat16) for c in columns]
    hiddens, keep, send, *down = pl.pallas_call(
        functools.partial(expert_kernel, len(entries), experts, width),
        out_shape=(
            jax.ShapeDtypeStruct((rows, experts * hidden), jnp.bfloat16),
            outs[0],
            outs[0],
            *(pltpu.VMEM(w.shape, w.dtype) for w in held[:experts]),
        ),
        in_specs=[anywhere] + [whole] * (len(entries) + len(held)) + [anywhere] * 2,
        out_specs=(whole,) * (3 + experts),
        input_output_aliases={1 + len(entries) + e: 3 + e for e in range(experts)},
        scratch_shapes=[
            pltpu.VMEM((rows, full), jnp.bfloat16),
            pltpu.VMEM((experts, rows, hidden), jnp.float32),
            pltpu.VMEM((1, *w_up.shape[1:]), w_up.dtype),
            pltpu.SemaphoreType.DMA((8,)),
            pltpu.SemaphoreType.DMA((experts, blocks)),
        ],
        compiler_params=pltpu.CompilerParams(vmem_limit_bytes=VMEM_LIMIT),
        cost_estimate=pl.CostEstimate(
            flops=5 * rows * w_down.size,
            bytes_accessed=2 * w_down.size,
            transcendentals=rows * experts * hidden,
        ),
        name="experts",
    )(
        token,
        *entries,
        *in_vmem(held),
        pltpu.with_memory_space_constraint(w_up, pltpu.HBM),
        pltpu.with_memory_space_constraint(w_down, pltpu.HBM),
    )
    later = pl.pallas_call(
        down_kernel,
        out_shape=(outs[1], outs[1]),
        in_specs=[whole] * (1 + experts),
        out_specs=(whole, whole),
        compiler_params=pltpu.CompilerParams(vmem_limit_bytes=VMEM_LIMIT),
        cost_estimate=pl.CostEstimate(
            flops=rows * w_down.size,
            bytes_accessed=2 * rows * columns[1],
            transcendentals=0,
        ),
        name="down",
    )(hiddens, *in_vmem(down))
    return (keep, send), later


def add(*values):
    total = values[0].astype(jnp.float32)
    for value in values[1:]:
        total = total + value.astype(jnp.float32)
    return total.astype(jnp.bfloat16)


def body(tokens, expert_ids, gate_weights, w_gate, w_up, w_down):
    sects, groups, lanes = (lax.axis_size(a) for a in AXES)
    row_count, width = tokens.shape
    experts = w_gate.shape[0]
    expert_count = sects * groups * experts

    half = -(-expert_count // 64) * 64
    block = extend(tokens, expert_ids, gate_weights, half)
    entries, held, token = gather_rows(block, w_gate, w_up, w_down)

    results = []
    halves = []
    for keep, send in expert_call(entries, held, w_up, w_down, token):
        value = add(keep, swap_core(send))
        for masks in rounds_of()[::-1]:
            middle = value.shape[0] // 2
            value = add(value[:middle], swap(value[middle:], masks))
        halves.append(value)
    value = jnp.concatenate(halves, axis=1)
    own = [value[m * row_count:(m + 1) * row_count] for m in range(lanes)]
    masks = list(zip(*line_orders()))
    return add(own[0], *(swap_line(own[i], masks[i]) for i in range(1, lanes)))


def solution(mesh):
    in_specs = (
        P(AXES, None),
        P(AXES, None),
        P(AXES, None),
        P(("sect", "grp"), None, "dev"),
        P(("sect", "grp"), None, "dev"),
        P(("sect", "grp"), "dev", None),
    )
    return jax.shard_map(
        body, mesh=mesh, in_specs=in_specs, out_specs=P(AXES, None), check_vma=False
    )
```

```python
import functools

import jax
import jax.numpy as jnp
from jax import lax
from jax.experimental import pallas as pl
from jax.experimental.pallas import tpu as pltpu
from jax.sharding import PartitionSpec as P

AXES = ("sect", "grp", "dev")
VMEM_LIMIT = 14 * 2**20


def rounds_of():
    sects, groups, _ = (lax.axis_size(a) for a in AXES)
    bits = [1 << b for b in range(groups.bit_length() - 1)]
    orders = [bits[::-1], bits]
    return list(zip(*(orders[s % 2] for s in range(sects))))


def swap(value, masks):
    count = lax.axis_size("grp")
    pairs = [
        (s * count + i, s * count + (i ^ mask)) for s, mask in enumerate(masks) for i in range(count)
    ]
    return lax.ppermute(value, ("sect", "grp"), pairs)


def line_orders():
    lanes = lax.axis_size("dev")
    near = list(range(lanes))
    orders = [[0, 2, 1, 3] if lanes == 4 else near, near]
    return [orders[s % 2] for s in range(lax.axis_size("sect"))]


def line_masks():
    lanes = lax.axis_size("dev")
    return (1, 3, 2) if lanes == 4 else range(1, lanes)


def swap_line(value, masks):
    lanes = lax.axis_size("dev")
    pairs = [
        (s * lanes + i, s * lanes + (i ^ mask)) for s, mask in enumerate(masks) for i in range(lanes)
    ]
    return lax.ppermute(value, ("sect", "dev"), pairs)


def swap_core(value):
    return lax.ppermute(value, "sect", [(0, 1), (1, 0)])


def vmem_call(kernel, out_shape, name, *operands):
    whole = pl.BlockSpec(memory_space=pltpu.VMEM)
    return pl.pallas_call(
        kernel,
        out_shape=out_shape,
        in_specs=[whole] * len(operands),
        out_specs=jax.tree.map(lambda _: whole, out_shape),
        compiler_params=pltpu.CompilerParams(vmem_limit_bytes=VMEM_LIMIT),
        name=name,
    )(*operands)


def extend_kernel(tokens_hbm, ids_hbm, weights_hbm, out_ref, tokens_ref, ids_ref, weights_ref, sems):
    pairs = ((ids_hbm, ids_ref), (weights_hbm, weights_ref), (tokens_hbm, tokens_ref))
    copies = [pltpu.make_async_copy(a, b, sems.at[i]) for i, (a, b) in enumerate(pairs)]
    for copy in copies:
        copy.start()
    rows, width = tokens_ref.shape
    half = (out_ref.shape[1] - width) // 2
    lane = lax.broadcasted_iota(jnp.int32, (rows, half * 2), 1)
    dense = jnp.zeros((rows, half * 2), jnp.float32)
    for copy in copies:
        copy.wait()
    for k in range(ids_ref.shape[1]):
        mine = lax.rem(lane, half) == ids_ref[:, k:k + 1]
        dense = dense + jnp.where(mine, weights_ref[:, k:k + 1], 0.0)
    high = dense.astype(jnp.bfloat16).astype(jnp.float32)
    out_ref[:, :width] = tokens_ref[...]
    out_ref[:, width:] = jnp.where(lane < half, high, dense - high).astype(jnp.bfloat16)


def extend(tokens, ids, weights, half):
    rows, width = tokens.shape
    return pl.pallas_call(
        extend_kernel,
        out_shape=jax.ShapeDtypeStruct((rows, width + 2 * half), tokens.dtype),
        in_specs=[pl.BlockSpec(memory_space=pl.ANY)] * 3,
        out_specs=pl.BlockSpec(memory_space=pltpu.VMEM),
        scratch_shapes=[pltpu.VMEM(v.shape, v.dtype) for v in (tokens, ids, weights)]
        + [pltpu.SemaphoreType.DMA((3,))],
        compiler_params=pltpu.CompilerParams(vmem_limit_bytes=VMEM_LIMIT),
        name="extend",
    )(*(pltpu.with_memory_space_constraint(v, pltpu.HBM) for v in (tokens, ids, weights)))


def stack_kernel(orders, *refs):
    pieces, out_ref = refs[:-1], refs[-1]
    for core, order in enumerate(orders):

        @pl.when(lax.axis_index("sect") == core)
        def _():
            values = [pieces[i][...].astype(jnp.float32) for i in order]
            out_ref[...] = jnp.concatenate(values, axis=0).astype(out_ref.dtype)


def stack(pieces, orders=None):
    rows = sum(p.shape[0] for p in pieces)
    out = jax.ShapeDtypeStruct((rows, pieces[0].shape[1]), pieces[0].dtype)
    if orders is None:
        orders = [range(len(pieces))] * lax.axis_size("sect")
    return vmem_call(functools.partial(stack_kernel, orders), out, "stack", *pieces)


def gather_rows(block, w_gate, w_up, w_down):
    experts, sects, lanes = w_gate.shape[0], lax.axis_size("sect"), lax.axis_size("dev")
    half, early = w_down.shape[1] // 2, early_columns(w_down)
    whole = [(w, e, 0, w.shape[1], w.shape[2]) for w in (w_gate, w_up) for e in range(experts)]
    whole = whole[:-1]
    parts = [(w_down, e, r, half, early) for e in range(experts) for r in (0, half)]
    held, token = {}, block

    def fetch_next(wholes, part, token):
        wanted = [whole.pop(0) for _ in range(min(wholes, len(whole)))] + parts[:part]
        del parts[:part]
        if not wanted:
            return token
        *arrays, token = fetch(wanted, token)
        for (weight, expert, row, _, _), array in zip(wanted, arrays):
            held[id(weight), expert, row] = array
        return token

    by_mask = {m: swap_line(block, (m,) * sects) for m in line_masks()}
    arrived = [by_mask[m] for m in range(1, lanes)]
    token = fetch_next(0, 2, token)
    arrived, token = lax.optimization_barrier((arrived, token))
    line = stack([block, *arrived], line_orders())
    rounds = rounds_of()
    for masks in rounds[:-1]:
        arrived = swap(line, masks)
        token = fetch_next(1, 1, token)
        arrived, token = lax.optimization_barrier((arrived, token))
        line = stack([line, arrived])
    last = swap(line, rounds[-1])
    token = fetch_next(1, 0, token)
    mine, token = lax.optimization_barrier((line, token))
    other = swap_core(mine)
    token = fetch_next(len(whole), 0, token)
    last, other, token = lax.optimization_barrier((last, other, token))
    last_other = swap_core(last)
    token = fetch_next(0, len(parts), token)
    last_other, token = lax.optimization_barrier((last_other, token))
    weights = [held[id(w_gate), e, 0] for e in range(experts)]
    weights += [held[id(w_up), e, 0] for e in range(experts - 1)]
    weights += [held[id(w_down), e, r] for e in range(experts) for r in (0, half)]
    return [line, last, other, last_other], weights, token


def early_columns(w_down):
    _, hidden, width = w_down.shape
    return width // hidden // 2 * hidden


def down_copy(expert, block, at, down_hbm, target_ref, sems):
    hidden = down_hbm.shape[1]
    return pltpu.make_async_copy(
        down_hbm.at[expert, :, pl.ds(block * hidden, hidden)],
        target_ref.at[pl.ds(at * hidden, hidden)],
        sems.at[expert, block],
    )


def down_block(span, hidden_ref, weights, keep_ref, send_ref):
    middle = keep_ref.shape[0]
    weight = jnp.concatenate(weights, axis=0)
    total = jnp.dot(hidden_ref[...], weight, preferred_element_type=jnp.float32)
    total = total.astype(jnp.bfloat16)
    keep_ref[:, span] = total[:middle]
    send_ref[:, span] = total[middle:]


def expert_kernel(entry_count, experts, width, token_ref, *refs):
    pieces, refs = refs[:entry_count], refs[entry_count:]
    gate_refs, up_refs, refs = refs[:experts], refs[experts:2 * experts - 1], refs[2 * experts - 1:]
    early_refs, refs = refs[:2 * experts], refs[2 * experts:]
    up_hbm, down_hbm, hidden_ref, keep_ref, send_ref = refs[:5]
    down_refs, (rows_ref, value_ref, last_up_ref, up_sems, sems) = refs[5:5 + experts], refs[5 + experts:]
    up_refs = [*up_refs, last_up_ref]
    hidden = gate_refs[0].shape[2]
    place = lax.axis_index("sect") * lax.axis_size("grp") + lax.axis_index("grp")
    first = place * experts
    block = min(256, hidden)
    blocks = width // hidden

    late = [
        [
            down_copy(e, step, step - blocks // 2, down_hbm, down_refs[e].at[0], sems)
            for step in range(blocks // 2, blocks)
        ]
        for e in range(experts)
    ]

    depth = width // up_sems.shape[0]
    up_copies = [
        pltpu.make_async_copy(
            up_hbm.at[experts - 1, pl.ds(p * depth, depth)],
            last_up_ref.at[0, pl.ds(p * depth, depth)],
            up_sems.at[p],
        )
        for p in range(up_sems.shape[0])
    ]
    for copy in up_copies:
        copy.start()

    at = 0
    for piece in pieces:
        rows_ref[pl.ds(at, piece.shape[0])] = piece[...]
        at += piece.shape[0]

    for e in range(experts):

        @pl.loop(0, hidden // block)
        def _(step):
            span = pl.ds(pl.multiple_of(step * block, block), block)
            gate = jnp.dot(
                rows_ref[:, :width], gate_refs[e][0, :, span], preferred_element_type=jnp.float32
            )
            value_ref[e, :, span] = gate / (1.0 + jnp.exp(-gate))

        for copy in late[e]:
            copy.start()

    extra = rows_ref[:, width:].astype(jnp.float32)
    lane = lax.broadcasted_iota(jnp.int32, extra.shape, 1)
    for e in range(experts):
        mine = lax.rem(lane, extra.shape[1] // 2) == first + e
        scale = jnp.sum(jnp.where(mine, extra, 0.0), axis=1, keepdims=True)
        if e == experts - 1:
            for copy in up_copies:
                copy.wait()

        @pl.loop(0, hidden // block)
        def _(step):
            span = pl.ds(pl.multiple_of(step * block, block), block)
            up = jnp.dot(
                rows_ref[:, :width], up_refs[e][0, :, span], preferred_element_type=jnp.float32
            )
            value = value_ref[e, :, span] * up * scale
            out = pl.ds(pl.multiple_of(e * hidden + step * block, block), block)
            hidden_ref[:, out] = value.astype(jnp.bfloat16)

    part = keep_ref.shape[1] // 2

    @pl.loop(0, 2)
    def _(step):
        span = pl.ds(pl.multiple_of(step * part, 128), part)
        down_block(span, hidden_ref, [ref[0, :, span] for ref in early_refs], keep_ref, send_ref)

    for copies in late:
        for copy in copies:
            copy.wait()


def down_kernel(hidden_ref, *refs):
    *down_refs, keep_ref, send_ref = refs
    hidden = down_refs[0].shape[2]
    for step in range(keep_ref.shape[1] // hidden):
        span = pl.ds(step * hidden, hidden)
        down_block(span, hidden_ref, [ref[0, span, :] for ref in down_refs], keep_ref, send_ref)


def fetch_kernel(wanted, after_ref, *refs):
    count = len(wanted)
    sources, targets, (token_ref, sems) = refs[:count], refs[count:2 * count], refs[2 * count:]
    copies = []
    for i, (_, expert, first, rows, columns) in enumerate(wanted):
        depth = rows // sems.shape[1]
        copies += [
            pltpu.make_async_copy(
                sources[i].at[expert, pl.ds(first + p * depth, depth), pl.ds(0, columns)],
                targets[i].at[0, pl.ds(p * depth, depth)],
                sems.at[i, p],
            )
            for p in range(sems.shape[1])
        ]
    for copy in copies:
        copy.start()
    token_ref[...] = jnp.zeros_like(token_ref)
    for copy in copies:
        copy.wait()


def fetch(wanted, after):
    in_hbm = pl.BlockSpec(memory_space=pl.ANY)
    whole = pl.BlockSpec(memory_space=pltpu.VMEM)
    return pl.pallas_call(
        functools.partial(fetch_kernel, [(None, *w[1:]) for w in wanted]),
        out_shape=(
            *(pltpu.VMEM((1, rows, columns), w.dtype) for w, _, _, rows, columns in wanted),
            jax.ShapeDtypeStruct((8, 128), jnp.float32),
        ),
        in_specs=[in_hbm] * (1 + len(wanted)),
        out_specs=(whole,) * (1 + len(wanted)),
        scratch_shapes=[pltpu.SemaphoreType.DMA((len(wanted), 8))],
        compiler_params=pltpu.CompilerParams(vmem_limit_bytes=VMEM_LIMIT),
        cost_estimate=pl.CostEstimate(
            flops=0,
            bytes_accessed=2 * sum(rows * columns for _, _, _, rows, columns in wanted),
            transcendentals=0,
        ),
        name="fetch",
    )(after, *(pltpu.with_memory_space_constraint(w[0], pltpu.HBM) for w in wanted))


def in_vmem(values):
    return [pltpu.with_memory_space_constraint(v, pltpu.VMEM) for v in values]


def expert_call(entries, held, w_up, w_down, token):
    experts, hidden, width = w_down.shape
    full = entries[0].shape[1]
    rows = sum(e.shape[0] for e in entries)
    blocks = width // hidden
    whole = pl.BlockSpec(memory_space=pltpu.VMEM)
    anywhere = pl.BlockSpec(memory_space=pl.ANY)
    columns = (early_columns(w_down), width - early_columns(w_down))
    outs = [jax.ShapeDtypeStruct((rows // 2, c), jnp.bfloat16) for c in columns]
    hiddens, keep, send, *down = pl.pallas_call(
        functools.partial(expert_kernel, len(entries), experts, width),
        out_shape=(
            jax.ShapeDtypeStruct((rows, experts * hidden), jnp.bfloat16),
            outs[0],
            outs[0],
            *(pltpu.VMEM(w.shape, w.dtype) for w in held[:experts]),
        ),
        in_specs=[anywhere] + [whole] * (len(entries) + len(held)) + [anywhere] * 2,
        out_specs=(whole,) * (3 + experts),
        input_output_aliases={1 + len(entries) + e: 3 + e for e in range(experts)},
        scratch_shapes=[
            pltpu.VMEM((rows, full), jnp.bfloat16),
            pltpu.VMEM((experts, rows, hidden), jnp.float32),
            pltpu.VMEM((1, *w_up.shape[1:]), w_up.dtype),
            pltpu.SemaphoreType.DMA((8,)),
            pltpu.SemaphoreType.DMA((experts, blocks)),
        ],
        compiler_params=pltpu.CompilerParams(vmem_limit_bytes=VMEM_LIMIT),
        cost_estimate=pl.CostEstimate(
            flops=5 * rows * w_down.size,
            bytes_accessed=2 * w_down.size,
            transcendentals=rows * experts * hidden,
        ),
        name="experts",
    )(
        token,
        *entries,
        *in_vmem(held),
        pltpu.with_memory_space_constraint(w_up, pltpu.HBM),
        pltpu.with_memory_space_constraint(w_down, pltpu.HBM),
    )
    later = pl.pallas_call(
        down_kernel,
        out_shape=(outs[1], outs[1]),
        in_specs=[whole] * (1 + experts),
        out_specs=(whole, whole),
        compiler_params=pltpu.CompilerParams(vmem_limit_bytes=VMEM_LIMIT),
        cost_estimate=pl.CostEstimate(
            flops=rows * w_down.size,
            bytes_accessed=2 * rows * columns[1],
            transcendentals=0,
        ),
        name="down",
    )(hiddens, *in_vmem(down))
    return (keep, send), later


def add(*values):
    total = values[0].astype(jnp.float32)
    for value in values[1:]:
        total = total + value.astype(jnp.float32)
    return total.astype(jnp.bfloat16)


def body(tokens, expert_ids, gate_weights, w_gate, w_up, w_down):
    sects, groups, lanes = (lax.axis_size(a) for a in AXES)
    row_count, width = tokens.shape
    experts = w_gate.shape[0]
    expert_count = sects * groups * experts

    half = -(-expert_count // 64) * 64
    block = extend(tokens, expert_ids, gate_weights, half)
    entries, held, token = gather_rows(block, w_gate, w_up, w_down)

    results = []
    halves = []
    for keep, send in expert_call(entries, held, w_up, w_down, token):
        value = add(keep, swap_core(send))
        for masks in rounds_of()[::-1]:
            middle = value.shape[0] // 2
            value = add(value[:middle], swap(value[middle:], masks))
        halves.append(value)
    value = jnp.concatenate(halves, axis=1)
    own = [value[m * row_count:(m + 1) * row_count] for m in range(lanes)]
    masks = list(zip(*line_orders()))
    return add(own[0], *(swap_line(own[i], masks[i]) for i in range(1, lanes)))


def solution(mesh):
    in_specs = (
        P(AXES, None),
        P(AXES, None),
        P(AXES, None),
        P(("sect", "grp"), None, "dev"),
        P(("sect", "grp"), None, "dev"),
        P(("sect", "grp"), "dev", None),
    )
    return jax.shard_map(
        body, mesh=mesh, in_specs=in_specs, out_specs=P(AXES, None), check_vma=False
    )
```

```python
import functools

import jax
import jax.numpy as jnp
from jax import lax
from jax.experimental import pallas as pl
from jax.experimental.pallas import tpu as pltpu
from jax.sharding import PartitionSpec as P

AXES = ("sect", "grp", "dev")
VMEM_LIMIT = 14 * 2**20


def rounds_of():
    sects, groups, _ = (lax.axis_size(a) for a in AXES)
    bits = [1 << b for b in range(groups.bit_length() - 1)]
    orders = [bits[::-1], bits]
    return list(zip(*(orders[s % 2] for s in range(sects))))


def swap(value, masks):
    count = lax.axis_size("grp")
    pairs = [
        (s * count + i, s * count + (i ^ mask)) for s, mask in enumerate(masks) for i in range(count)
    ]
    return lax.ppermute(value, ("sect", "grp"), pairs)


def line_orders():
    lanes = lax.axis_size("dev")
    near = list(range(1, lanes))
    orders = [[0] + near[-1:] + near[:-1], [0] + near]
    return [orders[s % 2] for s in range(lax.axis_size("sect"))]


def swap_line(value, masks):
    lanes = lax.axis_size("dev")
    pairs = [
        (s * lanes + i, s * lanes + (i ^ mask)) for s, mask in enumerate(masks) for i in range(lanes)
    ]
    return lax.ppermute(value, ("sect", "dev"), pairs)


def swap_core(value):
    return lax.ppermute(value, "sect", [(0, 1), (1, 0)])


def vmem_call(kernel, out_shape, name, *operands):
    whole = pl.BlockSpec(memory_space=pltpu.VMEM)
    return pl.pallas_call(
        kernel,
        out_shape=out_shape,
        in_specs=[whole] * len(operands),
        out_specs=jax.tree.map(lambda _: whole, out_shape),
        compiler_params=pltpu.CompilerParams(vmem_limit_bytes=VMEM_LIMIT),
        name=name,
    )(*operands)


def extend_kernel(tokens_hbm, ids_hbm, weights_hbm, out_ref, tokens_ref, ids_ref, weights_ref, sems):
    pairs = ((ids_hbm, ids_ref), (weights_hbm, weights_ref), (tokens_hbm, tokens_ref))
    copies = [pltpu.make_async_copy(a, b, sems.at[i]) for i, (a, b) in enumerate(pairs)]
    for copy in copies:
        copy.start()
    rows, width = tokens_ref.shape
    half = (out_ref.shape[1] - width) // 2
    lane = lax.broadcasted_iota(jnp.int32, (rows, half * 2), 1)
    dense = jnp.zeros((rows, half * 2), jnp.float32)
    for copy in copies:
        copy.wait()
    for k in range(ids_ref.shape[1]):
        mine = lax.rem(lane, half) == ids_ref[:, k:k + 1]
        dense = dense + jnp.where(mine, weights_ref[:, k:k + 1], 0.0)
    high = dense.astype(jnp.bfloat16).astype(jnp.float32)
    out_ref[:, :width] = tokens_ref[...]
    out_ref[:, width:] = jnp.where(lane < half, high, dense - high).astype(jnp.bfloat16)


def extend(tokens, ids, weights, half):
    rows, width = tokens.shape
    return pl.pallas_call(
        extend_kernel,
        out_shape=jax.ShapeDtypeStruct((rows, width + 2 * half), tokens.dtype),
        in_specs=[pl.BlockSpec(memory_space=pl.ANY)] * 3,
        out_specs=pl.BlockSpec(memory_space=pltpu.VMEM),
        scratch_shapes=[pltpu.VMEM(v.shape, v.dtype) for v in (tokens, ids, weights)]
        + [pltpu.SemaphoreType.DMA((3,))],
        compiler_params=pltpu.CompilerParams(vmem_limit_bytes=VMEM_LIMIT),
        name="extend",
    )(*(pltpu.with_memory_space_constraint(v, pltpu.HBM) for v in (tokens, ids, weights)))


def stack_kernel(orders, *refs):
    pieces, out_ref = refs[:-1], refs[-1]
    for core, order in enumerate(orders):

        @pl.when(lax.axis_index("sect") == core)
        def _():
            values = [pieces[i][...].astype(jnp.float32) for i in order]
            out_ref[...] = jnp.concatenate(values, axis=0).astype(out_ref.dtype)


def stack(pieces, orders=None):
    rows = sum(p.shape[0] for p in pieces)
    out = jax.ShapeDtypeStruct((rows, pieces[0].shape[1]), pieces[0].dtype)
    if orders is None:
        orders = [range(len(pieces))] * lax.axis_size("sect")
    return vmem_call(functools.partial(stack_kernel, orders), out, "stack", *pieces)


def gather_rows(block, w_gate, w_up, w_down):
    experts, sects, lanes = w_gate.shape[0], lax.axis_size("sect"), lax.axis_size("dev")
    half, early = w_down.shape[1] // 2, early_columns(w_down)
    whole = [(w, e, 0, w.shape[1], w.shape[2]) for w in (w_gate, w_up) for e in range(experts)]
    whole = whole[:-1]
    parts = [(w_down, e, r, half, early) for e in range(experts) for r in (0, half)]
    held, token = {}, block

    def fetch_next(wholes, part, token):
        wanted = [whole.pop(0) for _ in range(min(wholes, len(whole)))] + parts[:part]
        del parts[:part]
        if not wanted:
            return token
        *arrays, token = fetch(wanted, token)
        for (weight, expert, row, _, _), array in zip(wanted, arrays):
            held[id(weight), expert, row] = array
        return token

    masks = [1, 3, 2] if lanes == 4 else list(range(1, lanes))
    arrived = [swap_line(block, (m,) * sects) for m in masks]
    token = fetch_next(0, 2, token)
    arrived, token = lax.optimization_barrier((arrived, token))
    index = {m: i for i, m in enumerate([0] + masks)}
    line = stack([block, *arrived], [[index[m] for m in order] for order in line_orders()])
    rounds = rounds_of()
    for masks in rounds[:-1]:
        arrived = swap(line, masks)
        token = fetch_next(1, 1, token)
        arrived, token = lax.optimization_barrier((arrived, token))
        line = stack([line, arrived])
    last = swap(line, rounds[-1])
    token = fetch_next(1, 0, token)
    mine, token = lax.optimization_barrier((line, token))
    other = swap_core(mine)
    token = fetch_next(len(whole), 0, token)
    last, other, token = lax.optimization_barrier((last, other, token))
    last_other = swap_core(last)
    token = fetch_next(0, len(parts), token)
    last_other, token = lax.optimization_barrier((last_other, token))
    weights = [held[id(w_gate), e, 0] for e in range(experts)]
    weights += [held[id(w_up), e, 0] for e in range(experts - 1)]
    weights += [held[id(w_down), e, r] for e in range(experts) for r in (0, half)]
    return [line, last, other, last_other], weights, token


def early_columns(w_down):
    _, hidden, width = w_down.shape
    return width // hidden // 2 * hidden


def down_copy(expert, block, at, down_hbm, target_ref, sems):
    hidden = down_hbm.shape[1]
    return pltpu.make_async_copy(
        down_hbm.at[expert, :, pl.ds(block * hidden, hidden)],
        target_ref.at[pl.ds(at * hidden, hidden)],
        sems.at[expert, block],
    )


def down_block(span, hidden_ref, weights, keep_ref, send_ref):
    middle = keep_ref.shape[0]
    weight = jnp.concatenate(weights, axis=0)
    total = jnp.dot(hidden_ref[...], weight, preferred_element_type=jnp.float32)
    total = total.astype(jnp.bfloat16)
    keep_ref[:, span] = total[:middle]
    send_ref[:, span] = total[middle:]


def expert_kernel(entry_count, experts, width, token_ref, *refs):
    pieces, refs = refs[:entry_count], refs[entry_count:]
    gate_refs, up_refs, refs = refs[:experts], refs[experts:2 * experts - 1], refs[2 * experts - 1:]
    early_refs, refs = refs[:2 * experts], refs[2 * experts:]
    up_hbm, down_hbm, hidden_ref, keep_ref, send_ref = refs[:5]
    down_refs, (rows_ref, value_ref, last_up_ref, up_sems, sems) = refs[5:5 + experts], refs[5 + experts:]
    up_refs = [*up_refs, last_up_ref]
    hidden = gate_refs[0].shape[2]
    place = lax.axis_index("sect") * lax.axis_size("grp") + lax.axis_index("grp")
    first = place * experts
    block = min(256, hidden)
    blocks = width // hidden

    late = [
        [
            down_copy(e, step, step - blocks // 2, down_hbm, down_refs[e].at[0], sems)
            for step in range(blocks // 2, blocks)
        ]
        for e in range(experts)
    ]

    depth = width // up_sems.shape[0]
    up_copies = [
        pltpu.make_async_copy(
            up_hbm.at[experts - 1, pl.ds(p * depth, depth)],
            last_up_ref.at[0, pl.ds(p * depth, depth)],
            up_sems.at[p],
        )
        for p in range(up_sems.shape[0])
    ]
    for copy in up_copies:
        copy.start()

    at = 0
    for piece in pieces:
        rows_ref[pl.ds(at, piece.shape[0])] = piece[...]
        at += piece.shape[0]

    for e in range(experts):

        @pl.loop(0, hidden // block)
        def _(step):
            span = pl.ds(pl.multiple_of(step * block, block), block)
            gate = jnp.dot(
                rows_ref[:, :width], gate_refs[e][0, :, span], preferred_element_type=jnp.float32
            )
            value_ref[e, :, span] = gate / (1.0 + jnp.exp(-gate))

        for copy in late[e]:
            copy.start()

    extra = rows_ref[:, width:].astype(jnp.float32)
    lane = lax.broadcasted_iota(jnp.int32, extra.shape, 1)
    for e in range(experts):
        mine = lax.rem(lane, extra.shape[1] // 2) == first + e
        scale = jnp.sum(jnp.where(mine, extra, 0.0), axis=1, keepdims=True)
        if e == experts - 1:
            for copy in up_copies:
                copy.wait()

        @pl.loop(0, hidden // block)
        def _(step):
            span = pl.ds(pl.multiple_of(step * block, block), block)
            up = jnp.dot(
                rows_ref[:, :width], up_refs[e][0, :, span], preferred_element_type=jnp.float32
            )
            value = value_ref[e, :, span] * up * scale
            out = pl.ds(pl.multiple_of(e * hidden + step * block, block), block)
            hidden_ref[:, out] = value.astype(jnp.bfloat16)

    part = keep_ref.shape[1] // 2

    @pl.loop(0, 2)
    def _(step):
        span = pl.ds(pl.multiple_of(step * part, 128), part)
        down_block(span, hidden_ref, [ref[0, :, span] for ref in early_refs], keep_ref, send_ref)

    for copies in late:
        for copy in copies:
            copy.wait()


def down_kernel(hidden_ref, *refs):
    *down_refs, keep_ref, send_ref = refs
    hidden = down_refs[0].shape[2]
    for step in range(keep_ref.shape[1] // hidden):
        span = pl.ds(step * hidden, hidden)
        down_block(span, hidden_ref, [ref[0, span, :] for ref in down_refs], keep_ref, send_ref)


def fetch_kernel(wanted, after_ref, *refs):
    count = len(wanted)
    sources, targets, (token_ref, sems) = refs[:count], refs[count:2 * count], refs[2 * count:]
    copies = []
    for i, (_, expert, first, rows, columns) in enumerate(wanted):
        depth = rows // sems.shape[1]
        copies += [
            pltpu.make_async_copy(
                sources[i].at[expert, pl.ds(first + p * depth, depth), pl.ds(0, columns)],
                targets[i].at[0, pl.ds(p * depth, depth)],
                sems.at[i, p],
            )
            for p in range(sems.shape[1])
        ]
    for copy in copies:
        copy.start()
    token_ref[...] = jnp.zeros_like(token_ref)
    for copy in copies:
        copy.wait()


def fetch(wanted, after):
    in_hbm = pl.BlockSpec(memory_space=pl.ANY)
    whole = pl.BlockSpec(memory_space=pltpu.VMEM)
    return pl.pallas_call(
        functools.partial(fetch_kernel, [(None, *w[1:]) for w in wanted]),
        out_shape=(
            *(pltpu.VMEM((1, rows, columns), w.dtype) for w, _, _, rows, columns in wanted),
            jax.ShapeDtypeStruct((8, 128), jnp.float32),
        ),
        in_specs=[in_hbm] * (1 + len(wanted)),
        out_specs=(whole,) * (1 + len(wanted)),
        scratch_shapes=[pltpu.SemaphoreType.DMA((len(wanted), 8))],
        compiler_params=pltpu.CompilerParams(vmem_limit_bytes=VMEM_LIMIT),
        cost_estimate=pl.CostEstimate(
            flops=0,
            bytes_accessed=2 * sum(rows * columns for _, _, _, rows, columns in wanted),
            transcendentals=0,
        ),
        name="fetch",
    )(after, *(pltpu.with_memory_space_constraint(w[0], pltpu.HBM) for w in wanted))


def in_vmem(values):
    return [pltpu.with_memory_space_constraint(v, pltpu.VMEM) for v in values]


def expert_call(entries, held, w_up, w_down, token):
    experts, hidden, width = w_down.shape
    full = entries[0].shape[1]
    rows = sum(e.shape[0] for e in entries)
    blocks = width // hidden
    whole = pl.BlockSpec(memory_space=pltpu.VMEM)
    anywhere = pl.BlockSpec(memory_space=pl.ANY)
    columns = (early_columns(w_down), width - early_columns(w_down))
    outs = [jax.ShapeDtypeStruct((rows // 2, c), jnp.bfloat16) for c in columns]
    hiddens, keep, send, *down = pl.pallas_call(
        functools.partial(expert_kernel, len(entries), experts, width),
        out_shape=(
            jax.ShapeDtypeStruct((rows, experts * hidden), jnp.bfloat16),
            outs[0],
            outs[0],
            *(pltpu.VMEM(w.shape, w.dtype) for w in held[:experts]),
        ),
        in_specs=[anywhere] + [whole] * (len(entries) + len(held)) + [anywhere] * 2,
        out_specs=(whole,) * (3 + experts),
        input_output_aliases={1 + len(entries) + e: 3 + e for e in range(experts)},
        scratch_shapes=[
            pltpu.VMEM((rows, full), jnp.bfloat16),
            pltpu.VMEM((experts, rows, hidden), jnp.float32),
            pltpu.VMEM((1, *w_up.shape[1:]), w_up.dtype),
            pltpu.SemaphoreType.DMA((8,)),
            pltpu.SemaphoreType.DMA((experts, blocks)),
        ],
        compiler_params=pltpu.CompilerParams(vmem_limit_bytes=VMEM_LIMIT),
        cost_estimate=pl.CostEstimate(
            flops=5 * rows * w_down.size,
            bytes_accessed=2 * w_down.size,
            transcendentals=rows * experts * hidden,
        ),
        name="experts",
    )(
        token,
        *entries,
        *in_vmem(held),
        pltpu.with_memory_space_constraint(w_up, pltpu.HBM),
        pltpu.with_memory_space_constraint(w_down, pltpu.HBM),
    )
    later = pl.pallas_call(
        down_kernel,
        out_shape=(outs[1], outs[1]),
        in_specs=[whole] * (1 + experts),
        out_specs=(whole, whole),
        compiler_params=pltpu.CompilerParams(vmem_limit_bytes=VMEM_LIMIT),
        cost_estimate=pl.CostEstimate(
            flops=rows * w_down.size,
            bytes_accessed=2 * rows * columns[1],
            transcendentals=0,
        ),
        name="down",
    )(hiddens, *in_vmem(down))
    return (keep, send), later


def add(*values):
    total = values[0].astype(jnp.float32)
    for value in values[1:]:
        total = total + value.astype(jnp.float32)
    return total.astype(jnp.bfloat16)


def body(tokens, expert_ids, gate_weights, w_gate, w_up, w_down):
    sects, groups, lanes = (lax.axis_size(a) for a in AXES)
    row_count, width = tokens.shape
    experts = w_gate.shape[0]
    expert_count = sects * groups * experts

    half = -(-expert_count // 64) * 64
    block = extend(tokens, expert_ids, gate_weights, half)
    entries, held, token = gather_rows(block, w_gate, w_up, w_down)

    results = []
    halves = []
    for keep, send in expert_call(entries, held, w_up, w_down, token):
        value = add(keep, swap_core(send))
        for masks in rounds_of()[::-1]:
            middle = value.shape[0] // 2
            value = add(value[:middle], swap(value[middle:], masks))
        halves.append(value)
    value = jnp.concatenate(halves, axis=1)
    own = [value[m * row_count:(m + 1) * row_count] for m in range(lanes)]
    masks = list(zip(*line_orders()))
    return add(own[0], *(swap_line(own[i], masks[i]) for i in range(1, lanes)))


def solution(mesh):
    in_specs = (
        P(AXES, None),
        P(AXES, None),
        P(AXES, None),
        P(("sect", "grp"), None, "dev"),
        P(("sect", "grp"), None, "dev"),
        P(("sect", "grp"), "dev", None),
    )
    return jax.shard_map(
        body, mesh=mesh, in_specs=in_specs, out_specs=P(AXES, None), check_vma=False
    )
```

```python
import functools

import jax
import jax.numpy as jnp
from jax import lax
from jax.experimental import pallas as pl
from jax.experimental.pallas import tpu as pltpu
from jax.sharding import PartitionSpec as P

AXES = ("sect", "grp", "dev")
VMEM_LIMIT = 14 * 2**20


def rounds_of():
    sects, groups, _ = (lax.axis_size(a) for a in AXES)
    bits = [1 << b for b in range(groups.bit_length() - 1)]
    orders = [bits[::-1], bits]
    return list(zip(*(orders[s % 2] for s in range(sects))))


def swap(value, masks):
    count = lax.axis_size("grp")
    pairs = [
        (s * count + i, s * count + (i ^ mask)) for s, mask in enumerate(masks) for i in range(count)
    ]
    return lax.ppermute(value, ("sect", "grp"), pairs)


def line_orders():
    lanes = lax.axis_size("dev")
    near = list(range(1, lanes))
    orders = [[0] + near[-1:] + near[:-1], [0] + near]
    return [orders[s % 2] for s in range(lax.axis_size("sect"))]


def swap_line(value, masks):
    lanes = lax.axis_size("dev")
    pairs = [
        (s * lanes + i, s * lanes + (i ^ mask)) for s, mask in enumerate(masks) for i in range(lanes)
    ]
    return lax.ppermute(value, ("sect", "dev"), pairs)


def swap_core(value):
    return lax.ppermute(value, "sect", [(0, 1), (1, 0)])


def vmem_call(kernel, out_shape, name, *operands):
    whole = pl.BlockSpec(memory_space=pltpu.VMEM)
    return pl.pallas_call(
        kernel,
        out_shape=out_shape,
        in_specs=[whole] * len(operands),
        out_specs=jax.tree.map(lambda _: whole, out_shape),
        compiler_params=pltpu.CompilerParams(vmem_limit_bytes=VMEM_LIMIT),
        name=name,
    )(*operands)


def extend_kernel(tokens_hbm, ids_hbm, weights_hbm, out_ref, tokens_ref, ids_ref, weights_ref, sems):
    pairs = ((ids_hbm, ids_ref), (weights_hbm, weights_ref), (tokens_hbm, tokens_ref))
    copies = [pltpu.make_async_copy(a, b, sems.at[i]) for i, (a, b) in enumerate(pairs)]
    for copy in copies:
        copy.start()
    rows, width = tokens_ref.shape
    half = (out_ref.shape[1] - width) // 2
    lane = lax.broadcasted_iota(jnp.int32, (rows, half * 2), 1)
    dense = jnp.zeros((rows, half * 2), jnp.float32)
    for copy in copies[:2]:
        copy.wait()
    for k in range(ids_ref.shape[1]):
        mine = lax.rem(lane, half) == ids_ref[:, k:k + 1]
        dense = dense + jnp.where(mine, weights_ref[:, k:k + 1], 0.0)
    high = dense.astype(jnp.bfloat16).astype(jnp.float32)
    copies[2].wait()
    out_ref[:, :width] = tokens_ref[...]
    out_ref[:, width:] = jnp.where(lane < half, high, dense - high).astype(jnp.bfloat16)


def extend(tokens, ids, weights, half):
    rows, width = tokens.shape
    return pl.pallas_call(
        extend_kernel,
        out_shape=jax.ShapeDtypeStruct((rows, width + 2 * half), tokens.dtype),
        in_specs=[pl.BlockSpec(memory_space=pl.ANY)] * 3,
        out_specs=pl.BlockSpec(memory_space=pltpu.VMEM),
        scratch_shapes=[pltpu.VMEM(v.shape, v.dtype) for v in (tokens, ids, weights)]
        + [pltpu.SemaphoreType.DMA((3,))],
        compiler_params=pltpu.CompilerParams(vmem_limit_bytes=VMEM_LIMIT),
        name="extend",
    )(*(pltpu.with_memory_space_constraint(v, pltpu.HBM) for v in (tokens, ids, weights)))


def stack_kernel(orders, *refs):
    pieces, out_ref = refs[:-1], refs[-1]
    for core, order in enumerate(orders):

        @pl.when(lax.axis_index("sect") == core)
        def _():
            values = [pieces[i][...].astype(jnp.float32) for i in order]
            out_ref[...] = jnp.concatenate(values, axis=0).astype(out_ref.dtype)


def stack(pieces, orders=None):
    rows = sum(p.shape[0] for p in pieces)
    out = jax.ShapeDtypeStruct((rows, pieces[0].shape[1]), pieces[0].dtype)
    if orders is None:
        orders = [range(len(pieces))] * lax.axis_size("sect")
    return vmem_call(functools.partial(stack_kernel, orders), out, "stack", *pieces)


def gather_rows(block, w_gate, w_up, w_down):
    experts, sects, lanes = w_gate.shape[0], lax.axis_size("sect"), lax.axis_size("dev")
    half, early = w_down.shape[1] // 2, early_columns(w_down)
    whole = [(w, e, 0, w.shape[1], w.shape[2]) for w in (w_gate, w_up) for e in range(experts)]
    whole = whole[:-1]
    parts = [(w_down, e, r, half, early) for e in range(experts) for r in (0, half)]
    held, token = {}, block

    def fetch_next(wholes, part, token):
        wanted = [whole.pop(0) for _ in range(min(wholes, len(whole)))] + parts[:part]
        del parts[:part]
        if not wanted:
            return token
        *arrays, token = fetch(wanted, token)
        for (weight, expert, row, _, _), array in zip(wanted, arrays):
            held[id(weight), expert, row] = array
        return token

    masks = [1, 3, 2] if lanes == 4 else list(range(1, lanes))
    arrived = [swap_line(block, (m,) * sects) for m in masks]
    token = fetch_next(0, 3, token)
    arrived, token = lax.optimization_barrier((arrived, token))
    index = {m: i for i, m in enumerate([0] + masks)}
    line = stack([block, *arrived], [[index[m] for m in order] for order in line_orders()])
    rounds = rounds_of()
    for masks in rounds[:-1]:
        arrived = swap(line, masks)
        token = fetch_next(1, 1, token)
        arrived, token = lax.optimization_barrier((arrived, token))
        line = stack([line, arrived])
    last = swap(line, rounds[-1])
    token = fetch_next(1, 0, token)
    mine, token = lax.optimization_barrier((line, token))
    other = swap_core(mine)
    token = fetch_next(len(whole), 0, token)
    last, other, token = lax.optimization_barrier((last, other, token))
    last_other = swap_core(last)
    token = fetch_next(0, len(parts), token)
    last_other, token = lax.optimization_barrier((last_other, token))
    weights = [held[id(w_gate), e, 0] for e in range(experts)]
    weights += [held[id(w_up), e, 0] for e in range(experts - 1)]
    weights += [held[id(w_down), e, r] for e in range(experts) for r in (0, half)]
    return [line, last, other, last_other], weights, token


def early_columns(w_down):
    _, hidden, width = w_down.shape
    return width // hidden // 2 * hidden


def down_copy(expert, block, at, down_hbm, target_ref, sems):
    hidden = down_hbm.shape[1]
    return pltpu.make_async_copy(
        down_hbm.at[expert, :, pl.ds(block * hidden, hidden)],
        target_ref.at[pl.ds(at * hidden, hidden)],
        sems.at[expert, block],
    )


def down_block(span, hidden_ref, weights, keep_ref, send_ref):
    middle = keep_ref.shape[0]
    weight = jnp.concatenate(weights, axis=0)
    total = jnp.dot(hidden_ref[...], weight, preferred_element_type=jnp.float32)
    total = total.astype(jnp.bfloat16)
    keep_ref[:, span] = total[:middle]
    send_ref[:, span] = total[middle:]


def expert_kernel(entry_count, experts, width, token_ref, *refs):
    pieces, refs = refs[:entry_count], refs[entry_count:]
    gate_refs, up_refs, refs = refs[:experts], refs[experts:2 * experts - 1], refs[2 * experts - 1:]
    early_refs, refs = refs[:2 * experts], refs[2 * experts:]
    up_hbm, down_hbm, hidden_ref, keep_ref, send_ref = refs[:5]
    down_refs, (rows_ref, value_ref, last_up_ref, up_sems, sems) = refs[5:5 + experts], refs[5 + experts:]
    up_refs = [*up_refs, last_up_ref]
    hidden = gate_refs[0].shape[2]
    place = lax.axis_index("sect") * lax.axis_size("grp") + lax.axis_index("grp")
    first = place * experts
    block = min(256, hidden)
    blocks = width // hidden

    late = [
        [
            down_copy(e, step, step - blocks // 2, down_hbm, down_refs[e].at[0], sems)
            for step in range(blocks // 2, blocks)
        ]
        for e in range(experts)
    ]

    depth = width // up_sems.shape[0]
    up_copies = [
        pltpu.make_async_copy(
            up_hbm.at[experts - 1, pl.ds(p * depth, depth)],
            last_up_ref.at[0, pl.ds(p * depth, depth)],
            up_sems.at[p],
        )
        for p in range(up_sems.shape[0])
    ]
    for copy in up_copies:
        copy.start()

    at = 0
    for piece in pieces:
        rows_ref[pl.ds(at, piece.shape[0])] = piece[...]
        at += piece.shape[0]

    for e in range(experts):

        @pl.loop(0, hidden // block)
        def _(step):
            span = pl.ds(pl.multiple_of(step * block, block), block)
            gate = jnp.dot(
                rows_ref[:, :width], gate_refs[e][0, :, span], preferred_element_type=jnp.float32
            )
            value_ref[e, :, span] = gate / (1.0 + jnp.exp(-gate))

        for copy in late[e]:
            copy.start()

    extra = rows_ref[:, width:].astype(jnp.float32)
    lane = lax.broadcasted_iota(jnp.int32, extra.shape, 1)
    for e in range(experts):
        mine = lax.rem(lane, extra.shape[1] // 2) == first + e
        scale = jnp.sum(jnp.where(mine, extra, 0.0), axis=1, keepdims=True)
        if e == experts - 1:
            for copy in up_copies:
                copy.wait()

        @pl.loop(0, hidden // block)
        def _(step):
            span = pl.ds(pl.multiple_of(step * block, block), block)
            up = jnp.dot(
                rows_ref[:, :width], up_refs[e][0, :, span], preferred_element_type=jnp.float32
            )
            value = value_ref[e, :, span] * up * scale
            out = pl.ds(pl.multiple_of(e * hidden + step * block, block), block)
            hidden_ref[:, out] = value.astype(jnp.bfloat16)

    part = keep_ref.shape[1] // 2

    @pl.loop(0, 2)
    def _(step):
        span = pl.ds(pl.multiple_of(step * part, 128), part)
        down_block(span, hidden_ref, [ref[0, :, span] for ref in early_refs], keep_ref, send_ref)

    for copies in late:
        for copy in copies:
            copy.wait()


def down_kernel(hidden_ref, *refs):
    *down_refs, keep_ref, send_ref = refs
    hidden = down_refs[0].shape[2]
    for step in range(keep_ref.shape[1] // hidden):
        span = pl.ds(step * hidden, hidden)
        down_block(span, hidden_ref, [ref[0, span, :] for ref in down_refs], keep_ref, send_ref)


def fetch_kernel(wanted, after_ref, *refs):
    count = len(wanted)
    sources, targets, (token_ref, sems) = refs[:count], refs[count:2 * count], refs[2 * count:]
    copies = []
    for i, (_, expert, first, rows, columns) in enumerate(wanted):
        depth = rows // sems.shape[1]
        copies += [
            pltpu.make_async_copy(
                sources[i].at[expert, pl.ds(first + p * depth, depth), pl.ds(0, columns)],
                targets[i].at[0, pl.ds(p * depth, depth)],
                sems.at[i, p],
            )
            for p in range(sems.shape[1])
        ]
    for copy in copies:
        copy.start()
    token_ref[...] = jnp.zeros_like(token_ref)
    for copy in copies:
        copy.wait()


def fetch(wanted, after):
    in_hbm = pl.BlockSpec(memory_space=pl.ANY)
    whole = pl.BlockSpec(memory_space=pltpu.VMEM)
    return pl.pallas_call(
        functools.partial(fetch_kernel, [(None, *w[1:]) for w in wanted]),
        out_shape=(
            *(pltpu.VMEM((1, rows, columns), w.dtype) for w, _, _, rows, columns in wanted),
            jax.ShapeDtypeStruct((8, 128), jnp.float32),
        ),
        in_specs=[in_hbm] * (1 + len(wanted)),
        out_specs=(whole,) * (1 + len(wanted)),
        scratch_shapes=[pltpu.SemaphoreType.DMA((len(wanted), 8))],
        compiler_params=pltpu.CompilerParams(vmem_limit_bytes=VMEM_LIMIT),
        cost_estimate=pl.CostEstimate(
            flops=0,
            bytes_accessed=2 * sum(rows * columns for _, _, _, rows, columns in wanted),
            transcendentals=0,
        ),
        name="fetch",
    )(after, *(pltpu.with_memory_space_constraint(w[0], pltpu.HBM) for w in wanted))


def in_vmem(values):
    return [pltpu.with_memory_space_constraint(v, pltpu.VMEM) for v in values]


def expert_call(entries, held, w_up, w_down, token):
    experts, hidden, width = w_down.shape
    full = entries[0].shape[1]
    rows = sum(e.shape[0] for e in entries)
    blocks = width // hidden
    whole = pl.BlockSpec(memory_space=pltpu.VMEM)
    anywhere = pl.BlockSpec(memory_space=pl.ANY)
    columns = (early_columns(w_down), width - early_columns(w_down))
    outs = [jax.ShapeDtypeStruct((rows // 2, c), jnp.bfloat16) for c in columns]
    hiddens, keep, send, *down = pl.pallas_call(
        functools.partial(expert_kernel, len(entries), experts, width),
        out_shape=(
            jax.ShapeDtypeStruct((rows, experts * hidden), jnp.bfloat16),
            outs[0],
            outs[0],
            *(pltpu.VMEM(w.shape, w.dtype) for w in held[:experts]),
        ),
        in_specs=[anywhere] + [whole] * (len(entries) + len(held)) + [anywhere] * 2,
        out_specs=(whole,) * (3 + experts),
        input_output_aliases={1 + len(entries) + e: 3 + e for e in range(experts)},
        scratch_shapes=[
            pltpu.VMEM((rows, full), jnp.bfloat16),
            pltpu.VMEM((experts, rows, hidden), jnp.float32),
            pltpu.VMEM((1, *w_up.shape[1:]), w_up.dtype),
            pltpu.SemaphoreType.DMA((8,)),
            pltpu.SemaphoreType.DMA((experts, blocks)),
        ],
        compiler_params=pltpu.CompilerParams(vmem_limit_bytes=VMEM_LIMIT),
        cost_estimate=pl.CostEstimate(
            flops=5 * rows * w_down.size,
            bytes_accessed=2 * w_down.size,
            transcendentals=rows * experts * hidden,
        ),
        name="experts",
    )(
        token,
        *entries,
        *in_vmem(held),
        pltpu.with_memory_space_constraint(w_up, pltpu.HBM),
        pltpu.with_memory_space_constraint(w_down, pltpu.HBM),
    )
    later = pl.pallas_call(
        down_kernel,
        out_shape=(outs[1], outs[1]),
        in_specs=[whole] * (1 + experts),
        out_specs=(whole, whole),
        compiler_params=pltpu.CompilerParams(vmem_limit_bytes=VMEM_LIMIT),
        cost_estimate=pl.CostEstimate(
            flops=rows * w_down.size,
            bytes_accessed=2 * rows * columns[1],
            transcendentals=0,
        ),
        name="down",
    )(hiddens, *in_vmem(down))
    return (keep, send), later


def add(*values):
    total = values[0].astype(jnp.float32)
    for value in values[1:]:
        total = total + value.astype(jnp.float32)
    return total.astype(jnp.bfloat16)


def body(tokens, expert_ids, gate_weights, w_gate, w_up, w_down):
    sects, groups, lanes = (lax.axis_size(a) for a in AXES)
    row_count, width = tokens.shape
    experts = w_gate.shape[0]
    expert_count = sects * groups * experts

    half = -(-expert_count // 64) * 64
    block = extend(tokens, expert_ids, gate_weights, half)
    entries, held, token = gather_rows(block, w_gate, w_up, w_down)

    results = []
    halves = []
    for keep, send in expert_call(entries, held, w_up, w_down, token):
        value = add(keep, swap_core(send))
        for masks in rounds_of()[::-1]:
            middle = value.shape[0] // 2
            value = add(value[:middle], swap(value[middle:], masks))
        halves.append(value)
    value = jnp.concatenate(halves, axis=1)
    own = [value[m * row_count:(m + 1) * row_count] for m in range(lanes)]
    masks = list(zip(*line_orders()))
    return add(own[0], *(swap_line(own[i], masks[i]) for i in range(1, lanes)))


def solution(mesh):
    in_specs = (
        P(AXES, None),
        P(AXES, None),
        P(AXES, None),
        P(("sect", "grp"), None, "dev"),
        P(("sect", "grp"), None, "dev"),
        P(("sect", "grp"), "dev", None),
    )
    return jax.shard_map(
        body, mesh=mesh, in_specs=in_specs, out_specs=P(AXES, None), check_vma=False
    )
```
